512 devices in a mesh: dp: 32 (over x_hi, z, core), seq: 16 (over x_lo, y).
Axes of the slice: x: 4 (x_hi: 2, x_lo: 2; x = x_hi * 2 + x_lo), y: 8, z: 8, core: 2. Of those that a mesh axis runs over, the one named last changes fastest.
Arguments:
- hidden: bfloat16 [32, 16, 256, 1152], P('dp', 'seq'), may hold values from -6 to 6
- timesteps: int32 [32], P('dp'), may hold values from 0 to 999
- ada_weight: bfloat16 [128, 2304], replicated, may hold values from -0.1796875 to 0.1796875
- master: float32 [1152, 1728], P('dp'), may hold values from -6 to 6
- ema_slow: float32 [1152, 1728], P('dp'), may hold values from -1.8 to 1.8
- ema_fast: float32 [1152, 1728], P('dp'), may hold values from -1.8 to 1.8
- step_count: int32 [1], replicated, may hold values from 20 to 59
- cotangent: bfloat16 [32, 16, 256, 576], P('dp', 'seq'), may hold values from -6 to 6
Outputs:
- hidden_grad: bfloat16 [32, 16, 256, 1152], P('dp', 'seq')
- ema_slow_next: float32 [1152, 1728], P('dp')
- ema_fast_next: float32 [1152, 1728], P('dp')
The draws below stay inside these ranges and needn't reach their ends.
All inputs are finite; a program needn't handle non-finite values.
Results may differ from the reference program's by a relative error of at most 0.02.
Values may be sent and summed in bfloat16 or wider, within the bound.
No kernel may reach another device: no remote copies, remote signals or barrier semaphores. Data moves between devices by JAX's collectives and lax.ppermute only.
A program may use at most 64 MiB of HBM per device.

```python
import math
import jax
import jax.numpy as jnp
from jax import lax

D = 1152
HEADS = 8
HDIM = 72
FREQ = 128
PATCHES = 256
FR_DEV = 1
CLIPS_DEV = 1
HI = 576
FRAMES = 16
CLIPS = 32
N_SEQ = 16


def draw_master(key, part):
    inner = HEADS * HDIM
    second_key = jax.random.fold_in(jax.random.fold_in(key, 7), 1)
    base_values = jax.random.normal(second_key, (D, 3 * inner), jnp.float32)
    return jnp.clip(base_values, -6.0, 6.0) / D ** 0.5


def with_ends(result, key, low, top_value):
    spot = [jax.random.randint(jax.random.fold_in(key, axis), (), 0, length) for axis, length in enumerate(result.shape)]
    widest = result.shape.index(max(result.shape))
    neighbour = spot[:widest] + [(spot[widest] + 1) % result.shape[widest]] + spot[widest + 1:]
    return result.at[tuple(spot)].set(low).at[tuple(neighbour)].set(top_value)


def raised(drawn, key, source, target, parts, factor):
    owner, partner = [(jnp.arange(drawn.shape[dim]) // (drawn.shape[dim] // parts)).reshape([-1 if axis == dim else 1 for axis in range(drawn.ndim)]) for dim in (source, target)]
    chosen = jax.random.permutation(key, parts)[partner]
    strong = (owner == chosen) | (owner == (partner + parts // 2) % parts)
    return jnp.where(strong, factor * drawn, drawn)


def shard_levels(rng, dims, cuts, low, top_value):
    def one(dim, parts):
        steps = jax.random.uniform(jax.random.fold_in(jax.random.fold_in(rng, 6), dim), (parts,), jnp.float32, low / len(cuts), top_value / len(cuts))
        return jnp.repeat(jnp.exp(steps), dims[dim] // parts).reshape((-1,) + (1,) * (len(dims) - dim - 1))

    loudness = one(*cuts[0])
    for cut in cuts[1:]:
        loudness = loudness * one(*cut)
    return loudness


def bell_draw(own_key, shape, width, bound, shards=(), held_as=jnp.bfloat16):
    result = width * jax.random.normal(own_key, shape, jnp.float32)
    if shards:
        result = result * shard_levels(own_key, shape, shards, -0.22, 0.18)
    return jnp.clip(result, -bound, bound).astype(held_as)


def heavy_noise(own_key, extent, width, reach, shards, heavy, kind=jnp.bfloat16):
    result = width * jax.random.normal(own_key, extent, jnp.float32)
    if shards:
        result = result * shard_levels(own_key, extent, shards, -0.22, 0.18)
    return jnp.clip(raised(result, jax.random.fold_in(own_key, 3), *heavy), -reach, reach).astype(kind)


def setup_inputs(seed: int = 0) -> dict:
    arg_keys = jax.random.split(jax.random.key(seed), 9)
    hidden = heavy_noise(arg_keys[0], (CLIPS, FRAMES, PATCHES, D), 1.0, 6.0, ((0, 32), (1, 16)), (0, 3, 32, 2.75))
    timesteps = with_ends(jax.random.randint(arg_keys[1], (CLIPS,), 0, 1000), jax.random.fold_in(arg_keys[1], 1), 0, 999).astype(jnp.int32)
    ada_weight = bell_draw(arg_keys[2], (FREQ, 2 * D), 0.03, 0.1796875)
    master = draw_master(jax.random.fold_in(arg_keys[8], 71), 0)
    ema_slow = bell_draw(arg_keys[4], (D, 3 * HI), 0.3, 1.8, ((0, 32),), jnp.float32)
    ema_fast = bell_draw(arg_keys[5], (D, 3 * HI), 0.3, 1.8, ((0, 32),), jnp.float32)
    step_count = jax.random.randint(arg_keys[6], (1,), 20, 60).astype(jnp.int32)
    cotangent = bell_draw(arg_keys[7], (CLIPS, FRAMES, PATCHES, HI), 1.0, 6.0, ((0, 32), (1, 16)))
    return dict(hidden=hidden, timesteps=timesteps, ada_weight=ada_weight, master=master, ema_slow=ema_slow, ema_fast=ema_fast, step_count=step_count, cotangent=cotangent)


norm_eps = 1e-06
loss_scale = 128.0
gamma_slow = 16.97
gamma_fast = 6.94

def modulate_table(timesteps, ada_weight):
    half_freq = ada_weight.shape[0] // 2
    frequency = jnp.exp(-math.log(10000.0) * jnp.arange(half_freq, dtype=jnp.float32) / half_freq)
    angles = timesteps.astype(jnp.float32)[:, None] * frequency[None, :]
    embedding = jnp.concatenate([jnp.cos(angles), jnp.sin(angles)], axis=1).astype(jnp.bfloat16)
    return jnp.dot(embedding, ada_weight, preferred_element_type=jnp.float32)

def normalize(inputs, rows_mod):
    model_width = inputs.shape[-1]
    values = inputs.astype(jnp.float32)
    average = lax.optimization_barrier(jnp.mean(values, axis=-1, keepdims=True))
    variance = lax.optimization_barrier(jnp.mean((values - average) ** 2, axis=-1, keepdims=True))
    inverse_std = lax.rsqrt(variance + norm_eps)
    centered = (values - average) * inverse_std
    shift_rows = rows_mod[:, None, None, :model_width]
    scale_rows = rows_mod[:, None, None, model_width:]
    normed = (centered * (1.0 + scale_rows) + shift_rows).astype(jnp.bfloat16)
    return (normed, centered, inverse_std, scale_rows)

def normalize_back(normed_grads, centered, inverse_std, scale_rows):
    upstream = normed_grads.astype(jnp.float32) * (1.0 + scale_rows)
    first = lax.optimization_barrier(jnp.mean(upstream, axis=-1, keepdims=True))
    second = lax.optimization_barrier(jnp.mean(upstream * centered, axis=-1, keepdims=True))
    return (inverse_std * (upstream - first - centered * second)).astype(jnp.bfloat16)

def attend(projected, cot_block, head_count):
    inner = cot_block.shape[-1]
    head_size = inner // head_count
    factor = 1.0 / math.sqrt(head_size)
    lead = projected.shape[:-1]
    split_shape = lead + (head_count, head_size)
    query = projected[..., :inner].reshape(split_shape).astype(jnp.float32)
    keys = projected[..., inner:2 * inner].reshape(split_shape).astype(jnp.float32)
    values = projected[..., 2 * inner:].reshape(split_shape).astype(jnp.float32)
    out_grad = cot_block.reshape(split_shape).astype(jnp.float32)
    high = lax.Precision.HIGHEST
    scores = jnp.einsum('cfphd,cgphd->cphfg', query, keys, precision=high) * factor
    top = lax.optimization_barrier(jnp.max(scores, axis=-1, keepdims=True))
    expo = jnp.exp(scores - top)
    attention = expo / lax.optimization_barrier(jnp.sum(expo, axis=-1, keepdims=True))
    attention_low = attention.astype(jnp.bfloat16).astype(jnp.float32)
    value_grad = jnp.einsum('cphfg,cfphd->cgphd', attention_low, out_grad, precision=high)
    prob_grad = jnp.einsum('cfphd,cgphd->cphfg', out_grad, values, precision=high)
    row_dot = lax.optimization_barrier(jnp.sum(attention * prob_grad, axis=-1, keepdims=True))
    score_grad = (attention * (prob_grad - row_dot)).astype(jnp.bfloat16).astype(jnp.float32)
    query_grad = jnp.einsum('cphfg,cgphd->cfphd', score_grad, keys, precision=high) * factor
    key_grad = jnp.einsum('cphfg,cfphd->cgphd', score_grad, query, precision=high) * factor
    joined = jnp.concatenate([query_grad.reshape(lead + (inner,)), key_grad.reshape(lead + (inner,)), value_grad.reshape(lead + (inner,))], axis=-1)
    return joined.astype(jnp.bfloat16)

def reference(hidden, timesteps, ada_weight, master, ema_slow, ema_fast, step_count, cotangent):
    inner = HEADS * HDIM
    modulation = modulate_table(timesteps, ada_weight)
    weights_low = master.astype(jnp.bfloat16)
    blocks = CLIPS // CLIPS_DEV
    hidden_blocks = hidden.reshape(blocks, CLIPS_DEV, FRAMES, PATCHES, D)
    cot_blocks = cotangent.reshape(blocks, CLIPS_DEV, FRAMES, PATCHES, inner)
    mod_blocks = modulation.reshape(blocks, CLIPS_DEV, 2 * D)

    def block_step(running, block):
        inputs, rows_mod, cot_block = block
        normed, centered, inverse_std, scale_rows = normalize(inputs, rows_mod)
        projected = jnp.dot(normed.reshape(-1, D), weights_low, preferred_element_type=jnp.float32)
        projected = projected.astype(jnp.bfloat16).reshape(CLIPS_DEV, FRAMES, PATCHES, 3 * inner)
        projected_grads = attend(projected, cot_block, HEADS)
        grouped_rows = normed.astype(jnp.float32).reshape(CLIPS_DEV, N_SEQ, FR_DEV, PATCHES, D)
        grouped_grads = projected_grads.astype(jnp.float32).reshape(CLIPS_DEV, N_SEQ, FR_DEV, PATCHES, 3 * inner)
        partials = jnp.einsum('cgrpd,cgrpe->gde', grouped_rows, grouped_grads, precision=lax.Precision.HIGHEST)
        rounded = lax.optimization_barrier(partials.astype(jnp.bfloat16)).astype(jnp.float32)
        running = running + lax.optimization_barrier(jnp.sum(rounded, axis=0))
        normed_grads = jnp.dot(projected_grads.reshape(-1, 3 * inner), weights_low.T, preferred_element_type=jnp.float32)
        normed_grads = normed_grads.astype(jnp.bfloat16).reshape(CLIPS_DEV, FRAMES, PATCHES, D)
        input_grads = normalize_back(normed_grads, centered, inverse_std, scale_rows)
        return (running, input_grads)
    start_total = jnp.zeros((D, 3 * inner), jnp.float32)
    total, grads_out = lax.scan(block_step, start_total, (hidden_blocks, mod_blocks, cot_blocks))
    hidden_grad = grads_out.reshape(CLIPS, FRAMES, PATCHES, D)
    weight_grad = total / loss_scale
    base = 1.0 - 1.0 / step_count[0].astype(jnp.float32)
    decay_slow = jnp.power(base, gamma_slow + 1.0)
    decay_fast = jnp.power(base, gamma_fast + 1.0)
    ema_slow_next = decay_slow * ema_slow + (1.0 - decay_slow) * weight_grad
    ema_fast_next = decay_fast * ema_fast + (1.0 - decay_fast) * weight_grad
    return (hidden_grad, ema_slow_next, ema_fast_next)
```

```python
import math

import jax
import jax.numpy as jnp
from jax import lax
from jax.experimental import pallas as pl
from jax.experimental.pallas import tpu as pltpu
from jax.sharding import Mesh
from jax.sharding import PartitionSpec as P

HEADS = 8
HDIM = 72
norm_eps = 1e-06
loss_scale = 128.0
gamma_slow = 16.97
gamma_fast = 6.94
AXES = ("xh", "z", "c", "xl", "y")
SEQ = ("xl", "y")
ROWS = ("xh", "z")
F32 = jnp.float32
BF16 = jnp.bfloat16
MIB = 1024 * 1024


def params(mib=48):
    return pltpu.CompilerParams(vmem_limit_bytes=mib * MIB)


def cost(flops, moved):
    return pl.CostEstimate(flops=flops, bytes_accessed=moved, transcendentals=0)


def swap(value, axis):
    return lax.ppermute(value, axis, [(0, 1), (1, 0)])


def modulate_table(timesteps, ada_weight):
    half_freq = ada_weight.shape[0] // 2
    frequency = jnp.exp(-math.log(10000.0) * jnp.arange(half_freq, dtype=F32) / half_freq)
    angles = timesteps.astype(F32)[:, None] * frequency[None, :]
    embedding = jnp.concatenate([jnp.cos(angles), jnp.sin(angles)], axis=1).astype(BF16)
    return jnp.dot(embedding, ada_weight, preferred_element_type=F32)


def pack_kernel(hidden_ref, cot_ref, out_ref):
    width = hidden_ref.shape[1]
    out_ref[:, :width] = hidden_ref[...]
    out_ref[:, width:] = cot_ref[...].T


def stats(values):
    average = jnp.mean(values, axis=-1, keepdims=True)
    moved = values - average
    variance = jnp.mean(moved * moved, axis=-1, keepdims=True)
    inverse_std = lax.rsqrt(variance + norm_eps)
    return moved * inverse_std, inverse_std


def norm_kernel(packed_ref, mod_ref, out_ref):
    width = mod_ref.shape[1] // 2
    centered, _ = stats(packed_ref[:, :width].astype(F32))
    normed = centered * (1.0 + mod_ref[:, width:]) + mod_ref[:, :width]
    out_ref[:, :width] = normed.astype(BF16)
    out_ref[:, width:] = packed_ref[:, width:]


def norm_back_kernel(packed_ref, mod_ref, part_ref, other_ref, out_ref):
    width = mod_ref.shape[1] // 2
    centered, inverse_std = stats(packed_ref[:, :width].astype(F32))
    grads = (part_ref[...].astype(F32) + other_ref[...].astype(F32)).astype(BF16).astype(F32)
    upstream = grads * (1.0 + mod_ref[:, width:])
    first = jnp.mean(upstream, axis=-1, keepdims=True)
    second = jnp.mean(upstream * centered, axis=-1, keepdims=True)
    out_ref[...] = (inverse_std * (upstream - first - centered * second)).astype(BF16)


def dot(left, right, over):
    return lax.dot_general(left, right, ((over[0], over[1]), ((), ())), preferred_element_type=F32)


def attend_block(projected, out_grad, same, lane):
    factor = 1.0 / math.sqrt(HDIM)
    wide = 2 * HDIM
    query = projected[:, :wide]
    keys = projected[:, wide : 2 * wide]
    values = projected[:, 2 * wide :].astype(BF16)
    query_low, keys_low = query.astype(BF16), keys.astype(BF16)
    query_grad = key_grad = value_grad = None
    for head in range(2):
        mine = (lane >= head * HDIM) & (lane < (head + 1) * HDIM)
        own_query = jnp.where(mine, query, 0.0).astype(BF16)
        own_keys = jnp.where(mine, keys, 0.0).astype(BF16)
        own_out = jnp.where(mine, out_grad, 0.0).astype(BF16)
        scores = dot(own_query, keys_low, ((1,), (1,))) * factor
        scores = jnp.where(same, scores, -1e30)
        top = jnp.max(scores, axis=-1, keepdims=True)
        expo = jnp.exp(scores - top)
        attention = expo / jnp.sum(expo, axis=-1, keepdims=True)
        prob_grad = dot(own_out, values, ((1,), (1,)))
        row_dot = jnp.sum(attention * prob_grad, axis=-1, keepdims=True)
        score_grad = (attention * (prob_grad - row_dot)).astype(BF16)
        parts = (
            dot(score_grad, own_keys, ((1,), (0,))),
            dot(score_grad, own_query, ((0,), (0,))),
            dot(attention.astype(BF16), own_out, ((0,), (0,))),
        )
        if head == 0:
            query_grad, key_grad, value_grad = parts
        else:
            query_grad, key_grad, value_grad = (
                query_grad + parts[0],
                key_grad + parts[1],
                value_grad + parts[2],
            )
    return jnp.concatenate([query_grad * factor, key_grad * factor, value_grad], axis=1)


def main_kernel(spot_ref, own_ref, core_ref, side_ref, both_ref, weight_ref, grads_ref, wgrad_ref, total_ref):
    tokens = own_ref.shape[0]
    model_width = weight_ref.shape[0]
    quarter = weight_ref.shape[1] // 3
    spot = spot_ref[0]
    row = lax.broadcasted_iota(jnp.int32, (tokens, tokens), 0)
    col = lax.broadcasted_iota(jnp.int32, (tokens, tokens), 1)
    same = lax.rem(row, 16) == lax.rem(col, 16)
    lane = lax.broadcasted_iota(jnp.int32, (tokens, quarter), 1)
    for index, ref in enumerate((own_ref, core_ref, side_ref, both_ref)):
        projected = dot(ref[:, :model_width], weight_ref[...], ((1,), (0,)))
        projected = projected.astype(BF16).astype(F32)
        cot = ref[:, model_width:].astype(F32)
        out_grad = cot[:, :quarter]
        for other in range(1, 4):
            out_grad = jnp.where(spot == other, cot[:, other * quarter : (other + 1) * quarter], out_grad)
        grads = attend_block(projected, out_grad, same, lane).astype(BF16)
        grads_ref[index * tokens : (index + 1) * tokens, :] = grads
        part = dot(ref[:, :model_width], grads, ((0,), (0,)))
        if index == 0:
            total_ref[...] = part
        elif index < 3:
            total_ref[...] += part
        else:
            wgrad_ref[...] = (total_ref[...] + part).astype(BF16)


def input_kernel(grads_ref, weight_ref, near_ref, far_ref):
    half = near_ref.shape[0] // 2
    for index, (ref, place) in enumerate(((near_ref, 0), (far_ref, 0), (near_ref, 1), (far_ref, 1))):
        part = dot(grads_ref[index * half : (index + 1) * half, :], weight_ref[...], ((1,), (1,)))
        ref[place * half : (place + 1) * half, :] = part.astype(BF16)


def add_kernel(near_ref, got_ref, own_ref, side_ref):
    half = own_ref.shape[0]
    own_ref[...] = (near_ref[:half].astype(F32) + got_ref[:half].astype(F32)).astype(BF16)
    side_ref[...] = (near_ref[half:].astype(F32) + got_ref[half:].astype(F32)).astype(BF16)


def sum_kernel(parts_ref, out_ref):
    total = parts_ref[0].astype(F32)
    for index in range(1, parts_ref.shape[0]):
        total = total + parts_ref[index].astype(F32)
    out_ref[...] = total.astype(out_ref.dtype)


def call(kernel, outs, *args, flops=0, scratch=(), mib=48, smem=0):
    moved = sum(a.size * a.dtype.itemsize for a in args)
    moved += sum(math.prod(shape) * jnp.dtype(kind).itemsize for shape, kind in outs)
    shapes = [jax.ShapeDtypeStruct(shape, kind) for shape, kind in outs]
    specs = [pl.BlockSpec(memory_space=pltpu.SMEM if i < smem else pltpu.VMEM) for i in range(len(args))]
    got = pl.pallas_call(
        kernel,
        out_shape=shapes,
        in_specs=specs,
        out_specs=[pl.BlockSpec(memory_space=pltpu.VMEM)] * len(shapes),
        scratch_shapes=list(scratch),
        compiler_params=params(mib),
        cost_estimate=cost(flops, moved),
    )(*args)
    return got[0] if len(got) == 1 else got


def on_device(hidden, timesteps, ada_weight, master, ema_slow, ema_fast, step_count, cotangent):
    patches, width = hidden.shape[2:]
    inner = cotangent.shape[3]
    own_rows, triple = master.shape
    wide = width + inner
    n_seq = lax.axis_size("xl") * lax.axis_size("y")
    n_rows = lax.axis_size("xh") * lax.axis_size("z")
    n_y = lax.axis_size("y")
    quarter = inner // 4
    core, side = lax.axis_index("c"), lax.axis_index("xl")
    spot = 2 * core + side
    spot_arr = spot.astype(jnp.int32).reshape(1)

    packed = call(pack_kernel, [((patches, wide), BF16)], hidden[0, 0], cotangent[0, 0].T)
    tokens = lax.all_to_all(packed.reshape(n_seq, patches // n_seq, wide), SEQ, 0, 0, tiled=True)
    tokens = tokens.reshape(patches, wide)

    low = master.astype(BF16).reshape(own_rows, 3, 4, quarter)
    mine = lax.dynamic_index_in_dim(low, spot, 2, False).reshape(own_rows, 3 * quarter)
    theirs = lax.dynamic_index_in_dim(low, 2 * (1 - core) + side, 2, False).reshape(own_rows, 3 * quarter)
    theirs = swap(theirs, "c")
    pair = jnp.where(core == 0, jnp.concatenate([mine, theirs]), jnp.concatenate([theirs, mine]))
    copies = jnp.broadcast_to(pair[None], (n_rows,) + pair.shape)
    copies, tokens = lax.optimization_barrier((copies, tokens))
    weights = lax.all_to_all(copies, ROWS, 0, 0, tiled=True).reshape(width, 3 * quarter)

    modulation = modulate_table(timesteps, ada_weight)
    own = call(norm_kernel, [((patches, wide), BF16)], tokens, modulation)
    from_side = swap(own, "xl")
    from_core = swap(own, "c")
    from_both = swap(from_side, "c")

    grads, wgrad = call(
        main_kernel,
        [((4 * patches, 3 * quarter), BF16), ((width, 3 * quarter), BF16)],
        spot_arr, own, from_core, from_side, from_both, weights,
        flops=4 * 4 * patches * width * 3 * quarter,
        scratch=[pltpu.VMEM((width, 3 * quarter), F32)],
        smem=1,
    )

    parts = lax.all_to_all(wgrad.reshape(n_rows, 2 * own_rows, 3 * quarter), ROWS, 0, 0, tiled=True)
    summed = call(sum_kernel, [((2 * own_rows, 3 * quarter), BF16)], parts)
    summed = jnp.broadcast_to(summed[None], (n_y,) + summed.shape)
    parts = lax.all_to_all(summed, "y", 0, 0, tiled=True)
    total = call(sum_kernel, [((2 * own_rows, 3 * quarter), F32)], parts)
    keep = jnp.where(core == 0, total[:own_rows], total[own_rows:])
    give = jnp.where(core == 0, total[own_rows:], total[:own_rows])
    got = swap(give, "c")
    both = jnp.where(core == 0, jnp.stack([keep, got]), jnp.stack([got, keep]))
    over = swap(both, "xl")
    four = jnp.where(side == 0, jnp.stack([both, over], 1), jnp.stack([over, both], 1))
    four = four.reshape(4, own_rows, 3, quarter).transpose(1, 2, 0, 3)
    weight_grad = four.reshape(own_rows, triple) / loss_scale

    near, far = call(
        input_kernel,
        [((2 * patches, width), BF16), ((2 * patches, width), BF16)],
        grads, weights,
        flops=8 * patches * width * 3 * quarter,
    )
    got = swap(far, "c")
    part, give = call(add_kernel, [((patches, width), BF16)] * 2, near, got)
    got = swap(give, "xl")
    back = call(norm_back_kernel, [((patches, width), BF16)], tokens, modulation, part, got)
    back = lax.all_to_all(back.reshape(n_seq, patches // n_seq, width), SEQ, 0, 0, tiled=True)
    hidden_grad = back.reshape(hidden.shape)

    base = 1.0 - 1.0 / step_count[0].astype(F32)
    decay_slow = jnp.power(base, gamma_slow + 1.0)
    decay_fast = jnp.power(base, gamma_fast + 1.0)
    ema_slow_next = decay_slow * ema_slow + (1.0 - decay_slow) * weight_grad
    ema_fast_next = decay_fast * ema_fast + (1.0 - decay_fast) * weight_grad
    return (hidden_grad, ema_slow_next, ema_fast_next)


def solution(mesh):
    fine = Mesh(mesh.devices.reshape(2, 8, 2, 2, 8), AXES)
    dp, seq = ("xh", "z", "c"), SEQ
    placed = (
        P(dp, seq, None, None),
        P(dp),
        P(),
        P(dp, None),
        P(dp, None),
        P(dp, None),
        P(),
        P(dp, seq, None, None),
    )
    return jax.shard_map(
        on_device,
        mesh=fine,
        in_specs=placed,
        out_specs=(P(dp, seq, None, None), P(dp, None), P(dp, None)),
        check_vma=False,
    )
```

```python
import math

import jax
import jax.numpy as jnp
from jax import lax
from jax.experimental import pallas as pl
from jax.experimental.pallas import tpu as pltpu
from jax.sharding import Mesh
from jax.sharding import PartitionSpec as P

HEADS = 8
HDIM = 72
norm_eps = 1e-06
loss_scale = 128.0
gamma_slow = 16.97
gamma_fast = 6.94
AXES = ("xh", "z", "c", "xl", "y")
SEQ = ("xl", "y")
F32 = jnp.float32
BF16 = jnp.bfloat16
MIB = 1024 * 1024


def params(mib=48):
    return pltpu.CompilerParams(vmem_limit_bytes=mib * MIB)


def cost(flops, moved):
    return pl.CostEstimate(flops=flops, bytes_accessed=moved, transcendentals=0)


def swap(value, axis):
    return lax.ppermute(value, axis, [(0, 1), (1, 0)])


def shift(value, away):
    count = lax.axis_size("z")
    return lax.ppermute(value, "z", [(i, (i + away) % count) for i in range(count)])


def half_turn(value):
    return shift(value, lax.axis_size("z") // 2)


def both_turn(value):
    count = lax.axis_size("z")
    pairs = [(i, (count - count * (i // count)) + (i % count + count // 2) % count) for i in range(2 * count)]
    return lax.ppermute(value, ("xh", "z"), pairs)


def corner_swap(value):
    return lax.ppermute(value, ("c", "xl"), [(i, 3 - i) for i in range(4)])


def modulate_table(timesteps, ada_weight):
    half_freq = ada_weight.shape[0] // 2
    frequency = jnp.exp(-math.log(10000.0) * jnp.arange(half_freq, dtype=F32) / half_freq)
    angles = timesteps.astype(F32)[:, None] * frequency[None, :]
    embedding = jnp.concatenate([jnp.cos(angles), jnp.sin(angles)], axis=1).astype(BF16)
    return jnp.dot(embedding, ada_weight, preferred_element_type=F32)


def pack_kernel(hidden_ref, cot_ref, out_ref):
    width = hidden_ref.shape[1]
    out_ref[:, :width] = hidden_ref[...]
    out_ref[:, width:] = cot_ref[...].T


def stats(values):
    average = jnp.mean(values, axis=-1, keepdims=True)
    moved = values - average
    variance = jnp.mean(moved * moved, axis=-1, keepdims=True)
    inverse_std = lax.rsqrt(variance + norm_eps)
    return moved * inverse_std, inverse_std


def pick(spot, pieces):
    out = pieces[0]
    for index in range(1, 4):
        out = jnp.where(spot == index, pieces[index], out)
    return out


def norm_kernel(spot_ref, packed_ref, mod_ref, own_ref, core_ref, side_ref):
    width = mod_ref.shape[1] // 2
    quarter = (packed_ref.shape[1] - width) // 4
    centered, _ = stats(packed_ref[:, :width].astype(F32))
    normed = (centered * (1.0 + mod_ref[:, width:]) + mod_ref[:, :width]).astype(BF16)
    cot = packed_ref[:, width:].astype(F32)
    pieces = [cot[:, i * quarter : (i + 1) * quarter] for i in range(4)]
    spot = spot_ref[0]
    own, side, core, both = (pick(spot, [pieces[i ^ flip] for i in range(4)]) for flip in range(4))
    own_ref[:, :width] = normed
    own_ref[:, width : width + quarter] = own.astype(BF16)
    core_ref[:, :width] = normed
    core_ref[:, width : width + quarter] = core.astype(BF16)
    side_ref[:, :width] = normed
    side_ref[:, width : width + 2 * quarter] = jnp.concatenate([side, both], axis=1).astype(BF16)


def norm_back_kernel(packed_ref, mod_ref, *refs):
    out_ref = refs[-1]
    width = mod_ref.shape[1] // 2
    centered, inverse_std = stats(packed_ref[:, :width].astype(F32))
    grads = refs[0][...].astype(F32)
    for ref in refs[1:-1]:
        grads = grads + ref[...].astype(F32)
    grads = grads.astype(BF16).astype(F32)
    upstream = grads * (1.0 + mod_ref[:, width:])
    first = jnp.mean(upstream, axis=-1, keepdims=True)
    second = jnp.mean(upstream * centered, axis=-1, keepdims=True)
    out_ref[...] = (inverse_std * (upstream - first - centered * second)).astype(BF16)


def dot(left, right, over):
    return lax.dot_general(left, right, ((over[0], over[1]), ((), ())), preferred_element_type=F32)


def attend_block(projected, out_grad, same, lane):
    factor = 1.0 / math.sqrt(HDIM)
    wide = 2 * HDIM
    query = projected[:, :wide]
    keys = projected[:, wide : 2 * wide]
    values = projected[:, 2 * wide :].astype(BF16)
    query_low, keys_low = query.astype(BF16), keys.astype(BF16)
    query_grad = key_grad = value_grad = None
    for head in range(2):
        mine = (lane >= head * HDIM) & (lane < (head + 1) * HDIM)
        own_query = jnp.where(mine, query, 0.0).astype(BF16)
        own_keys = jnp.where(mine, keys, 0.0).astype(BF16)
        own_out = jnp.where(mine, out_grad, 0.0).astype(BF16)
        scores = dot(own_query, keys_low, ((1,), (1,))) * factor
        scores = jnp.where(same, scores, -1e30)
        top = jnp.max(scores, axis=-1, keepdims=True)
        expo = jnp.exp(scores - top)
        attention = expo / jnp.sum(expo, axis=-1, keepdims=True)
        prob_grad = dot(own_out, values, ((1,), (1,)))
        row_dot = jnp.sum(attention * prob_grad, axis=-1, keepdims=True)
        score_grad = (attention * (prob_grad - row_dot)).astype(BF16)
        parts = (
            dot(score_grad, own_keys, ((1,), (0,))),
            dot(score_grad, own_query, ((0,), (0,))),
            dot(attention.astype(BF16), own_out, ((0,), (0,))),
        )
        if head == 0:
            query_grad, key_grad, value_grad = parts
        else:
            query_grad, key_grad, value_grad = (
                query_grad + parts[0],
                key_grad + parts[1],
                value_grad + parts[2],
            )
    return jnp.concatenate([query_grad * factor, key_grad * factor, value_grad], axis=1)


def main_kernel(spot_ref, own_ref, core_ref, side_ref, both_ref, weight_ref, grads_ref, near_ref, up_ref, down_ref, low_ref, high_ref, total_ref):
    tokens = own_ref.shape[0]
    model_width = weight_ref.shape[0]
    quarter = weight_ref.shape[1] // 3
    row = lax.broadcasted_iota(jnp.int32, (tokens, tokens), 0)
    col = lax.broadcasted_iota(jnp.int32, (tokens, tokens), 1)
    same = lax.rem(row, 16) == lax.rem(col, 16)
    lane = lax.broadcasted_iota(jnp.int32, (tokens, quarter), 1)
    for index, (ref, skip) in enumerate(((own_ref, 0), (core_ref, 0), (side_ref, 0), (both_ref, 1))):
        projected = dot(ref[:, :model_width], weight_ref[...], ((1,), (0,)))
        projected = projected.astype(BF16).astype(F32)
        cot = ref[:, model_width:].astype(F32)
        out_grad = cot[:, skip * quarter : (skip + 1) * quarter]
        grads = attend_block(projected, out_grad, same, lane).astype(BF16)
        grads_ref[index * tokens : (index + 1) * tokens, :] = grads
        part = dot(ref[:, :model_width], grads, ((0,), (0,)))
        if index == 0:
            total_ref[...] = part
        else:
            total_ref[...] += part
    place = spot_ref[1]
    height = model_width // 16
    for ahead, targets in enumerate(((near_ref,), (up_ref,), (low_ref, high_ref), (down_ref,))):
        lowest = lax.rem(place + ahead, 4)
        for group in range(4):
            ref = targets[group * len(targets) // 4]
            first = pl.multiple_of((4 * group + lowest) * height, 8)
            ref[group % ref.shape[0]] = total_ref[pl.ds(first, height), :].astype(BF16)


def input_kernel(grads_ref, weight_ref, *refs):
    height = refs[0].shape[0]
    for index, ref in enumerate(refs):
        part = dot(grads_ref[index * height : (index + 1) * height, :], weight_ref[...], ((1,), (1,)))
        ref[...] = part.astype(BF16)


def columns_kernel(spot_ref, master_ref, mine_ref, theirs_ref):
    quarter = master_ref.shape[1] // 12
    spot = spot_ref[0]
    for flip, ref in ((0, mine_ref), (2, theirs_ref)):
        parts = []
        for part in range(3):
            pieces = [master_ref[:, (4 * part + i) * quarter : (4 * part + i + 1) * quarter] for i in range(4)]
            parts.append(pick(spot, [pieces[i ^ flip] for i in range(4)]))
        ref[...] = jnp.concatenate(parts, axis=1).astype(BF16)


def pair_kernel(spot_ref, mine_ref, theirs_ref, out_ref):
    mine, theirs = mine_ref[...].astype(F32), theirs_ref[...].astype(F32)
    first = spot_ref[0] < 2
    upper, lower = jnp.where(first, mine, theirs), jnp.where(first, theirs, mine)
    out_ref[...] = jnp.concatenate([upper, lower], axis=0).astype(BF16)


def quad_kernel(spot_ref, own_ref, far_ref, across_ref, both_ref, out_ref):
    place = spot_ref[2]
    out_ref[place] = own_ref[...]
    out_ref[place + 1 - 2 * lax.rem(place, 2)] = far_ref[...]
    out_ref[lax.rem(place + 2, 4)] = across_ref[...]
    out_ref[3 - place] = both_ref[...]


def gather_kernel(spot_ref, near_ref, up_ref, low_ref, high_ref, down_ref, out_ref):
    place = spot_ref[1]
    for ahead, sources in enumerate(((near_ref,), (up_ref,), (low_ref, high_ref), (down_ref,))):
        lowest = lax.rem(place + ahead, 4)
        for group in range(4):
            ref = sources[group * len(sources) // 4]
            out_ref[4 * group + lowest] = ref[group % ref.shape[0]]


def reduce_kernel(spot_ref, near_ref, up_ref, low_ref, high_ref, down_ref, own_ref, far_ref, across_ref, both_ref, total_ref):
    place = spot_ref[2]
    for group in range(4):
        far = low_ref if group < 2 else high_ref
        total = near_ref[group].astype(F32) + up_ref[group].astype(F32)
        total_ref[group] = total + down_ref[group].astype(F32) + far[group % 2].astype(F32)
    own_ref[...] = total_ref[place]
    far_ref[...] = total_ref[place + 1 - 2 * lax.rem(place, 2)].astype(BF16)
    across_ref[...] = total_ref[lax.rem(place + 2, 4)].astype(BF16)
    both_ref[...] = total_ref[3 - place].astype(BF16)


def copies_kernel(own_ref, far_ref, across_ref, both_ref, out_ref):
    total = own_ref[...] + far_ref[...].astype(F32) + across_ref[...].astype(F32) + both_ref[...].astype(F32)
    total = total.astype(BF16)
    for index in range(out_ref.shape[0]):
        out_ref[index] = total


def rows_kernel(spot_ref, parts_ref, own_ref, other_ref):
    total = parts_ref[0].astype(F32)
    for index in range(1, parts_ref.shape[0]):
        total = total + parts_ref[index].astype(F32)
    height = own_ref.shape[0]
    first = spot_ref[0] < 2
    upper, lower = total[:height], total[height:]
    own_ref[...] = jnp.where(first, upper, lower)
    other_ref[...] = jnp.where(first, lower, upper)


def average_kernel(spot_ref, decay_ref, own_ref, side_ref, core_ref, both_ref, slow_ref, fast_ref, slow_out, fast_out):
    quarter = own_ref.shape[1] // 3
    spot = spot_ref[0]
    values = [ref[...] for ref in (own_ref, side_ref, core_ref, both_ref)]
    picked = [pick(spot, [values[i ^ place] for i in range(4)]) for place in range(4)]
    columns = [picked[place][:, part * quarter : (part + 1) * quarter] for part in range(3) for place in range(4)]
    grad = jnp.concatenate(columns, axis=1) / loss_scale
    slow_out[...] = decay_ref[0] * slow_ref[...] + (1.0 - decay_ref[0]) * grad
    fast_out[...] = decay_ref[1] * fast_ref[...] + (1.0 - decay_ref[1]) * grad


def call(kernel, outs, *args, flops=0, scratch=(), mib=48, smem=0):
    moved = sum(a.size * a.dtype.itemsize for a in args)
    moved += sum(math.prod(shape) * jnp.dtype(kind).itemsize for shape, kind in outs)
    shapes = [jax.ShapeDtypeStruct(shape, kind) for shape, kind in outs]
    specs = [pl.BlockSpec(memory_space=pltpu.SMEM if i < smem else pltpu.VMEM) for i in range(len(args))]
    got = pl.pallas_call(
        kernel,
        out_shape=shapes,
        in_specs=specs,
        out_specs=[pl.BlockSpec(memory_space=pltpu.VMEM)] * len(shapes),
        scratch_shapes=list(scratch),
        compiler_params=params(mib),
        cost_estimate=cost(flops, moved),
    )(*args)
    return got[0] if len(got) == 1 else got


def lanes(count):
    return -(-count // 128) * 128


def on_device(hidden, timesteps, ada_weight, master, ema_slow, ema_fast, step_count, cotangent):
    patches, width = hidden.shape[2:]
    inner = cotangent.shape[3]
    own_rows, triple = master.shape
    wide = width + inner
    n_seq = lax.axis_size("xl") * lax.axis_size("y")
    n_y = lax.axis_size("y")
    quarter = inner // 4
    cols = 3 * quarter
    pair_rows = 2 * own_rows
    core, side = lax.axis_index("c"), lax.axis_index("xl")
    across, along = lax.axis_index("xh"), lax.axis_index("z")
    spots = jnp.stack([2 * core + side, lax.rem(along, 4), 2 * across + along // 4]).astype(jnp.int32)

    packed = call(pack_kernel, [((patches, wide), BF16)], hidden[0, 0], cotangent[0, 0].T)
    tokens = lax.all_to_all(packed.reshape(n_seq, patches // n_seq, wide), SEQ, 0, 0, tiled=True)
    tokens = tokens.reshape(patches, wide)

    mine, theirs = call(columns_kernel, [((own_rows, cols), BF16)] * 2, spots, master, smem=1)
    pair = call(pair_kernel, [((pair_rows, cols), BF16)], spots, mine, swap(theirs, "c"), smem=1)
    quad = call(
        quad_kernel,
        [((4, pair_rows, cols), BF16)],
        spots, pair, half_turn(pair), swap(pair, "xh"), both_turn(pair),
        smem=1,
    )
    weights = call(
        gather_kernel,
        [((16, pair_rows, cols), BF16)],
        spots, quad, shift(quad, -1), shift(quad[:2], -2), shift(quad[2:], 2), shift(quad, 1),
        smem=1,
    ).reshape(width, cols)

    modulation = modulate_table(timesteps, ada_weight)
    narrow, broad = lanes(width + quarter), lanes(width + 2 * quarter)
    own, to_core, to_side = call(
        norm_kernel,
        [((patches, narrow), BF16), ((patches, narrow), BF16), ((patches, broad), BF16)],
        spots, tokens, modulation,
        smem=1,
    )
    from_side = swap(to_side, "xl")
    from_core = swap(to_core, "c")
    from_both = swap(from_side, "c")

    quads = ((4, pair_rows, cols), BF16)
    halves = ((2, pair_rows, cols), BF16)
    grads, near, up, down, low, high = call(
        main_kernel,
        [((4 * patches, cols), BF16), quads, quads, quads, halves, halves],
        spots, own, from_core, from_side, from_both, weights,
        flops=4 * 4 * patches * width * cols,
        scratch=[pltpu.VMEM((width, cols), F32)],
        smem=1,
    )

    block = (pair_rows, cols)
    own_part, far, beside, corner = call(
        reduce_kernel,
        [(block, F32), (block, BF16), (block, BF16), (block, BF16)],
        spots, near, shift(up, 1), shift(low, 2), shift(high, -2), shift(down, -1),
        scratch=[pltpu.VMEM((4,) + block, F32)],
        smem=1,
    )
    copies = call(
        copies_kernel,
        [((n_y,) + block, BF16)],
        own_part, half_turn(far), swap(beside, "xh"), both_turn(corner),
    )
    parts = lax.all_to_all(copies, "y", 0, 0, tiled=True)
    own_grad, other_grad = call(rows_kernel, [((own_rows, cols), F32)] * 2, spots, parts, smem=1)
    base = 1.0 - 1.0 / step_count[0].astype(F32)
    decays = jnp.stack([jnp.power(base, gamma_slow + 1.0), jnp.power(base, gamma_fast + 1.0)])
    ema_slow_next, ema_fast_next = call(
        average_kernel,
        [((own_rows, triple), F32)] * 2,
        spots, decays, own_grad, swap(own_grad, "xl"), swap(other_grad, "c"), corner_swap(other_grad), ema_slow, ema_fast,
        smem=2,
    )

    whole = ((patches, width), BF16)
    mine_in, core_in, side_in, both_in = call(
        input_kernel,
        [whole] * 4,
        grads, weights,
        flops=8 * patches * width * cols,
    )
    back = call(
        norm_back_kernel,
        [whole],
        tokens, modulation, mine_in, swap(core_in, "c"), swap(side_in, "xl"), corner_swap(both_in),
    )
    back = lax.all_to_all(back.reshape(n_seq, patches // n_seq, width), SEQ, 0, 0, tiled=True)
    return (back.reshape(hidden.shape), ema_slow_next, ema_fast_next)


def solution(mesh):
    fine = Mesh(mesh.devices.reshape(2, 8, 2, 2, 8), AXES)
    dp, seq = ("xh", "z", "c"), SEQ
    placed = (
        P(dp, seq, None, None),
        P(dp),
        P(),
        P(dp, None),
        P(dp, None),
        P(dp, None),
        P(),
        P(dp, seq, None, None),
    )
    return jax.shard_map(
        on_device,
        mesh=fine,
        in_specs=placed,
        out_specs=(P(dp, seq, None, None), P(dp, None), P(dp, None)),
        check_vma=False,
    )
```

```python
import math

import jax
import jax.numpy as jnp
from jax import lax
from jax.experimental import pallas as pl
from jax.experimental.pallas import tpu as pltpu
from jax.sharding import Mesh
from jax.sharding import PartitionSpec as P

HEADS = 8
HDIM = 72
norm_eps = 1e-06
loss_scale = 128.0
gamma_slow = 16.97
gamma_fast = 6.94
AXES = ("xh", "z", "c", "xl", "y")
SEQ = ("xl", "y")
ROWS = ("xh", "z")
F32 = jnp.float32
BF16 = jnp.bfloat16
MIB = 1024 * 1024


def params(mib=48):
    return pltpu.CompilerParams(vmem_limit_bytes=mib * MIB)


def cost(flops, moved):
    return pl.CostEstimate(flops=flops, bytes_accessed=moved, transcendentals=0)


def swap(value, axis):
    return lax.ppermute(value, axis, [(0, 1), (1, 0)])


def corner_swap(value):
    return lax.ppermute(value, ("c", "xl"), [(i, 3 - i) for i in range(4)])


def modulate_table(timesteps, ada_weight):
    half_freq = ada_weight.shape[0] // 2
    frequency = jnp.exp(-math.log(10000.0) * jnp.arange(half_freq, dtype=F32) / half_freq)
    angles = timesteps.astype(F32)[:, None] * frequency[None, :]
    embedding = jnp.concatenate([jnp.cos(angles), jnp.sin(angles)], axis=1).astype(BF16)
    return jnp.dot(embedding, ada_weight, preferred_element_type=F32)


def pack_kernel(hidden_ref, cot_ref, out_ref):
    width = hidden_ref.shape[1]
    out_ref[:, :width] = hidden_ref[...]
    out_ref[:, width:] = cot_ref[...].T


def stats(values):
    average = jnp.mean(values, axis=-1, keepdims=True)
    moved = values - average
    variance = jnp.mean(moved * moved, axis=-1, keepdims=True)
    inverse_std = lax.rsqrt(variance + norm_eps)
    return moved * inverse_std, inverse_std


def pick(spot, pieces):
    out = pieces[0]
    for index in range(1, 4):
        out = jnp.where(spot == index, pieces[index], out)
    return out


def norm_kernel(spot_ref, packed_ref, mod_ref, own_ref, core_ref, side_ref):
    width = mod_ref.shape[1] // 2
    quarter = (packed_ref.shape[1] - width) // 4
    centered, _ = stats(packed_ref[:, :width].astype(F32))
    normed = (centered * (1.0 + mod_ref[:, width:]) + mod_ref[:, :width]).astype(BF16)
    cot = packed_ref[:, width:].astype(F32)
    pieces = [cot[:, i * quarter : (i + 1) * quarter] for i in range(4)]
    spot = spot_ref[0]
    own, side, core, both = (pick(spot, [pieces[i ^ flip] for i in range(4)]) for flip in range(4))
    own_ref[:, :width] = normed
    own_ref[:, width : width + quarter] = own.astype(BF16)
    core_ref[:, :width] = normed
    core_ref[:, width : width + quarter] = core.astype(BF16)
    side_ref[:, :width] = normed
    side_ref[:, width : width + 2 * quarter] = jnp.concatenate([side, both], axis=1).astype(BF16)


def norm_back_kernel(packed_ref, mod_ref, *refs):
    out_ref = refs[-1]
    width = mod_ref.shape[1] // 2
    centered, inverse_std = stats(packed_ref[:, :width].astype(F32))
    grads = refs[0][...].astype(F32)
    for ref in refs[1:-1]:
        grads = grads + ref[...].astype(F32)
    grads = grads.astype(BF16).astype(F32)
    upstream = grads * (1.0 + mod_ref[:, width:])
    first = jnp.mean(upstream, axis=-1, keepdims=True)
    second = jnp.mean(upstream * centered, axis=-1, keepdims=True)
    out_ref[...] = (inverse_std * (upstream - first - centered * second)).astype(BF16)


def dot(left, right, over):
    return lax.dot_general(left, right, ((over[0], over[1]), ((), ())), preferred_element_type=F32)


def attend_block(projected, out_grad, same, lane):
    factor = 1.0 / math.sqrt(HDIM)
    wide = 2 * HDIM
    query = projected[:, :wide]
    keys = projected[:, wide : 2 * wide]
    values = projected[:, 2 * wide :].astype(BF16)
    query_low, keys_low = query.astype(BF16), keys.astype(BF16)
    query_grad = key_grad = value_grad = None
    for head in range(2):
        mine = (lane >= head * HDIM) & (lane < (head + 1) * HDIM)
        own_query = jnp.where(mine, query, 0.0).astype(BF16)
        own_keys = jnp.where(mine, keys, 0.0).astype(BF16)
        own_out = jnp.where(mine, out_grad, 0.0).astype(BF16)
        scores = dot(own_query, keys_low, ((1,), (1,))) * factor
        scores = jnp.where(same, scores, -1e30)
        top = jnp.max(scores, axis=-1, keepdims=True)
        expo = jnp.exp(scores - top)
        attention = expo / jnp.sum(expo, axis=-1, keepdims=True)
        prob_grad = dot(own_out, values, ((1,), (1,)))
        row_dot = jnp.sum(attention * prob_grad, axis=-1, keepdims=True)
        score_grad = (attention * (prob_grad - row_dot)).astype(BF16)
        parts = (
            dot(score_grad, own_keys, ((1,), (0,))),
            dot(score_grad, own_query, ((0,), (0,))),
            dot(attention.astype(BF16), own_out, ((0,), (0,))),
        )
        if head == 0:
            query_grad, key_grad, value_grad = parts
        else:
            query_grad, key_grad, value_grad = (
                query_grad + parts[0],
                key_grad + parts[1],
                value_grad + parts[2],
            )
    return jnp.concatenate([query_grad * factor, key_grad * factor, value_grad], axis=1)


def tiles_of(block):
    rows = [block[8 * i : 8 * i + 8] for i in range(block.shape[0] // 8)]
    tiles = [row[:, 128 * k : 128 * k + 128] for row in rows for k in range(3)]
    rest = [row[:, 384:] for row in rows] + [jnp.zeros_like(rows[0][:, 384:])]
    pad = jnp.zeros((8, 128 - 2 * rest[0].shape[1]), block.dtype)
    tiles += [jnp.concatenate([rest[i], rest[i + 1], pad], axis=1) for i in range(0, len(rest), 2)]
    return tiles


def block_of(tiles, height):
    count = height // 8
    rows = []
    for i in range(count):
        last = tiles[3 * count + i // 2][:, 48 * (i % 2) : 48 * (i % 2) + 48]
        rows.append(jnp.concatenate(tiles[3 * i : 3 * i + 3] + [last], axis=1))
    return jnp.concatenate(rows, axis=0)


def main_kernel(own_ref, core_ref, side_ref, both_ref, weight_ref, grads_ref, packed_ref, total_ref):
    tokens = own_ref.shape[0]
    model_width, cols = total_ref.shape
    quarter = cols // 3
    row = lax.broadcasted_iota(jnp.int32, (tokens, tokens), 0)
    col = lax.broadcasted_iota(jnp.int32, (tokens, tokens), 1)
    same = lax.rem(row, 16) == lax.rem(col, 16)
    lane = lax.broadcasted_iota(jnp.int32, (tokens, quarter), 1)
    for index, (ref, skip) in enumerate(((own_ref, 0), (core_ref, 0), (side_ref, 0), (both_ref, 1))):
        projected = dot(ref[:, :model_width], weight_ref[:, :cols], ((1,), (0,)))
        projected = projected.astype(BF16).astype(F32)
        cot = ref[:, model_width:].astype(F32)
        out_grad = cot[:, skip * quarter : (skip + 1) * quarter]
        grads = attend_block(projected, out_grad, same, lane).astype(BF16)
        grads_ref[index * tokens : (index + 1) * tokens, :] = grads
        part = dot(ref[:, :model_width], grads, ((0,), (0,)))
        if index == 0:
            total_ref[...] = part
        else:
            total_ref[...] += part
    height = model_width // 16
    pieces = packed_ref.shape[0] // 16
    for owner in range(16):
        tiles = tiles_of(total_ref[owner * height : (owner + 1) * height, :])
        each = len(tiles) // pieces
        for piece in range(pieces):
            packed_ref[owner * pieces + piece] = jnp.concatenate(tiles[each * piece : each * piece + each], axis=0).astype(BF16)


def input_kernel(grads_ref, weight_ref, *refs):
    height = refs[0].shape[0]
    for index, ref in enumerate(refs):
        part = dot(grads_ref[index * height : (index + 1) * height, :], weight_ref[:, : grads_ref.shape[1]], ((1,), (1,)))
        ref[...] = part.astype(BF16)


def columns_kernel(spot_ref, master_ref, mine_ref, theirs_ref):
    quarter = master_ref.shape[1] // 12
    spot = spot_ref[0]
    for flip, ref in ((0, mine_ref), (2, theirs_ref)):
        parts = []
        for part in range(3):
            pieces = [master_ref[:, (4 * part + i) * quarter : (4 * part + i + 1) * quarter] for i in range(4)]
            parts.append(pick(spot, [pieces[i ^ flip] for i in range(4)]))
        ref[...] = jnp.concatenate(parts, axis=1).astype(BF16)


def pair_kernel(spot_ref, mine_ref, theirs_ref, out_ref):
    mine, theirs = mine_ref[...].astype(F32), theirs_ref[...].astype(F32)
    first = spot_ref[0] < 2
    upper, lower = jnp.where(first, mine, theirs), jnp.where(first, theirs, mine)
    pair = jnp.concatenate([upper, lower], axis=0)
    rest = jnp.zeros((pair.shape[0], out_ref.shape[1] - pair.shape[1]), F32)
    out_ref[...] = jnp.concatenate([pair, rest], axis=1).astype(BF16)


def payload_kernel(parts_ref, back_ref, out_ref):
    total = parts_ref[0].astype(F32)
    for index in range(1, parts_ref.shape[0]):
        total = total + parts_ref[index].astype(F32)
    half = total.shape[0] // 2
    piece = jnp.concatenate([total[:half], total[half:]], axis=1).astype(BF16)
    width = back_ref.shape[1]
    out_ref[:, :width] = back_ref[...]
    for index in range(out_ref.shape[0] // half):
        out_ref[index * half : (index + 1) * half, width:] = piece


def rows_kernel(spot_ref, pieces_ref, own_ref, other_ref):
    width = pieces_ref.shape[2] - 256
    count = pieces_ref.shape[0] // 2
    height = own_ref.shape[1]
    first = spot_ref[0] < 2
    for side in range(2):
        tiles = []
        for index in range(count):
            piece = pieces_ref[side * count + index][:, width:].astype(F32)
            tiles += [piece[:8, :128], piece[8:, :128], piece[:8, 128:], piece[8:, 128:]]
        total = block_of(tiles, 2 * height)
        upper, lower = total[:height], total[height:]
        own_ref[side] = jnp.where(first, upper, lower)
        other_ref[side] = jnp.where(first, lower, upper)


def average_kernel(spot_ref, decay_ref, own_ref, core_ref, slow_ref, fast_ref, slow_out, fast_out):
    quarter = own_ref.shape[2] // 3
    first = spot_ref[0] < 2
    own, other = [own_ref[0], own_ref[1]], [core_ref[0], core_ref[1]]
    places = [jnp.where(first, a, b) for a, b in zip(own + other, other + own)]
    columns = [place[:, part * quarter : (part + 1) * quarter] for part in range(3) for place in places]
    grad = jnp.concatenate(columns, axis=1) / loss_scale
    slow_out[...] = decay_ref[0] * slow_ref[...] + (1.0 - decay_ref[0]) * grad
    fast_out[...] = decay_ref[1] * fast_ref[...] + (1.0 - decay_ref[1]) * grad


def call(kernel, outs, *args, flops=0, scratch=(), mib=16, smem=0):
    moved = sum(a.size * a.dtype.itemsize for a in args)
    moved += sum(math.prod(shape) * jnp.dtype(kind).itemsize for shape, kind in outs)
    shapes = [jax.ShapeDtypeStruct(shape, kind) for shape, kind in outs]
    specs = [pl.BlockSpec(memory_space=pltpu.SMEM if i < smem else pltpu.VMEM) for i in range(len(args))]
    got = pl.pallas_call(
        kernel,
        out_shape=shapes,
        in_specs=specs,
        out_specs=[pl.BlockSpec(memory_space=pltpu.VMEM)] * len(shapes),
        scratch_shapes=list(scratch),
        compiler_params=params(mib),
        cost_estimate=cost(flops, moved),
    )(*args)
    return got[0] if len(got) == 1 else got


def lanes(count):
    return -(-count // 128) * 128


def on_device(hidden, timesteps, ada_weight, master, ema_slow, ema_fast, step_count, cotangent):
    patches, width = hidden.shape[2:]
    inner = cotangent.shape[3]
    own_rows, triple = master.shape
    wide = width + inner
    n_seq = lax.axis_size("xl") * lax.axis_size("y")
    n_rows = lax.axis_size("xh") * lax.axis_size("z")
    n_y = lax.axis_size("y")
    quarter = inner // 4
    cols = 3 * quarter
    pair_rows = 2 * own_rows
    core, side = lax.axis_index("c"), lax.axis_index("xl")
    spots = jnp.stack([2 * core + side]).astype(jnp.int32)

    packed = call(pack_kernel, [((patches, wide), BF16)], hidden[0, 0], cotangent[0, 0].T)
    tokens = lax.all_to_all(packed.reshape(n_seq, patches // n_seq, wide), SEQ, 0, 0, tiled=True)
    tokens = tokens.reshape(patches, wide)

    mine, theirs = call(columns_kernel, [((own_rows, cols), BF16)] * 2, spots, master, smem=1)
    pair = call(pair_kernel, [((pair_rows, lanes(cols)), BF16)], spots, mine, swap(theirs, "c"), smem=1)
    weights = lax.all_gather(pair, ROWS, axis=0, tiled=True)

    modulation = modulate_table(timesteps, ada_weight)
    narrow, broad = lanes(width + quarter), lanes(width + 2 * quarter)
    own, to_core, to_side = call(
        norm_kernel,
        [((patches, narrow), BF16), ((patches, narrow), BF16), ((patches, broad), BF16)],
        spots, tokens, modulation,
        smem=1,
    )
    from_side = swap(to_side, "xl")
    from_core = swap(to_core, "c")
    from_side, from_core = lax.optimization_barrier((from_side, from_core))
    from_both = swap(from_side, "c")

    pieces = n_rows * n_y
    grads, packed = call(
        main_kernel,
        [((4 * patches, cols), BF16), ((pieces, 32, 128), BF16)],
        own, from_core, from_side, from_both, weights,
        flops=4 * 4 * patches * width * cols,
        scratch=[pltpu.VMEM((width, cols), F32)],
    )

    whole = ((patches, width), BF16)
    mine_in, core_in, side_in, both_in = call(
        input_kernel,
        [whole] * 4,
        grads, weights,
        flops=8 * patches * width * cols,
    )
    back = call(
        norm_back_kernel,
        [whole],
        tokens, modulation, mine_in, swap(core_in, "c"), swap(side_in, "xl"), corner_swap(both_in),
    )

    parts = lax.all_to_all(packed, ROWS + ("y",), 0, 0, tiled=True)
    joint = call(payload_kernel, [((patches, width + 256), BF16)], parts, back)
    joint = lax.all_to_all(joint.reshape(n_seq, patches // n_seq, width + 256), SEQ, 0, 0, tiled=True)
    own_grad, other_grad = call(rows_kernel, [((2, own_rows, cols), F32)] * 2, spots, joint, smem=1)
    base = 1.0 - 1.0 / step_count[0].astype(F32)
    decays = jnp.stack([jnp.power(base, gamma_slow + 1.0), jnp.power(base, gamma_fast + 1.0)])
    ema_slow_next, ema_fast_next = call(
        average_kernel,
        [((own_rows, triple), F32)] * 2,
        spots, decays, own_grad, swap(other_grad, "c"), ema_slow, ema_fast,
        smem=2,
    )
    return (joint[:, :, :width].reshape(hidden.shape), ema_slow_next, ema_fast_next)


def solution(mesh):
    fine = Mesh(mesh.devices.reshape(2, 8, 2, 2, 8), AXES)
    dp, seq = ("xh", "z", "c"), SEQ
    placed = (
        P(dp, seq, None, None),
        P(dp),
        P(),
        P(dp, None),
        P(dp, None),
        P(dp, None),
        P(),
        P(dp, seq, None, None),
    )
    return jax.shard_map(
        on_device,
        mesh=fine,
        in_specs=placed,
        out_specs=(P(dp, seq, None, None), P(dp, None), P(dp, None)),
        check_vma=False,
    )
```

```python
import math

import jax
import jax.numpy as jnp
from jax import lax
from jax.experimental import pallas as pl
from jax.experimental.pallas import tpu as pltpu
from jax.sharding import Mesh
from jax.sharding import PartitionSpec as P

HEADS = 8
HDIM = 72
norm_eps = 1e-06
loss_scale = 128.0
gamma_slow = 16.97
gamma_fast = 6.94
AXES = ("xh", "z", "c", "xl", "y")
SEQ = ("xl", "y")
ROWS = ("xh", "z")
F32 = jnp.float32
BF16 = jnp.bfloat16
MIB = 1024 * 1024


def params(mib=48):
    return pltpu.CompilerParams(vmem_limit_bytes=mib * MIB)


def cost(flops, moved):
    return pl.CostEstimate(flops=flops, bytes_accessed=moved, transcendentals=0)


def swap(value, axis):
    return lax.ppermute(value, axis, [(0, 1), (1, 0)])


def shift(value, away):
    count = lax.axis_size("z")
    return lax.ppermute(value, "z", [(i, (i + away) % count) for i in range(count)])


def half_turn(value):
    return shift(value, lax.axis_size("z") // 2)


def both_turn(value):
    count = lax.axis_size("z")
    pairs = [(i, (count - count * (i // count)) + (i % count + count // 2) % count) for i in range(2 * count)]
    return lax.ppermute(value, ("xh", "z"), pairs)


def modulate_table(timesteps, ada_weight):
    half_freq = ada_weight.shape[0] // 2
    frequency = jnp.exp(-math.log(10000.0) * jnp.arange(half_freq, dtype=F32) / half_freq)
    angles = timesteps.astype(F32)[:, None] * frequency[None, :]
    embedding = jnp.concatenate([jnp.cos(angles), jnp.sin(angles)], axis=1).astype(BF16)
    return jnp.dot(embedding, ada_weight, preferred_element_type=F32)


def pack_kernel(hidden_ref, cot_ref, out_ref):
    width = hidden_ref.shape[1]
    out_ref[:, :width] = hidden_ref[...]
    out_ref[:, width:] = cot_ref[...].T


def stats(values):
    average = jnp.mean(values, axis=-1, keepdims=True)
    moved = values - average
    variance = jnp.mean(moved * moved, axis=-1, keepdims=True)
    inverse_std = lax.rsqrt(variance + norm_eps)
    return moved * inverse_std, inverse_std


def pick(spot, pieces):
    out = pieces[0]
    for index in range(1, 4):
        out = jnp.where(spot == index, pieces[index], out)
    return out


def norm_kernel(spot_ref, packed_ref, mod_ref, own_ref, core_ref, side_ref, held_ref, sem):
    width = mod_ref.shape[1] // 2
    quarter = (packed_ref.shape[1] - width) // 4
    centered, _ = stats(packed_ref[:, :width].astype(F32))
    normed = (centered * (1.0 + mod_ref[:, width:]) + mod_ref[:, :width]).astype(BF16)
    cot = packed_ref[:, width:].astype(F32)
    pieces = [cot[:, i * quarter : (i + 1) * quarter] for i in range(4)]
    spot = spot_ref[0]
    own, side, core, both = (pick(spot, [pieces[i ^ flip] for i in range(4)]) for flip in range(4))
    held_ref[:, :width] = normed
    held_ref[:, width : width + quarter] = own.astype(BF16)
    copy = pltpu.make_async_copy(held_ref, own_ref, sem)
    copy.start()
    core_ref[:, :width] = normed
    core_ref[:, width : width + quarter] = core.astype(BF16)
    side_ref[:, :width] = normed
    side_ref[:, width : width + 2 * quarter] = jnp.concatenate([side, both], axis=1).astype(BF16)
    copy.wait()


def norm_back_kernel(packed_ref, mod_ref, *refs):
    out_ref = refs[-1]
    width = mod_ref.shape[1] // 2
    centered, inverse_std = stats(packed_ref[:, :width].astype(F32))
    grads = refs[0][...].astype(F32)
    for ref in refs[1:-1]:
        grads = grads + ref[...].astype(F32)
    grads = grads.astype(BF16).astype(F32)
    upstream = grads * (1.0 + mod_ref[:, width:])
    first = jnp.mean(upstream, axis=-1, keepdims=True)
    second = jnp.mean(upstream * centered, axis=-1, keepdims=True)
    out_ref[...] = (inverse_std * (upstream - first - centered * second)).astype(BF16)


def dot(left, right, over):
    return lax.dot_general(left, right, ((over[0], over[1]), ((), ())), preferred_element_type=F32)


def attend_block(projected, out_grad, same, lane):
    factor = 1.0 / math.sqrt(HDIM)
    wide = 2 * HDIM
    query = projected[:, :wide]
    keys = projected[:, wide : 2 * wide]
    values = projected[:, 2 * wide :].astype(BF16)
    query_low, keys_low = query.astype(BF16), keys.astype(BF16)
    query_grad = key_grad = value_grad = None
    for head in range(2):
        mine = (lane >= head * HDIM) & (lane < (head + 1) * HDIM)
        own_query = jnp.where(mine, query, 0.0).astype(BF16)
        own_keys = jnp.where(mine, keys, 0.0).astype(BF16)
        own_out = jnp.where(mine, out_grad, 0.0).astype(BF16)
        scores = dot(own_query, keys_low, ((1,), (1,))) * factor
        scores = jnp.where(same, scores, -1e30)
        top = jnp.max(scores, axis=-1, keepdims=True)
        expo = jnp.exp(scores - top)
        attention = expo / jnp.sum(expo, axis=-1, keepdims=True)
        prob_grad = dot(own_out, values, ((1,), (1,)))
        row_dot = jnp.sum(attention * prob_grad, axis=-1, keepdims=True)
        score_grad = (attention * (prob_grad - row_dot)).astype(BF16)
        parts = (
            dot(score_grad, own_keys, ((1,), (0,))),
            dot(score_grad, own_query, ((0,), (0,))),
            dot(attention.astype(BF16), own_out, ((0,), (0,))),
        )
        if head == 0:
            query_grad, key_grad, value_grad = parts
        else:
            query_grad, key_grad, value_grad = (
                query_grad + parts[0],
                key_grad + parts[1],
                value_grad + parts[2],
            )
    return jnp.concatenate([query_grad * factor, key_grad * factor, value_grad], axis=1)


def tiles_of(block):
    rows = [block[8 * i : 8 * i + 8] for i in range(block.shape[0] // 8)]
    tiles = [row[:, 128 * k : 128 * k + 128] for row in rows for k in range(3)]
    rest = [row[:, 384:] for row in rows] + [jnp.zeros_like(rows[0][:, 384:])]
    pad = jnp.zeros((8, 128 - 2 * rest[0].shape[1]), block.dtype)
    tiles += [jnp.concatenate([rest[i], rest[i + 1], pad], axis=1) for i in range(0, len(rest), 2)]
    return tiles


def block_of(tiles, height):
    count = height // 8
    rows = []
    for i in range(count):
        last = tiles[3 * count + i // 2][:, 48 * (i % 2) : 48 * (i % 2) + 48]
        rows.append(jnp.concatenate(tiles[3 * i : 3 * i + 3] + [last], axis=1))
    return jnp.concatenate(rows, axis=0)


def main_kernel(
    weight_hbm, own_hbm, core_hbm, side_hbm, both_hbm, packed_hbm, near_hbm, far_hbm,
    weight_ref, own_ref, core_ref, side_ref, both_ref, packed_ref, parts_ref, total_ref, in_sems, out_sems,
):
    tokens = own_ref.shape[0]
    model_width, cols = total_ref.shape
    quarter = cols // 3
    pairs = (
        (weight_hbm, weight_ref), (own_hbm, own_ref), (core_hbm, core_ref), (side_hbm, side_ref), (both_hbm, both_ref),
    )
    loads = [pltpu.make_async_copy(source, target, in_sems.at[i]) for i, (source, target) in enumerate(pairs)]
    for load in loads:
        load.start()
    row = lax.broadcasted_iota(jnp.int32, (tokens, tokens), 0)
    col = lax.broadcasted_iota(jnp.int32, (tokens, tokens), 1)
    same = lax.rem(row, 16) == lax.rem(col, 16)
    lane = lax.broadcasted_iota(jnp.int32, (tokens, quarter), 1)
    stores = []
    loads[0].wait()
    places = ((near_hbm, 0, 0), (far_hbm, 0, 0), (near_hbm, 1, 0), (far_hbm, 1, 1))
    for index, (target, place, skip) in enumerate(places):
        ref = pairs[index + 1][1]
        loads[index + 1].wait()
        projected = dot(ref[:, :model_width], weight_ref[...], ((1,), (0,)))
        projected = projected.astype(BF16).astype(F32)
        cot = ref[:, model_width:].astype(F32)
        out_grad = cot[:, skip * quarter : (skip + 1) * quarter]
        grads = attend_block(projected, out_grad, same, lane).astype(BF16)
        part = dot(ref[:, :model_width], grads, ((0,), (0,)))
        if index == 0:
            total_ref[...] = part
        else:
            total_ref[...] += part
        parts_ref[index] = dot(grads, weight_ref[...], ((1,), (1,))).astype(BF16)
        stores.append(
            pltpu.make_async_copy(
                parts_ref.at[index], target.at[pl.ds(place * tokens, tokens)], out_sems.at[index]
            )
        )
        stores[-1].start()
    height = model_width // 16
    pieces = packed_ref.shape[0] // 16
    for owner in range(16):
        tiles = tiles_of(total_ref[owner * height : (owner + 1) * height, :])
        each = len(tiles) // pieces
        for piece in range(pieces):
            packed_ref[owner * pieces + piece] = jnp.concatenate(tiles[each * piece : each * piece + each], axis=0).astype(BF16)
        if owner % 4 == 3:
            part = pl.ds((owner - 3) * pieces, 4 * pieces)
            stores.append(pltpu.make_async_copy(packed_ref.at[part], packed_hbm.at[part], out_sems.at[4 + owner // 4]))
            stores[-1].start()
    for store in stores:
        store.wait()


def add_kernel(near_ref, got_ref, own_ref, side_ref):
    half = own_ref.shape[0]
    side_ref[...] = (near_ref[half:].astype(F32) + got_ref[half:].astype(F32)).astype(BF16)
    own_ref[...] = (near_ref[:half].astype(F32) + got_ref[:half].astype(F32)).astype(BF16)


def columns_kernel(spot_ref, master_ref, mine_ref, theirs_ref):
    quarter = master_ref.shape[1] // 12
    spot = spot_ref[0]
    for flip, ref in ((0, mine_ref), (2, theirs_ref)):
        parts = []
        for part in range(3):
            pieces = [master_ref[:, (4 * part + i) * quarter : (4 * part + i + 1) * quarter] for i in range(4)]
            parts.append(pick(spot, [pieces[i ^ flip] for i in range(4)]))
        ref[...] = jnp.concatenate(parts, axis=1).astype(BF16)


def pair_kernel(spot_ref, mine_ref, theirs_ref, out_ref):
    mine, theirs = mine_ref[...].astype(F32), theirs_ref[...].astype(F32)
    first = spot_ref[0] < 2
    upper, lower = jnp.where(first, mine, theirs), jnp.where(first, theirs, mine)
    out_ref[...] = jnp.concatenate([upper, lower], axis=0).astype(BF16)


def quad_kernel(spot_ref, own_ref, far_ref, across_ref, both_ref, out_ref):
    place = spot_ref[2]
    out_ref[place] = own_ref[...]
    out_ref[place + 1 - 2 * lax.rem(place, 2)] = far_ref[...]
    out_ref[lax.rem(place + 2, 4)] = across_ref[...]
    out_ref[3 - place] = both_ref[...]


def gather_kernel(spot_ref, near_ref, up_ref, low_ref, high_ref, down_ref, out_ref):
    place = spot_ref[1]
    for ahead, sources in enumerate(((near_ref,), (up_ref,), (low_ref, high_ref), (down_ref,))):
        lowest = lax.rem(place + ahead, 4)
        for group in range(4):
            ref = sources[group * len(sources) // 4]
            out_ref[4 * group + lowest] = ref[group % ref.shape[0]]


def payload_kernel(parts_ref, back_ref, out_ref):
    total = parts_ref[0].astype(F32)
    for index in range(1, parts_ref.shape[0]):
        total = total + parts_ref[index].astype(F32)
    half = total.shape[0] // 2
    piece = jnp.concatenate([total[:half], total[half:]], axis=1).astype(BF16)
    width = back_ref.shape[1]
    out_ref[:, :width] = back_ref[...]
    for index in range(out_ref.shape[0] // half):
        out_ref[index * half : (index + 1) * half, width:] = piece


def rows_kernel(spot_ref, pieces_ref, own_ref, other_ref):
    width = pieces_ref.shape[2] - 256
    count = pieces_ref.shape[0] // 2
    height = own_ref.shape[1]
    first = spot_ref[0] < 2
    for side in range(2):
        tiles = []
        for index in range(count):
            piece = pieces_ref[side * count + index][:, width:].astype(F32)
            tiles += [piece[:8, :128], piece[8:, :128], piece[:8, 128:], piece[8:, 128:]]
        total = block_of(tiles, 2 * height)
        upper, lower = total[:height], total[height:]
        own_ref[side] = jnp.where(first, upper, lower)
        other_ref[side] = jnp.where(first, lower, upper)


def average_kernel(spot_ref, decay_ref, own_ref, core_ref, slow_ref, fast_ref, slow_out, fast_out):
    quarter = own_ref.shape[2] // 3
    first = spot_ref[0] < 2
    own, other = [own_ref[0], own_ref[1]], [core_ref[0], core_ref[1]]
    places = [jnp.where(first, a, b) for a, b in zip(own + other, other + own)]
    columns = [place[:, part * quarter : (part + 1) * quarter] for part in range(3) for place in places]
    grad = jnp.concatenate(columns, axis=1) / loss_scale
    slow_out[...] = decay_ref[0] * slow_ref[...] + (1.0 - decay_ref[0]) * grad
    fast_out[...] = decay_ref[1] * fast_ref[...] + (1.0 - decay_ref[1]) * grad


def call(kernel, outs, *args, flops=0, scratch=(), mib=16, smem=0, hbm_in=False, hbm_out=()):
    moved = sum(a.size * a.dtype.itemsize for a in args)
    moved += sum(math.prod(shape) * jnp.dtype(kind).itemsize for shape, kind in outs)
    shapes = [jax.ShapeDtypeStruct(shape, kind) for shape, kind in outs]
    body = pltpu.HBM if hbm_in else pltpu.VMEM
    specs = [pl.BlockSpec(memory_space=pltpu.SMEM if i < smem else body) for i in range(len(args))]
    got = pl.pallas_call(
        kernel,
        out_shape=shapes,
        in_specs=specs,
        out_specs=[pl.BlockSpec(memory_space=pltpu.HBM if i in hbm_out else pltpu.VMEM) for i in range(len(shapes))],
        scratch_shapes=list(scratch),
        compiler_params=params(mib),
        cost_estimate=cost(flops, moved),
    )(*args)
    return got[0] if len(got) == 1 else got


def lanes(count):
    return -(-count // 128) * 128


def on_device(hidden, timesteps, ada_weight, master, ema_slow, ema_fast, step_count, cotangent):
    patches, width = hidden.shape[2:]
    inner = cotangent.shape[3]
    own_rows, triple = master.shape
    wide = width + inner
    n_seq = lax.axis_size("xl") * lax.axis_size("y")
    n_rows = lax.axis_size("xh") * lax.axis_size("z")
    n_y = lax.axis_size("y")
    quarter = inner // 4
    cols = 3 * quarter
    pair_rows = 2 * own_rows
    core, side = lax.axis_index("c"), lax.axis_index("xl")
    across, along = lax.axis_index("xh"), lax.axis_index("z")
    spots = jnp.stack([2 * core + side, lax.rem(along, 4), 2 * across + along // 4]).astype(jnp.int32)

    packed = call(pack_kernel, [((patches, wide), BF16)], hidden[0, 0], cotangent[0, 0].T)
    tokens = lax.all_to_all(packed.reshape(n_seq, patches // n_seq, wide), SEQ, 0, 0, tiled=True)
    tokens = tokens.reshape(patches, wide)

    mine, theirs = call(columns_kernel, [((own_rows, cols), BF16)] * 2, spots, master, smem=1)
    pair = call(pair_kernel, [((pair_rows, cols), BF16)], spots, mine, swap(theirs, "c"), smem=1)
    quad = call(
        quad_kernel,
        [((4, pair_rows, cols), BF16)],
        spots, pair, half_turn(pair), swap(pair, "xh"), both_turn(pair),
        smem=1,
    )
    quad, tokens = lax.optimization_barrier((quad, tokens))

    modulation = modulate_table(timesteps, ada_weight)
    narrow, broad = lanes(width + quarter), lanes(width + 2 * quarter)
    own, to_core, to_side = call(
        norm_kernel,
        [((patches, narrow), BF16), ((patches, narrow), BF16), ((patches, broad), BF16)],
        spots, tokens, modulation,
        scratch=[pltpu.VMEM((patches, narrow), BF16), pltpu.SemaphoreType.DMA(())],
        smem=1,
        hbm_out=(0,),
    )
    from_side = swap(to_side, "xl")
    from_core = swap(to_core, "c")
    up, low, high, down = shift(quad, -1), shift(quad[:2], -2), shift(quad[2:], 2), shift(quad, 1)
    from_side, from_core, up, low, high, down = lax.optimization_barrier((from_side, from_core, up, low, high, down))
    from_both = swap(from_side, "c")
    weights = call(
        gather_kernel, [((16, pair_rows, cols), BF16)], spots, quad, up, low, high, down, smem=1
    ).reshape(width, cols)

    pieces = n_rows * n_y
    packed, near, far = call(
        main_kernel,
        [((pieces, 32, 128), BF16), ((2 * patches, width), BF16), ((2 * patches, width), BF16)],
        weights, own, from_core, from_side, from_both,
        flops=6 * 4 * patches * width * cols,
        scratch=[
            pltpu.VMEM((width, cols), BF16),
            pltpu.VMEM((patches, narrow), BF16),
            pltpu.VMEM((patches, narrow), BF16),
            pltpu.VMEM((patches, broad), BF16),
            pltpu.VMEM((patches, broad), BF16),
            pltpu.VMEM((pieces, 32, 128), BF16),
            pltpu.VMEM((4, patches, width), BF16),
            pltpu.VMEM((width, cols), F32),
            pltpu.SemaphoreType.DMA((5,)),
            pltpu.SemaphoreType.DMA((8,)),
        ],
        mib=58,
        hbm_in=True,
        hbm_out=(0, 1, 2),
    )

    part, give = call(add_kernel, [((patches, width), BF16)] * 2, near, swap(far, "c"))
    back = call(norm_back_kernel, [((patches, width), BF16)], tokens, modulation, part, swap(give, "xl"))

    parts = lax.all_to_all(packed, ROWS + ("y",), 0, 0, tiled=True)
    joint = call(payload_kernel, [((patches, width + 256), BF16)], parts, back)
    joint = lax.all_to_all(joint.reshape(n_seq, patches // n_seq, width + 256), SEQ, 0, 0, tiled=True)
    own_grad, other_grad = call(rows_kernel, [((2, own_rows, cols), F32)] * 2, spots, joint, smem=1)
    base = 1.0 - 1.0 / step_count[0].astype(F32)
    decays = jnp.stack([jnp.power(base, gamma_slow + 1.0), jnp.power(base, gamma_fast + 1.0)])
    ema_slow_next, ema_fast_next = call(
        average_kernel,
        [((own_rows, triple), F32)] * 2,
        spots, decays, own_grad, swap(other_grad, "c"), ema_slow, ema_fast,
        smem=2,
    )
    return (joint[:, :, :width].reshape(hidden.shape), ema_slow_next, ema_fast_next)


def solution(mesh):
    fine = Mesh(mesh.devices.reshape(2, 8, 2, 2, 8), AXES)
    dp, seq = ("xh", "z", "c"), SEQ
    placed = (
        P(dp, seq, None, None),
        P(dp),
        P(),
        P(dp, None),
        P(dp, None),
        P(dp, None),
        P(),
        P(dp, seq, None, None),
    )
    return jax.shard_map(
        on_device,
        mesh=fine,
        in_specs=placed,
        out_specs=(P(dp, seq, None, None), P(dp, None), P(dp, None)),
        check_vma=False,
    )
```

```python
import math

import jax
import jax.numpy as jnp
from jax import lax
from jax.experimental import pallas as pl
from jax.experimental.pallas import tpu as pltpu
from jax.sharding import Mesh
from jax.sharding import PartitionSpec as P

HEADS = 8
HDIM = 72
norm_eps = 1e-06
loss_scale = 128.0
gamma_slow = 16.97
gamma_fast = 6.94
AXES = ("xh", "zh", "zl", "c", "xl", "y")
SEQ = ("xl", "y")
ROWS = ("xh", "zh", "zl")
F32 = jnp.float32
BF16 = jnp.bfloat16
MIB = 1024 * 1024


def params(mib=48):
    return pltpu.CompilerParams(vmem_limit_bytes=mib * MIB)


def cost(flops, moved):
    return pl.CostEstimate(flops=flops, bytes_accessed=moved, transcendentals=0)


def swap(value, axis):
    return lax.ppermute(value, axis, [(0, 1), (1, 0)])


def modulate_table(timesteps, ada_weight):
    half_freq = ada_weight.shape[0] // 2
    frequency = jnp.exp(-math.log(10000.0) * jnp.arange(half_freq, dtype=F32) / half_freq)
    angles = timesteps.astype(F32)[:, None] * frequency[None, :]
    embedding = jnp.concatenate([jnp.cos(angles), jnp.sin(angles)], axis=1).astype(BF16)
    return jnp.dot(embedding, ada_weight, preferred_element_type=F32)


def pack_kernel(hidden_ref, cot_ref, out_ref):
    width = hidden_ref.shape[1]
    out_ref[:, :width] = hidden_ref[...]
    out_ref[:, width:] = cot_ref[...].T


def stats(values):
    average = jnp.mean(values, axis=-1, keepdims=True)
    moved = values - average
    variance = jnp.mean(moved * moved, axis=-1, keepdims=True)
    inverse_std = lax.rsqrt(variance + norm_eps)
    return moved * inverse_std, inverse_std


def pick(spot, pieces):
    out = pieces[0]
    for index in range(1, 4):
        out = jnp.where(spot == index, pieces[index], out)
    return out


def norm_kernel(spot_ref, packed_ref, mod_ref, core_ref, side_ref):
    width = mod_ref.shape[1] // 2
    quarter = (packed_ref.shape[1] - width) // 4
    centered, _ = stats(packed_ref[:, :width].astype(F32))
    normed = (centered * (1.0 + mod_ref[:, width:]) + mod_ref[:, :width]).astype(BF16)
    cot = packed_ref[:, width:].astype(F32)
    pieces = [cot[:, i * quarter : (i + 1) * quarter] for i in range(4)]
    spot = spot_ref[0]
    own, side, core, both = (pick(spot, [pieces[i ^ flip] for i in range(4)]) for flip in range(4))
    side_ref[:, :width] = normed
    side_ref[:, width : width + 2 * quarter] = jnp.concatenate([side, both], axis=1).astype(BF16)
    core_ref[:, :width] = normed
    core_ref[:, width : width + 2 * quarter] = jnp.concatenate([core, own], axis=1).astype(BF16)


def norm_back_kernel(packed_ref, mod_ref, *refs):
    out_ref = refs[-1]
    width = mod_ref.shape[1] // 2
    centered, inverse_std = stats(packed_ref[:, :width].astype(F32))
    grads = refs[0][...].astype(F32)
    for ref in refs[1:-1]:
        grads = grads + ref[...].astype(F32)
    grads = grads.astype(BF16).astype(F32)
    upstream = grads * (1.0 + mod_ref[:, width:])
    first = jnp.mean(upstream, axis=-1, keepdims=True)
    second = jnp.mean(upstream * centered, axis=-1, keepdims=True)
    out_ref[...] = (inverse_std * (upstream - first - centered * second)).astype(BF16)


def dot(left, right, over):
    return lax.dot_general(left, right, ((over[0], over[1]), ((), ())), preferred_element_type=F32)


def attend_block(projected, out_grad, same, lane):
    factor = 1.0 / math.sqrt(HDIM)
    wide = 2 * HDIM
    query = projected[:, :wide]
    keys = projected[:, wide : 2 * wide]
    values = projected[:, 2 * wide :].astype(BF16)
    query_low, keys_low = query.astype(BF16), keys.astype(BF16)
    query_grad = key_grad = value_grad = None
    for head in range(2):
        mine = (lane >= head * HDIM) & (lane < (head + 1) * HDIM)
        own_query = jnp.where(mine, query, 0.0).astype(BF16)
        own_keys = jnp.where(mine, keys, 0.0).astype(BF16)
        own_out = jnp.where(mine, out_grad, 0.0).astype(BF16)
        scores = dot(own_query, keys_low, ((1,), (1,))) * factor
        scores = jnp.where(same, scores, -1e30)
        top = jnp.max(scores, axis=-1, keepdims=True)
        expo = jnp.exp(scores - top)
        attention = expo / jnp.sum(expo, axis=-1, keepdims=True)
        prob_grad = dot(own_out, values, ((1,), (1,)))
        row_dot = jnp.sum(attention * prob_grad, axis=-1, keepdims=True)
        score_grad = (attention * (prob_grad - row_dot)).astype(BF16)
        parts = (
            dot(score_grad, own_keys, ((1,), (0,))),
            dot(score_grad, own_query, ((0,), (0,))),
            dot(attention.astype(BF16), own_out, ((0,), (0,))),
        )
        if head == 0:
            query_grad, key_grad, value_grad = parts
        else:
            query_grad, key_grad, value_grad = (
                query_grad + parts[0],
                key_grad + parts[1],
                value_grad + parts[2],
            )
    return jnp.concatenate([query_grad * factor, key_grad * factor, value_grad], axis=1)


def tiles_of(block):
    rows = [block[8 * i : 8 * i + 8] for i in range(block.shape[0] // 8)]
    tiles = [row[:, 128 * k : 128 * k + 128] for row in rows for k in range(3)]
    rest = [row[:, 384:] for row in rows] + [jnp.zeros_like(rows[0][:, 384:])]
    pad = jnp.zeros((8, 128 - 2 * rest[0].shape[1]), block.dtype)
    tiles += [jnp.concatenate([rest[i], rest[i + 1], pad], axis=1) for i in range(0, len(rest), 2)]
    return tiles


def block_of(tiles, height):
    count = height // 8
    rows = []
    for i in range(count):
        last = tiles[3 * count + i // 2][:, 48 * (i % 2) : 48 * (i % 2) + 48]
        rows.append(jnp.concatenate(tiles[3 * i : 3 * i + 3] + [last], axis=1))
    return jnp.concatenate(rows, axis=0)


def main_kernel(
    weight_hbm, own_hbm, core_hbm, side_hbm, both_hbm, packed_hbm, near_hbm, far_hbm,
    raw_ref, own_ref, core_ref, side_ref, both_ref, weight_ref, packed_ref, parts_ref, total_ref, in_sems, out_sems,
):
    tokens = own_ref.shape[0]
    model_width, cols = total_ref.shape
    quarter = cols // 3
    pairs = (
        (weight_hbm, raw_ref), (own_hbm, own_ref), (core_hbm, core_ref), (side_hbm, side_ref), (both_hbm, both_ref),
    )
    loads = [pltpu.make_async_copy(source, target, in_sems.at[i]) for i, (source, target) in enumerate(pairs)]
    for load in loads:
        load.start()
    row = lax.broadcasted_iota(jnp.int32, (tokens, tokens), 0)
    col = lax.broadcasted_iota(jnp.int32, (tokens, tokens), 1)
    same = lax.rem(row, 16) == lax.rem(col, 16)
    lane = lax.broadcasted_iota(jnp.int32, (tokens, quarter), 1)
    stores = []
    loads[0].wait()
    blocks = [raw_ref[low, group][:, :cols].astype(F32) for group in range(4) for low in range(4)]
    weight_ref[...] = jnp.concatenate(blocks, axis=0).astype(BF16)
    places = ((near_hbm, 0, 1), (far_hbm, 0, 0), (near_hbm, 1, 0), (far_hbm, 1, 1))
    for index, (target, place, skip) in enumerate(places):
        ref = pairs[index + 1][1]
        loads[index + 1].wait()
        projected = dot(ref[:, :model_width], weight_ref[...], ((1,), (0,)))
        projected = projected.astype(BF16).astype(F32)
        cot = ref[:, model_width:].astype(F32)
        out_grad = cot[:, skip * quarter : (skip + 1) * quarter]
        grads = attend_block(projected, out_grad, same, lane).astype(BF16)
        part = dot(ref[:, :model_width], grads, ((0,), (0,)))
        if index == 0:
            total_ref[...] = part
        else:
            total_ref[...] += part
        parts_ref[index] = dot(grads, weight_ref[...], ((1,), (1,))).astype(BF16)
        stores.append(
            pltpu.make_async_copy(
                parts_ref.at[index], target.at[pl.ds(place * tokens, tokens)], out_sems.at[index]
            )
        )
        stores[-1].start()
    height = model_width // 16
    pieces = packed_ref.shape[0] // 16
    for owner in range(16):
        tiles = tiles_of(total_ref[owner * height : (owner + 1) * height, :])
        each = len(tiles) // pieces
        for piece in range(pieces):
            packed_ref[owner * pieces + piece] = jnp.concatenate(tiles[each * piece : each * piece + each], axis=0).astype(BF16)
        if owner % 4 == 3:
            part = pl.ds((owner - 3) * pieces, 4 * pieces)
            stores.append(pltpu.make_async_copy(packed_ref.at[part], packed_hbm.at[part], out_sems.at[4 + owner // 4]))
            stores[-1].start()
    for store in stores:
        store.wait()


def add_kernel(near_ref, got_ref, own_ref, side_ref):
    half = own_ref.shape[0]
    side_ref[...] = (near_ref[half:].astype(F32) + got_ref[half:].astype(F32)).astype(BF16)
    own_ref[...] = (near_ref[:half].astype(F32) + got_ref[:half].astype(F32)).astype(BF16)


def columns_kernel(spot_ref, master_ref, mine_ref, theirs_ref):
    quarter = master_ref.shape[1] // 12
    spot = spot_ref[0]
    for flip, ref in ((0, mine_ref), (2, theirs_ref)):
        parts = []
        for part in range(3):
            pieces = [master_ref[:, (4 * part + i) * quarter : (4 * part + i + 1) * quarter] for i in range(4)]
            parts.append(pick(spot, [pieces[i ^ flip] for i in range(4)]))
        ref[...] = jnp.concatenate(parts, axis=1).astype(BF16)


def pair_kernel(spot_ref, mine_ref, theirs_ref, out_ref):
    mine, theirs = mine_ref[...].astype(F32), theirs_ref[...].astype(F32)
    first = spot_ref[0] < 2
    upper, lower = jnp.where(first, mine, theirs), jnp.where(first, theirs, mine)
    pair = jnp.concatenate([upper, lower], axis=0)
    rest = jnp.zeros((pair.shape[0], out_ref.shape[1] - pair.shape[1]), F32)
    out_ref[...] = jnp.concatenate([pair, rest], axis=1).astype(BF16)


def double_kernel(spot_ref, own_ref, got_ref, out_ref):
    out_ref[spot_ref[1]] = own_ref[...]
    out_ref[1 - spot_ref[1]] = got_ref[...]


def quad_kernel(spot_ref, own_ref, got_ref, out_ref):
    for across in range(2):
        out_ref[2 * across + spot_ref[2]] = own_ref[across]
        out_ref[2 * across + 1 - spot_ref[2]] = got_ref[across]


def payload_kernel(parts_ref, back_ref, out_ref):
    total = parts_ref[0].astype(F32)
    for index in range(1, parts_ref.shape[0]):
        total = total + parts_ref[index].astype(F32)
    half = total.shape[0] // 2
    piece = jnp.concatenate([total[:half], total[half:]], axis=1).astype(BF16)
    width = back_ref.shape[1]
    out_ref[:, :width] = back_ref[...]
    for index in range(out_ref.shape[0] // half):
        out_ref[index * half : (index + 1) * half, width:] = piece


def rows_kernel(spot_ref, pieces_ref, own_ref, other_ref):
    width = pieces_ref.shape[2] - 256
    count = pieces_ref.shape[0] // 2
    height = own_ref.shape[1]
    first = spot_ref[0] < 2
    for side in range(2):
        tiles = []
        for index in range(count):
            piece = pieces_ref[side * count + index][:, width:].astype(F32)
            tiles += [piece[:8, :128], piece[8:, :128], piece[:8, 128:], piece[8:, 128:]]
        total = block_of(tiles, 2 * height)
        upper, lower = total[:height], total[height:]
        own_ref[side] = jnp.where(first, upper, lower)
        other_ref[side] = jnp.where(first, lower, upper)


def average_kernel(spot_ref, decay_ref, own_ref, core_ref, slow_ref, fast_ref, slow_out, fast_out):
    quarter = own_ref.shape[2] // 3
    first = spot_ref[0] < 2
    own, other = [own_ref[0], own_ref[1]], [core_ref[0], core_ref[1]]
    places = [jnp.where(first, a, b) for a, b in zip(own + other, other + own)]
    columns = [place[:, part * quarter : (part + 1) * quarter] for part in range(3) for place in places]
    grad = jnp.concatenate(columns, axis=1) / loss_scale
    slow_out[...] = decay_ref[0] * slow_ref[...] + (1.0 - decay_ref[0]) * grad
    fast_out[...] = decay_ref[1] * fast_ref[...] + (1.0 - decay_ref[1]) * grad


def call(kernel, outs, *args, flops=0, scratch=(), mib=16, smem=0, hbm_in=False, hbm_out=()):
    moved = sum(a.size * a.dtype.itemsize for a in args)
    moved += sum(math.prod(shape) * jnp.dtype(kind).itemsize for shape, kind in outs)
    shapes = [jax.ShapeDtypeStruct(shape, kind) for shape, kind in outs]
    body = pltpu.HBM if hbm_in else pltpu.VMEM
    specs = [pl.BlockSpec(memory_space=pltpu.SMEM if i < smem else body) for i in range(len(args))]
    got = pl.pallas_call(
        kernel,
        out_shape=shapes,
        in_specs=specs,
        out_specs=[pl.BlockSpec(memory_space=pltpu.HBM if i in hbm_out else pltpu.VMEM) for i in range(len(shapes))],
        scratch_shapes=list(scratch),
        compiler_params=params(mib),
        cost_estimate=cost(flops, moved),
    )(*args)
    return got[0] if len(got) == 1 else got


def lanes(count):
    return -(-count // 128) * 128


def on_device(hidden, timesteps, ada_weight, master, ema_slow, ema_fast, step_count, cotangent):
    patches, width = hidden.shape[2:]
    inner = cotangent.shape[3]
    own_rows, triple = master.shape
    wide = width + inner
    n_seq = lax.axis_size("xl") * lax.axis_size("y")
    n_rows = lax.axis_size("xh") * lax.axis_size("zh") * lax.axis_size("zl")
    n_y = lax.axis_size("y")
    quarter = inner // 4
    cols = 3 * quarter
    pair_rows = 2 * own_rows
    core, side = lax.axis_index("c"), lax.axis_index("xl")
    spots = jnp.stack([2 * core + side, lax.axis_index("xh"), lax.axis_index("zh")]).astype(jnp.int32)

    packed = call(pack_kernel, [((patches, wide), BF16)], hidden[0, 0], cotangent[0, 0].T)
    tokens = lax.all_to_all(packed.reshape(n_seq, patches // n_seq, wide), SEQ, 0, 0, tiled=True)
    tokens = tokens.reshape(patches, wide)

    mine, theirs = call(columns_kernel, [((own_rows, cols), BF16)] * 2, spots, master, smem=1)
    padded = lanes(cols)
    pair = call(pair_kernel, [((pair_rows, padded), BF16)], spots, mine, swap(theirs, "c"), smem=1)
    double = call(double_kernel, [((2, pair_rows, padded), BF16)], spots, pair, swap(pair, "xh"), smem=1)
    quad = call(quad_kernel, [((4, pair_rows, padded), BF16)], spots, double, swap(double, "zh"), smem=1)
    weights = lax.all_gather(quad.reshape(4 * pair_rows, padded), "zl", axis=0, tiled=True)
    weights = weights.reshape(4, 4, pair_rows, padded)

    modulation = modulate_table(timesteps, ada_weight)
    broad = lanes(width + 2 * quarter)
    to_core, to_side = call(norm_kernel, [((patches, broad), BF16)] * 2, spots, tokens, modulation, smem=1)
    from_side = swap(to_side, "xl")
    from_core = swap(to_core, "c")
    from_side, from_core = lax.optimization_barrier((from_side, from_core))
    from_both = swap(from_side, "c")

    pieces = n_rows * n_y
    packed, near, far = call(
        main_kernel,
        [((pieces, 32, 128), BF16), ((2 * patches, width), BF16), ((2 * patches, width), BF16)],
        weights, to_core, from_core, from_side, from_both,
        flops=6 * 4 * patches * width * cols,
        scratch=[
            pltpu.VMEM((4, 4, pair_rows, padded), BF16),
            pltpu.VMEM((patches, broad), BF16),
            pltpu.VMEM((patches, broad), BF16),
            pltpu.VMEM((patches, broad), BF16),
            pltpu.VMEM((patches, broad), BF16),
            pltpu.VMEM((width, cols), BF16),
            pltpu.VMEM((pieces, 32, 128), BF16),
            pltpu.VMEM((4, patches, width), BF16),
            pltpu.VMEM((width, cols), F32),
            pltpu.SemaphoreType.DMA((5,)),
            pltpu.SemaphoreType.DMA((8,)),
        ],
        mib=58,
        hbm_in=True,
        hbm_out=(0, 1, 2),
    )

    part, give = call(add_kernel, [((patches, width), BF16)] * 2, near, swap(far, "c"))
    back = call(norm_back_kernel, [((patches, width), BF16)], tokens, modulation, part, swap(give, "xl"))

    parts = lax.all_to_all(packed, ROWS + ("y",), 0, 0, tiled=True)
    joint = call(payload_kernel, [((patches, width + 256), BF16)], parts, back)
    joint = lax.all_to_all(joint.reshape(n_seq, patches // n_seq, width + 256), SEQ, 0, 0, tiled=True)
    own_grad, other_grad = call(rows_kernel, [((2, own_rows, cols), F32)] * 2, spots, joint, smem=1)
    base = 1.0 - 1.0 / step_count[0].astype(F32)
    decays = jnp.stack([jnp.power(base, gamma_slow + 1.0), jnp.power(base, gamma_fast + 1.0)])
    ema_slow_next, ema_fast_next = call(
        average_kernel,
        [((own_rows, triple), F32)] * 2,
        spots, decays, own_grad, swap(other_grad, "c"), ema_slow, ema_fast,
        smem=2,
    )
    return (joint[:, :, :width].reshape(hidden.shape), ema_slow_next, ema_fast_next)


def solution(mesh):
    fine = Mesh(mesh.devices.reshape(2, 2, 4, 2, 2, 8), AXES)
    dp, seq = ROWS + ("c",), SEQ
    placed = (
        P(dp, seq, None, None),
        P(dp),
        P(),
        P(dp, None),
        P(dp, None),
        P(dp, None),
        P(),
        P(dp, seq, None, None),
    )
    return jax.shard_map(
        on_device,
        mesh=fine,
        in_specs=placed,
        out_specs=(P(dp, seq, None, None), P(dp, None), P(dp, None)),
        check_vma=False,
    )
```

```python
import math

import jax
import jax.numpy as jnp
from jax import lax
from jax.experimental import pallas as pl
from jax.experimental.pallas import tpu as pltpu
from jax.sharding import Mesh
from jax.sharding import PartitionSpec as P

HEADS = 8
HDIM = 72
norm_eps = 1e-06
loss_scale = 128.0
gamma_slow = 16.97
gamma_fast = 6.94
AXES = ("xh", "z", "c", "xl", "y")
SEQ = ("xl", "y")
ROWS = ("xh", "z")
F32 = jnp.float32
BF16 = jnp.bfloat16
MIB = 1024 * 1024


def params(mib=48):
    return pltpu.CompilerParams(vmem_limit_bytes=mib * MIB)


def cost(flops, moved):
    return pl.CostEstimate(flops=flops, bytes_accessed=moved, transcendentals=0)


def swap(value, axis):
    return lax.ppermute(value, axis, [(0, 1), (1, 0)])


def shift(value, away):
    count = lax.axis_size("z")
    return lax.ppermute(value, "z", [(i, (i + away) % count) for i in range(count)])


def half_turn(value):
    return shift(value, lax.axis_size("z") // 2)


def both_turn(value):
    count = lax.axis_size("z")
    pairs = [(i, (count - count * (i // count)) + (i % count + count // 2) % count) for i in range(2 * count)]
    return lax.ppermute(value, ("xh", "z"), pairs)


def modulate_table(timesteps, ada_weight):
    half_freq = ada_weight.shape[0] // 2
    frequency = jnp.exp(-math.log(10000.0) * jnp.arange(half_freq, dtype=F32) / half_freq)
    angles = timesteps.astype(F32)[:, None] * frequency[None, :]
    embedding = jnp.concatenate([jnp.cos(angles), jnp.sin(angles)], axis=1).astype(BF16)
    return jnp.dot(embedding, ada_weight, preferred_element_type=F32)


def pack_kernel(hidden_hbm, cot_hbm, out_hbm, cot_ref, turned_ref, sems):
    width = hidden_hbm.shape[1]
    whole = pltpu.make_async_copy(hidden_hbm, out_hbm.at[:, pl.ds(0, width)], sems.at[0])
    whole.start()
    load = pltpu.make_async_copy(cot_hbm, cot_ref, sems.at[1])
    load.start()
    load.wait()
    inner = cot_ref.shape[0]
    turned_ref[:, :inner] = cot_ref[...].T
    store = pltpu.make_async_copy(turned_ref, out_hbm.at[:, pl.ds(width, turned_ref.shape[1])], sems.at[2])
    store.start()
    store.wait()
    whole.wait()


def stats(values):
    average = jnp.mean(values, axis=-1, keepdims=True)
    moved = values - average
    variance = jnp.mean(moved * moved, axis=-1, keepdims=True)
    inverse_std = lax.rsqrt(variance + norm_eps)
    return moved * inverse_std, inverse_std


def pick(spot, pieces):
    out = pieces[0]
    for index in range(1, 4):
        out = jnp.where(spot == index, pieces[index], out)
    return out


def norm_kernel(spot_ref, packed_ref, mod_ref, core_ref, side_ref):
    width = mod_ref.shape[1] // 2
    quarter = width // 8
    centered, _ = stats(packed_ref[:, :width].astype(F32))
    normed = (centered * (1.0 + mod_ref[:, width:]) + mod_ref[:, :width]).astype(BF16)
    cot = packed_ref[:, width : width + 4 * quarter].astype(F32)
    pieces = [cot[:, i * quarter : (i + 1) * quarter] for i in range(4)]
    spot = spot_ref[0]
    own, side, core, both = (pick(spot, [pieces[i ^ flip] for i in range(4)]) for flip in range(4))
    side_ref[:, :width] = normed
    side_ref[:, width : width + 2 * quarter] = jnp.concatenate([side, both], axis=1).astype(BF16)
    core_ref[:, :width] = normed
    core_ref[:, width : width + 2 * quarter] = jnp.concatenate([core, own], axis=1).astype(BF16)


def norm_back_kernel(packed_ref, mod_ref, *refs):
    out_ref = refs[-1]
    width = mod_ref.shape[1] // 2
    centered, inverse_std = stats(packed_ref[:, :width].astype(F32))
    grads = refs[0][...].astype(F32)
    for ref in refs[1:-1]:
        grads = grads + ref[...].astype(F32)
    grads = grads.astype(BF16).astype(F32)
    upstream = grads * (1.0 + mod_ref[:, width:])
    first = jnp.mean(upstream, axis=-1, keepdims=True)
    second = jnp.mean(upstream * centered, axis=-1, keepdims=True)
    out_ref[...] = (inverse_std * (upstream - first - centered * second)).astype(BF16)


def dot(left, right, over):
    return lax.dot_general(left, right, ((over[0], over[1]), ((), ())), preferred_element_type=F32)


def attend_block(projected, out_grad, same, lane):
    factor = 1.0 / math.sqrt(HDIM)
    wide = 2 * HDIM
    query = projected[:, :wide]
    keys = projected[:, wide : 2 * wide]
    values = projected[:, 2 * wide :].astype(BF16)
    query_low, keys_low = query.astype(BF16), keys.astype(BF16)
    query_grad = key_grad = value_grad = None
    for head in range(2):
        mine = (lane >= head * HDIM) & (lane < (head + 1) * HDIM)
        own_query = jnp.where(mine, query, 0.0).astype(BF16)
        own_keys = jnp.where(mine, keys, 0.0).astype(BF16)
        own_out = jnp.where(mine, out_grad, 0.0).astype(BF16)
        scores = dot(own_query, keys_low, ((1,), (1,))) * factor
        scores = jnp.where(same, scores, -1e30)
        top = jnp.max(scores, axis=-1, keepdims=True)
        expo = jnp.exp(scores - top)
        attention = expo / jnp.sum(expo, axis=-1, keepdims=True)
        prob_grad = dot(own_out, values, ((1,), (1,)))
        row_dot = jnp.sum(attention * prob_grad, axis=-1, keepdims=True)
        score_grad = (attention * (prob_grad - row_dot)).astype(BF16)
        parts = (
            dot(score_grad, own_keys, ((1,), (0,))),
            dot(score_grad, own_query, ((0,), (0,))),
            dot(attention.astype(BF16), own_out, ((0,), (0,))),
        )
        if head == 0:
            query_grad, key_grad, value_grad = parts
        else:
            query_grad, key_grad, value_grad = (
                query_grad + parts[0],
                key_grad + parts[1],
                value_grad + parts[2],
            )
    return jnp.concatenate([query_grad * factor, key_grad * factor, value_grad], axis=1)


def tiles_of(block):
    rows = [block[8 * i : 8 * i + 8] for i in range(block.shape[0] // 8)]
    tiles = [row[:, 128 * k : 128 * k + 128] for row in rows for k in range(3)]
    rest = [row[:, 384:] for row in rows] + [jnp.zeros_like(rows[0][:, 384:])]
    pad = jnp.zeros((8, 128 - 2 * rest[0].shape[1]), block.dtype)
    tiles += [jnp.concatenate([rest[i], rest[i + 1], pad], axis=1) for i in range(0, len(rest), 2)]
    return tiles


def block_of(tiles, height):
    count = height // 8
    rows = []
    for i in range(count):
        last = tiles[3 * count + i // 2][:, 48 * (i % 2) : 48 * (i % 2) + 48]
        rows.append(jnp.concatenate(tiles[3 * i : 3 * i + 3] + [last], axis=1))
    return jnp.concatenate(rows, axis=0)


def main_kernel(
    spot_ref, near_hbm, up_hbm, low_hbm, high_hbm, down_hbm, own_hbm, core_hbm, side_hbm, both_hbm, packed_hbm, inner_hbm, outer_hbm,
    raw_ref, own_ref, core_ref, side_ref, both_ref, weight_ref, packed_ref, parts_ref, total_ref, in_sems, out_sems,
):
    tokens = own_ref.shape[0]
    model_width, cols = total_ref.shape
    quarter = cols // 3
    lows = [lax.rem(spot_ref[1] + ahead, 4) for ahead in range(4)]
    half = raw_ref.shape[1] // 2
    tokens_in = ((own_hbm, own_ref), (core_hbm, core_ref), (side_hbm, side_ref), (both_hbm, both_ref))
    pairs = (
        (near_hbm, raw_ref.at[lows[0]]),
        (up_hbm, raw_ref.at[lows[1]]),
        (low_hbm, raw_ref.at[lows[2], pl.ds(0, half)]),
        (high_hbm, raw_ref.at[lows[2], pl.ds(half, half)]),
        (down_hbm, raw_ref.at[lows[3]]),
    ) + tokens_in
    loads = [pltpu.make_async_copy(source, target, in_sems.at[i]) for i, (source, target) in enumerate(pairs)]
    for load in loads:
        load.start()
    row = lax.broadcasted_iota(jnp.int32, (tokens, tokens), 0)
    col = lax.broadcasted_iota(jnp.int32, (tokens, tokens), 1)
    same = lax.rem(row, 16) == lax.rem(col, 16)
    lane = lax.broadcasted_iota(jnp.int32, (tokens, quarter), 1)
    stores = []
    for load in loads[:5]:
        load.wait()
    blocks = [raw_ref[low, group].astype(F32) for group in range(4) for low in range(4)]
    weight_ref[...] = jnp.concatenate(blocks, axis=0).astype(BF16)
    places = ((inner_hbm, 0, 1), (outer_hbm, 0, 0), (inner_hbm, 1, 0), (outer_hbm, 1, 1))
    for index, (target, place, skip) in enumerate(places):
        ref = tokens_in[index][1]
        loads[index + 5].wait()
        projected = dot(ref[:, :model_width], weight_ref[...], ((1,), (0,)))
        projected = projected.astype(BF16).astype(F32)
        cot = ref[:, model_width:].astype(F32)
        out_grad = cot[:, skip * quarter : (skip + 1) * quarter]
        grads = attend_block(projected, out_grad, same, lane).astype(BF16)
        part = dot(ref[:, :model_width], grads, ((0,), (0,)))
        if index == 0:
            total_ref[...] = part
        else:
            total_ref[...] += part
        parts_ref[index] = dot(grads, weight_ref[...], ((1,), (1,))).astype(BF16)
        stores.append(
            pltpu.make_async_copy(
                parts_ref.at[index], target.at[pl.ds(place * tokens, tokens)], out_sems.at[index]
            )
        )
        stores[-1].start()
    height = model_width // 16
    pieces = packed_ref.shape[0] // 16
    for owner in range(16):
        tiles = tiles_of(total_ref[owner * height : (owner + 1) * height, :])
        each = len(tiles) // pieces
        for piece in range(pieces):
            packed_ref[owner * pieces + piece] = jnp.concatenate(tiles[each * piece : each * piece + each], axis=0).astype(BF16)
        if owner % 4 == 3:
            part = pl.ds((owner - 3) * pieces, 4 * pieces)
            stores.append(pltpu.make_async_copy(packed_ref.at[part], packed_hbm.at[part], out_sems.at[4 + owner // 4]))
            stores[-1].start()
    for store in stores:
        store.wait()


def add_kernel(near_ref, got_ref, own_ref, side_ref):
    half = own_ref.shape[0]
    side_ref[...] = (near_ref[half:].astype(F32) + got_ref[half:].astype(F32)).astype(BF16)
    own_ref[...] = (near_ref[:half].astype(F32) + got_ref[:half].astype(F32)).astype(BF16)


def columns_kernel(spot_ref, master_ref, mine_ref, theirs_ref):
    quarter = master_ref.shape[1] // 12
    spot = spot_ref[0]
    for flip, ref in ((0, mine_ref), (2, theirs_ref)):
        parts = []
        for part in range(3):
            pieces = [master_ref[:, (4 * part + i) * quarter : (4 * part + i + 1) * quarter] for i in range(4)]
            parts.append(pick(spot, [pieces[i ^ flip] for i in range(4)]))
        ref[...] = jnp.concatenate(parts, axis=1).astype(BF16)


def pair_kernel(spot_ref, mine_ref, theirs_ref, out_ref):
    mine, theirs = mine_ref[...].astype(F32), theirs_ref[...].astype(F32)
    first = spot_ref[0] < 2
    upper, lower = jnp.where(first, mine, theirs), jnp.where(first, theirs, mine)
    out_ref[...] = jnp.concatenate([upper, lower], axis=0).astype(BF16)


def quad_kernel(spot_ref, own_ref, far_ref, across_ref, both_ref, out_ref):
    place = spot_ref[2]
    out_ref[place] = own_ref[...]
    out_ref[place + 1 - 2 * lax.rem(place, 2)] = far_ref[...]
    out_ref[lax.rem(place + 2, 4)] = across_ref[...]
    out_ref[3 - place] = both_ref[...]


def payload_kernel(parts_ref, back_ref, out_ref):
    total = parts_ref[0].astype(F32)
    for index in range(1, parts_ref.shape[0]):
        total = total + parts_ref[index].astype(F32)
    half = total.shape[0] // 2
    piece = jnp.concatenate([total[:half], total[half:]], axis=1).astype(BF16)
    width = back_ref.shape[1]
    out_ref[:, :width] = back_ref[...]
    for index in range(out_ref.shape[0] // half):
        out_ref[index * half : (index + 1) * half, width:] = piece


def rows_kernel(spot_ref, pieces_ref, own_ref, other_ref):
    width = pieces_ref.shape[2] - 256
    count = pieces_ref.shape[0] // 2
    height = own_ref.shape[1]
    first = spot_ref[0] < 2
    for side in range(2):
        tiles = []
        for index in range(count):
            piece = pieces_ref[side * count + index][:, width:].astype(F32)
            tiles += [piece[:8, :128], piece[8:, :128], piece[:8, 128:], piece[8:, 128:]]
        total = block_of(tiles, 2 * height)
        upper, lower = total[:height], total[height:]
        own_ref[side] = jnp.where(first, upper, lower)
        other_ref[side] = jnp.where(first, lower, upper)


def average_kernel(spot_ref, decay_ref, own_ref, core_ref, slow_ref, fast_ref, slow_out, fast_out):
    quarter = own_ref.shape[2] // 3
    first = spot_ref[0] < 2
    own, other = [own_ref[0], own_ref[1]], [core_ref[0], core_ref[1]]
    places = [jnp.where(first, a, b) for a, b in zip(own + other, other + own)]
    columns = [place[:, part * quarter : (part + 1) * quarter] for part in range(3) for place in places]
    grad = jnp.concatenate(columns, axis=1) / loss_scale
    slow_out[...] = decay_ref[0] * slow_ref[...] + (1.0 - decay_ref[0]) * grad
    fast_out[...] = decay_ref[1] * fast_ref[...] + (1.0 - decay_ref[1]) * grad


def call(kernel, outs, *args, flops=0, scratch=(), mib=16, smem=0, hbm_in=False, hbm_out=()):
    moved = sum(a.size * a.dtype.itemsize for a in args)
    moved += sum(math.prod(shape) * jnp.dtype(kind).itemsize for shape, kind in outs)
    shapes = [jax.ShapeDtypeStruct(shape, kind) for shape, kind in outs]
    body = pltpu.HBM if hbm_in else pltpu.VMEM
    specs = [pl.BlockSpec(memory_space=pltpu.SMEM if i < smem else body) for i in range(len(args))]
    got = pl.pallas_call(
        kernel,
        out_shape=shapes,
        in_specs=specs,
        out_specs=[pl.BlockSpec(memory_space=pltpu.HBM if i in hbm_out else pltpu.VMEM) for i in range(len(shapes))],
        scratch_shapes=list(scratch),
        compiler_params=params(mib),
        cost_estimate=cost(flops, moved),
    )(*args)
    return got[0] if len(got) == 1 else got


def lanes(count):
    return -(-count // 128) * 128


def on_device(hidden, timesteps, ada_weight, master, ema_slow, ema_fast, step_count, cotangent):
    patches, width = hidden.shape[2:]
    inner = cotangent.shape[3]
    own_rows, triple = master.shape
    n_seq = lax.axis_size("xl") * lax.axis_size("y")
    n_rows = lax.axis_size("xh") * lax.axis_size("z")
    n_y = lax.axis_size("y")
    quarter = inner // 4
    cols = 3 * quarter
    pair_rows = 2 * own_rows
    core, side = lax.axis_index("c"), lax.axis_index("xl")
    across, along = lax.axis_index("xh"), lax.axis_index("z")
    spots = jnp.stack([2 * core + side, lax.rem(along, 4), 2 * across + along // 4]).astype(jnp.int32)

    loose = lanes(inner)
    packed = call(
        pack_kernel,
        [((patches, width + loose), BF16)],
        hidden[0, 0], cotangent[0, 0].T,
        scratch=[pltpu.VMEM((inner, patches), BF16), pltpu.VMEM((patches, loose), BF16), pltpu.SemaphoreType.DMA((3,))],
        mib=58,
        hbm_in=True,
        hbm_out=(0,),
    )
    tokens = lax.all_to_all(packed.reshape(n_seq, patches // n_seq, width + loose), SEQ, 0, 0, tiled=True)
    tokens = tokens.reshape(patches, width + loose)

    mine, theirs = call(columns_kernel, [((own_rows, cols), BF16)] * 2, spots, master, smem=1)
    pair = call(pair_kernel, [((pair_rows, cols), BF16)], spots, mine, swap(theirs, "c"), smem=1)
    quad = call(
        quad_kernel,
        [((4, pair_rows, cols), BF16)],
        spots, pair, half_turn(pair), swap(pair, "xh"), both_turn(pair),
        smem=1,
    )
    quad, tokens = lax.optimization_barrier((quad, tokens))

    modulation = modulate_table(timesteps, ada_weight)
    broad = lanes(width + 2 * quarter)
    to_core, to_side = call(norm_kernel, [((patches, broad), BF16)] * 2, spots, tokens, modulation, smem=1)
    from_side = swap(to_side, "xl")
    up, low, high, down = shift(quad, -1), shift(quad[:2], -2), shift(quad[2:], 2), shift(quad, 1)
    to_core, low = lax.optimization_barrier((to_core, low))
    from_core = swap(to_core, "c")
    from_side, up, low, high, down = lax.optimization_barrier((from_side, up, low, high, down))
    from_both = swap(from_side, "c")

    pieces = n_rows * n_y
    packed, near, far = call(
        main_kernel,
        [((pieces, 32, 128), BF16), ((2 * patches, width), BF16), ((2 * patches, width), BF16)],
        spots, quad, up, low, high, down, to_core, from_core, from_side, from_both,
        flops=6 * 4 * patches * width * cols,
        scratch=[
            pltpu.VMEM((4, 4, pair_rows, cols), BF16),
            pltpu.VMEM((patches, broad), BF16),
            pltpu.VMEM((patches, broad), BF16),
            pltpu.VMEM((patches, broad), BF16),
            pltpu.VMEM((patches, broad), BF16),
            pltpu.VMEM((width, cols), BF16),
            pltpu.VMEM((pieces, 32, 128), BF16),
            pltpu.VMEM((4, patches, width), BF16),
            pltpu.VMEM((width, cols), F32),
            pltpu.SemaphoreType.DMA((9,)),
            pltpu.SemaphoreType.DMA((8,)),
        ],
        mib=58,
        smem=1,
        hbm_in=True,
        hbm_out=(0, 1, 2),
    )

    part, give = call(add_kernel, [((patches, width), BF16)] * 2, near, swap(far, "c"))
    back = call(norm_back_kernel, [((patches, width), BF16)], tokens, modulation, part, swap(give, "xl"))

    parts = lax.all_to_all(packed, ROWS + ("y",), 0, 0, tiled=True)
    joint = call(payload_kernel, [((patches, width + 256), BF16)], parts, back)
    joint = lax.all_to_all(joint.reshape(n_seq, patches // n_seq, width + 256), SEQ, 0, 0, tiled=True)
    own_grad, other_grad = call(rows_kernel, [((2, own_rows, cols), F32)] * 2, spots, joint, smem=1)
    base = 1.0 - 1.0 / step_count[0].astype(F32)
    decays = jnp.stack([jnp.power(base, gamma_slow + 1.0), jnp.power(base, gamma_fast + 1.0)])
    ema_slow_next, ema_fast_next = call(
        average_kernel,
        [((own_rows, triple), F32)] * 2,
        spots, decays, own_grad, swap(other_grad, "c"), ema_slow, ema_fast,
        smem=2,
    )
    return (joint[:, :, :width].reshape(hidden.shape), ema_slow_next, ema_fast_next)


def solution(mesh):
    fine = Mesh(mesh.devices.reshape(2, 8, 2, 2, 8), AXES)
    dp, seq = ROWS + ("c",), SEQ
    placed = (
        P(dp, seq, None, None),
        P(dp),
        P(),
        P(dp, None),
        P(dp, None),
        P(dp, None),
        P(),
        P(dp, seq, None, None),
    )
    return jax.shard_map(
        on_device,
        mesh=fine,
        in_specs=placed,
        out_specs=(P(dp, seq, None, None), P(dp, None), P(dp, None)),
        check_vma=False,
    )
```

```python
import math

import jax
import jax.numpy as jnp
from jax import lax
from jax.experimental import pallas as pl
from jax.experimental.pallas import tpu as pltpu
from jax.sharding import Mesh
from jax.sharding import PartitionSpec as P

HEADS = 8
HDIM = 72
norm_eps = 1e-06
loss_scale = 128.0
gamma_slow = 16.97
gamma_fast = 6.94
AXES = ("xh", "z", "c", "xl", "y")
SEQ = ("xl", "y")
ROWS = ("xh", "z")
F32 = jnp.float32
BF16 = jnp.bfloat16
MIB = 1024 * 1024


def params(mib=48):
    return pltpu.CompilerParams(vmem_limit_bytes=mib * MIB)


def cost(flops, moved):
    return pl.CostEstimate(flops=flops, bytes_accessed=moved, transcendentals=0)


def swap(value, axis):
    return lax.ppermute(value, axis, [(0, 1), (1, 0)])


def shift(value, away):
    count = lax.axis_size("z")
    return lax.ppermute(value, "z", [(i, (i + away) % count) for i in range(count)])


def half_turn(value):
    return shift(value, lax.axis_size("z") // 2)


def both_turn(value):
    count = lax.axis_size("z")
    pairs = [(i, (count - count * (i // count)) + (i % count + count // 2) % count) for i in range(2 * count)]
    return lax.ppermute(value, ("xh", "z"), pairs)


def modulate_table(timesteps, ada_weight):
    half_freq = ada_weight.shape[0] // 2
    frequency = jnp.exp(-math.log(10000.0) * jnp.arange(half_freq, dtype=F32) / half_freq)
    angles = timesteps.astype(F32)[:, None] * frequency[None, :]
    embedding = jnp.concatenate([jnp.cos(angles), jnp.sin(angles)], axis=1).astype(BF16)
    return jnp.dot(embedding, ada_weight, preferred_element_type=F32)


def pack_kernel(hidden_hbm, cot_hbm, out_hbm, hidden_ref, cot_ref, turned_ref, sems):
    width = hidden_hbm.shape[1]
    first = pltpu.make_async_copy(cot_hbm, cot_ref, sems.at[0])
    second = pltpu.make_async_copy(hidden_hbm, hidden_ref, sems.at[1])
    first.start()
    second.start()
    first.wait()
    inner = cot_ref.shape[0]
    turned_ref[:, :inner] = cot_ref[...].T
    right = pltpu.make_async_copy(turned_ref, out_hbm.at[:, pl.ds(width, turned_ref.shape[1])], sems.at[2])
    right.start()
    second.wait()
    left = pltpu.make_async_copy(hidden_ref, out_hbm.at[:, pl.ds(0, width)], sems.at[3])
    left.start()
    right.wait()
    left.wait()


def stats(values):
    average = jnp.mean(values, axis=-1, keepdims=True)
    moved = values - average
    variance = jnp.mean(moved * moved, axis=-1, keepdims=True)
    inverse_std = lax.rsqrt(variance + norm_eps)
    return moved * inverse_std, inverse_std


def pick(spot, pieces):
    out = pieces[0]
    for index in range(1, 4):
        out = jnp.where(spot == index, pieces[index], out)
    return out


def norm_kernel(spot_ref, packed_ref, mod_ref, core_ref, side_ref):
    width = mod_ref.shape[1] // 2
    quarter = width // 8
    centered, _ = stats(packed_ref[:, :width].astype(F32))
    normed = (centered * (1.0 + mod_ref[:, width:]) + mod_ref[:, :width]).astype(BF16)
    cot = packed_ref[:, width : width + 4 * quarter].astype(F32)
    pieces = [cot[:, i * quarter : (i + 1) * quarter] for i in range(4)]
    spot = spot_ref[0]
    own, side, core, both = (pick(spot, [pieces[i ^ flip] for i in range(4)]) for flip in range(4))
    side_ref[:, :width] = normed
    side_ref[:, width : width + 2 * quarter] = jnp.concatenate([side, both], axis=1).astype(BF16)
    core_ref[:, :width] = normed
    core_ref[:, width : width + 2 * quarter] = jnp.concatenate([core, own], axis=1).astype(BF16)


def norm_back_kernel(packed_ref, mod_ref, *refs):
    out_ref = refs[-1]
    width = mod_ref.shape[1] // 2
    centered, inverse_std = stats(packed_ref[:, :width].astype(F32))
    grads = refs[0][...].astype(F32)
    for ref in refs[1:-1]:
        grads = grads + ref[...].astype(F32)
    grads = grads.astype(BF16).astype(F32)
    upstream = grads * (1.0 + mod_ref[:, width:])
    first = jnp.mean(upstream, axis=-1, keepdims=True)
    second = jnp.mean(upstream * centered, axis=-1, keepdims=True)
    out_ref[...] = (inverse_std * (upstream - first - centered * second)).astype(BF16)


def dot(left, right, over):
    return lax.dot_general(left, right, ((over[0], over[1]), ((), ())), preferred_element_type=F32)


def attend_block(projected, out_grad, same, lane):
    factor = 1.0 / math.sqrt(HDIM)
    wide = 2 * HDIM
    query = projected[:, :wide]
    keys = projected[:, wide : 2 * wide]
    values = projected[:, 2 * wide :].astype(BF16)
    query_low, keys_low = query.astype(BF16), keys.astype(BF16)
    query_grad = key_grad = value_grad = None
    for head in range(2):
        mine = (lane >= head * HDIM) & (lane < (head + 1) * HDIM)
        own_query = jnp.where(mine, query, 0.0).astype(BF16)
        own_keys = jnp.where(mine, keys, 0.0).astype(BF16)
        own_out = jnp.where(mine, out_grad, 0.0).astype(BF16)
        scores = dot(own_query, keys_low, ((1,), (1,))) * factor
        scores = jnp.where(same, scores, -1e30)
        top = jnp.max(scores, axis=-1, keepdims=True)
        expo = jnp.exp(scores - top)
        attention = expo / jnp.sum(expo, axis=-1, keepdims=True)
        prob_grad = dot(own_out, values, ((1,), (1,)))
        row_dot = jnp.sum(attention * prob_grad, axis=-1, keepdims=True)
        score_grad = (attention * (prob_grad - row_dot)).astype(BF16)
        parts = (
            dot(score_grad, own_keys, ((1,), (0,))),
            dot(score_grad, own_query, ((0,), (0,))),
            dot(attention.astype(BF16), own_out, ((0,), (0,))),
        )
        if head == 0:
            query_grad, key_grad, value_grad = parts
        else:
            query_grad, key_grad, value_grad = (
                query_grad + parts[0],
                key_grad + parts[1],
                value_grad + parts[2],
            )
    return jnp.concatenate([query_grad * factor, key_grad * factor, value_grad], axis=1)


def tiles_of(block):
    rows = [block[8 * i : 8 * i + 8] for i in range(block.shape[0] // 8)]
    tiles = [row[:, 128 * k : 128 * k + 128] for row in rows for k in range(3)]
    rest = [row[:, 384:] for row in rows] + [jnp.zeros_like(rows[0][:, 384:])]
    pad = jnp.zeros((8, 128 - 2 * rest[0].shape[1]), block.dtype)
    tiles += [jnp.concatenate([rest[i], rest[i + 1], pad], axis=1) for i in range(0, len(rest), 2)]
    return tiles


def block_of(tiles, height):
    count = height // 8
    rows = []
    for i in range(count):
        last = tiles[3 * count + i // 2][:, 48 * (i % 2) : 48 * (i % 2) + 48]
        rows.append(jnp.concatenate(tiles[3 * i : 3 * i + 3] + [last], axis=1))
    return jnp.concatenate(rows, axis=0)


def main_kernel(
    spot_ref, near_hbm, up_hbm, low_hbm, high_hbm, down_hbm, own_hbm, core_hbm, side_hbm, both_hbm, packed_hbm, inner_hbm, outer_hbm,
    raw_ref, own_ref, core_ref, side_ref, both_ref, weight_ref, packed_ref, parts_ref, total_ref, in_sems, out_sems,
):
    tokens = own_ref.shape[0]
    model_width, cols = total_ref.shape
    quarter = cols // 3
    lows = [lax.rem(spot_ref[1] + ahead, 4) for ahead in range(4)]
    half = raw_ref.shape[1] // 2
    tokens_in = ((own_hbm, own_ref), (core_hbm, core_ref), (side_hbm, side_ref), (both_hbm, both_ref))
    pairs = (
        (near_hbm, raw_ref.at[lows[0]]),
        (up_hbm, raw_ref.at[lows[1]]),
        (low_hbm, raw_ref.at[lows[2], pl.ds(0, half)]),
        (high_hbm, raw_ref.at[lows[2], pl.ds(half, half)]),
        (down_hbm, raw_ref.at[lows[3]]),
    ) + tokens_in
    loads = [pltpu.make_async_copy(source, target, in_sems.at[i]) for i, (source, target) in enumerate(pairs)]
    for load in loads:
        load.start()
    row = lax.broadcasted_iota(jnp.int32, (tokens, tokens), 0)
    col = lax.broadcasted_iota(jnp.int32, (tokens, tokens), 1)
    same = lax.rem(row, 16) == lax.rem(col, 16)
    lane = lax.broadcasted_iota(jnp.int32, (tokens, quarter), 1)
    stores = []
    for load in loads[:5]:
        load.wait()
    blocks = [raw_ref[low, group].astype(F32) for group in range(4) for low in range(4)]
    weight_ref[...] = jnp.concatenate(blocks, axis=0).astype(BF16)
    places = ((inner_hbm, 0, 1), (outer_hbm, 0, 0), (inner_hbm, 1, 0), (outer_hbm, 1, 1))
    for index, (target, place, skip) in enumerate(places):
        ref = tokens_in[index][1]
        loads[index + 5].wait()
        projected = dot(ref[:, :model_width], weight_ref[...], ((1,), (0,)))
        projected = projected.astype(BF16).astype(F32)
        cot = ref[:, model_width:].astype(F32)
        out_grad = cot[:, skip * quarter : (skip + 1) * quarter]
        grads = attend_block(projected, out_grad, same, lane).astype(BF16)
        part = dot(ref[:, :model_width], grads, ((0,), (0,)))
        if index == 0:
            total_ref[...] = part
        else:
            total_ref[...] += part
        parts_ref[index] = dot(grads, weight_ref[...], ((1,), (1,))).astype(BF16)
        stores.append(
            pltpu.make_async_copy(
                parts_ref.at[index], target.at[pl.ds(place * tokens, tokens)], out_sems.at[index]
            )
        )
        stores[-1].start()
    height = model_width // 16
    pieces = packed_ref.shape[0] // 16
    for owner in range(16):
        tiles = tiles_of(total_ref[owner * height : (owner + 1) * height, :])
        each = len(tiles) // pieces
        for piece in range(pieces):
            packed_ref[owner * pieces + piece] = jnp.concatenate(tiles[each * piece : each * piece + each], axis=0).astype(BF16)
        if owner % 4 == 3:
            part = pl.ds((owner - 3) * pieces, 4 * pieces)
            stores.append(pltpu.make_async_copy(packed_ref.at[part], packed_hbm.at[part], out_sems.at[4 + owner // 4]))
            stores[-1].start()
    for store in stores:
        store.wait()


def add_kernel(near_ref, got_ref, own_ref, side_ref):
    half = own_ref.shape[0]
    side_ref[...] = (near_ref[half:].astype(F32) + got_ref[half:].astype(F32)).astype(BF16)
    own_ref[...] = (near_ref[:half].astype(F32) + got_ref[:half].astype(F32)).astype(BF16)


def columns_kernel(spot_ref, master_ref, mine_ref, theirs_ref):
    quarter = master_ref.shape[1] // 12
    spot = spot_ref[0]
    for flip, ref in ((0, mine_ref), (2, theirs_ref)):
        parts = []
        for part in range(3):
            pieces = [master_ref[:, (4 * part + i) * quarter : (4 * part + i + 1) * quarter] for i in range(4)]
            parts.append(pick(spot, [pieces[i ^ flip] for i in range(4)]))
        ref[...] = jnp.concatenate(parts, axis=1).astype(BF16)


def pair_kernel(spot_ref, mine_ref, theirs_ref, out_ref):
    mine, theirs = mine_ref[...].astype(F32), theirs_ref[...].astype(F32)
    first = spot_ref[0] < 2
    upper, lower = jnp.where(first, mine, theirs), jnp.where(first, theirs, mine)
    out_ref[...] = jnp.concatenate([upper, lower], axis=0).astype(BF16)


def quad_kernel(spot_ref, own_ref, far_ref, across_ref, both_ref, out_ref):
    place = spot_ref[2]
    out_ref[place] = own_ref[...]
    out_ref[place + 1 - 2 * lax.rem(place, 2)] = far_ref[...]
    out_ref[lax.rem(place + 2, 4)] = across_ref[...]
    out_ref[3 - place] = both_ref[...]


def payload_kernel(parts_ref, back_ref, out_ref):
    total = parts_ref[0].astype(F32)
    for index in range(1, parts_ref.shape[0]):
        total = total + parts_ref[index].astype(F32)
    half = total.shape[0] // 2
    piece = jnp.concatenate([total[:half], total[half:]], axis=1).astype(BF16)
    width = back_ref.shape[1]
    out_ref[:, :width] = back_ref[...]
    for index in range(out_ref.shape[0] // half):
        out_ref[index * half : (index + 1) * half, width:] = piece


def rows_kernel(spot_ref, pieces_ref, own_ref, other_ref):
    width = pieces_ref.shape[2] - 256
    count = pieces_ref.shape[0] // 2
    height = own_ref.shape[1]
    first = spot_ref[0] < 2
    for side in range(2):
        tiles = []
        for index in range(count):
            piece = pieces_ref[side * count + index][:, width:].astype(F32)
            tiles += [piece[:8, :128], piece[8:, :128], piece[:8, 128:], piece[8:, 128:]]
        total = block_of(tiles, 2 * height)
        upper, lower = total[:height], total[height:]
        own_ref[side] = jnp.where(first, upper, lower)
        other_ref[side] = jnp.where(first, lower, upper)


def average_kernel(spot_ref, decay_ref, own_ref, core_ref, slow_ref, fast_ref, slow_out, fast_out):
    quarter = own_ref.shape[2] // 3
    first = spot_ref[0] < 2
    own, other = [own_ref[0], own_ref[1]], [core_ref[0], core_ref[1]]
    places = [jnp.where(first, a, b) for a, b in zip(own + other, other + own)]
    columns = [place[:, part * quarter : (part + 1) * quarter] for part in range(3) for place in places]
    grad = jnp.concatenate(columns, axis=1) / loss_scale
    slow_out[...] = decay_ref[0] * slow_ref[...] + (1.0 - decay_ref[0]) * grad
    fast_out[...] = decay_ref[1] * fast_ref[...] + (1.0 - decay_ref[1]) * grad


def call(kernel, outs, *args, flops=0, scratch=(), mib=16, smem=0, hbm_in=False, hbm_out=()):
    moved = sum(a.size * a.dtype.itemsize for a in args)
    moved += sum(math.prod(shape) * jnp.dtype(kind).itemsize for shape, kind in outs)
    shapes = [jax.ShapeDtypeStruct(shape, kind) for shape, kind in outs]
    body = pltpu.HBM if hbm_in else pltpu.VMEM
    specs = [pl.BlockSpec(memory_space=pltpu.SMEM if i < smem else body) for i in range(len(args))]
    got = pl.pallas_call(
        kernel,
        out_shape=shapes,
        in_specs=specs,
        out_specs=[pl.BlockSpec(memory_space=pltpu.HBM if i in hbm_out else pltpu.VMEM) for i in range(len(shapes))],
        scratch_shapes=list(scratch),
        compiler_params=params(mib),
        cost_estimate=cost(flops, moved),
    )(*args)
    return got[0] if len(got) == 1 else got


def lanes(count):
    return -(-count // 128) * 128


def on_device(hidden, timesteps, ada_weight, master, ema_slow, ema_fast, step_count, cotangent):
    patches, width = hidden.shape[2:]
    inner = cotangent.shape[3]
    own_rows, triple = master.shape
    n_seq = lax.axis_size("xl") * lax.axis_size("y")
    n_rows = lax.axis_size("xh") * lax.axis_size("z")
    n_y = lax.axis_size("y")
    quarter = inner // 4
    cols = 3 * quarter
    pair_rows = 2 * own_rows
    core, side = lax.axis_index("c"), lax.axis_index("xl")
    across, along = lax.axis_index("xh"), lax.axis_index("z")
    spots = jnp.stack([2 * core + side, lax.rem(along, 4), 2 * across + along // 4]).astype(jnp.int32)

    loose = lanes(inner)
    packed = call(
        pack_kernel,
        [((patches, width + loose), BF16)],
        hidden[0, 0], cotangent[0, 0].T,
        scratch=[
            pltpu.VMEM((patches, width), BF16),
            pltpu.VMEM((inner, patches), BF16),
            pltpu.VMEM((patches, loose), BF16),
            pltpu.SemaphoreType.DMA((4,)),
        ],
        mib=58,
        hbm_in=True,
        hbm_out=(0,),
    )
    tokens = lax.all_to_all(packed.reshape(n_seq, patches // n_seq, width + loose), SEQ, 0, 0, tiled=True)
    tokens = tokens.reshape(patches, width + loose)

    mine, theirs = call(columns_kernel, [((own_rows, cols), BF16)] * 2, spots, master, smem=1)
    pair = call(pair_kernel, [((pair_rows, cols), BF16)], spots, mine, swap(theirs, "c"), smem=1)
    quad = call(
        quad_kernel,
        [((4, pair_rows, cols), BF16)],
        spots, pair, half_turn(pair), swap(pair, "xh"), both_turn(pair),
        smem=1,
    )
    quad, tokens = lax.optimization_barrier((quad, tokens))

    modulation = modulate_table(timesteps, ada_weight)
    broad = lanes(width + 2 * quarter)
    to_core, to_side = call(norm_kernel, [((patches, broad), BF16)] * 2, spots, tokens, modulation, smem=1)
    from_side = swap(to_side, "xl")
    from_core = swap(to_core, "c")
    up, down, low = shift(quad, -1), shift(quad, 1), shift(quad[:2], -2)
    upper, from_core = lax.optimization_barrier((quad[2:], from_core))
    high = shift(upper, 2)
    from_side, up, low, high, down = lax.optimization_barrier((from_side, up, low, high, down))
    from_both = swap(from_side, "c")

    pieces = n_rows * n_y
    packed, near, far = call(
        main_kernel,
        [((pieces, 32, 128), BF16), ((2 * patches, width), BF16), ((2 * patches, width), BF16)],
        spots, quad, up, low, high, down, to_core, from_core, from_side, from_both,
        flops=6 * 4 * patches * width * cols,
        scratch=[
            pltpu.VMEM((4, 4, pair_rows, cols), BF16),
            pltpu.VMEM((patches, broad), BF16),
            pltpu.VMEM((patches, broad), BF16),
            pltpu.VMEM((patches, broad), BF16),
            pltpu.VMEM((patches, broad), BF16),
            pltpu.VMEM((width, cols), BF16),
            pltpu.VMEM((pieces, 32, 128), BF16),
            pltpu.VMEM((4, patches, width), BF16),
            pltpu.VMEM((width, cols), F32),
            pltpu.SemaphoreType.DMA((9,)),
            pltpu.SemaphoreType.DMA((8,)),
        ],
        mib=58,
        smem=1,
        hbm_in=True,
        hbm_out=(0, 1, 2),
    )

    part, give = call(add_kernel, [((patches, width), BF16)] * 2, near, swap(far, "c"))
    back = call(norm_back_kernel, [((patches, width), BF16)], tokens, modulation, part, swap(give, "xl"))

    parts = lax.all_to_all(packed, ROWS + ("y",), 0, 0, tiled=True)
    joint = call(payload_kernel, [((patches, width + 256), BF16)], parts, back)
    joint = lax.all_to_all(joint.reshape(n_seq, patches // n_seq, width + 256), SEQ, 0, 0, tiled=True)
    own_grad, other_grad = call(rows_kernel, [((2, own_rows, cols), F32)] * 2, spots, joint, smem=1)
    base = 1.0 - 1.0 / step_count[0].astype(F32)
    decays = jnp.stack([jnp.power(base, gamma_slow + 1.0), jnp.power(base, gamma_fast + 1.0)])
    ema_slow_next, ema_fast_next = call(
        average_kernel,
        [((own_rows, triple), F32)] * 2,
        spots, decays, own_grad, swap(other_grad, "c"), ema_slow, ema_fast,
        smem=2,
    )
    return (joint[:, :, :width].reshape(hidden.shape), ema_slow_next, ema_fast_next)


def solution(mesh):
    fine = Mesh(mesh.devices.reshape(2, 8, 2, 2, 8), AXES)
    dp, seq = ROWS + ("c",), SEQ
    placed = (
        P(dp, seq, None, None),
        P(dp),
        P(),
        P(dp, None),
        P(dp, None),
        P(dp, None),
        P(),
        P(dp, seq, None, None),
    )
    return jax.shard_map(
        on_device,
        mesh=fine,
        in_specs=placed,
        out_specs=(P(dp, seq, None, None), P(dp, None), P(dp, None)),
        check_vma=False,
    )
```

```python
import math

import jax
import jax.numpy as jnp
from jax import lax
from jax.experimental import pallas as pl
from jax.experimental.pallas import tpu as pltpu
from jax.sharding import Mesh
from jax.sharding import PartitionSpec as P

HEADS = 8
HDIM = 72
norm_eps = 1e-06
loss_scale = 128.0
gamma_slow = 16.97
gamma_fast = 6.94
AXES = ("xh", "z", "c", "xl", "y")
SEQ = ("xl", "y")
ROWS = ("xh", "z")
F32 = jnp.float32
BF16 = jnp.bfloat16
MIB = 1024 * 1024


def params(mib=48):
    return pltpu.CompilerParams(vmem_limit_bytes=mib * MIB)


def cost(flops, moved):
    return pl.CostEstimate(flops=flops, bytes_accessed=moved, transcendentals=0)


def swap(value, axis):
    return lax.ppermute(value, axis, [(0, 1), (1, 0)])


def shift(value, away):
    count = lax.axis_size("z")
    return lax.ppermute(value, "z", [(i, (i + away) % count) for i in range(count)])


def half_turn(value):
    return shift(value, lax.axis_size("z") // 2)


def both_turn(value):
    count = lax.axis_size("z")
    pairs = [(i, (count - count * (i // count)) + (i % count + count // 2) % count) for i in range(2 * count)]
    return lax.ppermute(value, ("xh", "z"), pairs)


def corner_swap(value):
    return lax.ppermute(value, ("c", "xl"), [(i, 3 - i) for i in range(4)])


def flip(value, bit):
    return lax.ppermute(value, "y", [(i, i ^ bit) for i in range(lax.axis_size("y"))])


def modulate_table(timesteps, ada_weight):
    half_freq = ada_weight.shape[0] // 2
    frequency = jnp.exp(-math.log(10000.0) * jnp.arange(half_freq, dtype=F32) / half_freq)
    angles = timesteps.astype(F32)[:, None] * frequency[None, :]
    embedding = jnp.concatenate([jnp.cos(angles), jnp.sin(angles)], axis=1).astype(BF16)
    return jnp.dot(embedding, ada_weight, preferred_element_type=F32)


def pack_kernel(hidden_hbm, cot_hbm, out_hbm, hidden_ref, cot_ref, turned_ref, sems):
    width = hidden_hbm.shape[1]
    first = pltpu.make_async_copy(cot_hbm, cot_ref, sems.at[0])
    second = pltpu.make_async_copy(hidden_hbm, hidden_ref, sems.at[1])
    first.start()
    second.start()
    first.wait()
    inner = cot_ref.shape[0]
    turned_ref[:, :inner] = cot_ref[...].T
    right = pltpu.make_async_copy(turned_ref, out_hbm.at[:, pl.ds(width, turned_ref.shape[1])], sems.at[2])
    right.start()
    second.wait()
    left = pltpu.make_async_copy(hidden_ref, out_hbm.at[:, pl.ds(0, width)], sems.at[3])
    left.start()
    right.wait()
    left.wait()


def stats(values):
    average = jnp.mean(values, axis=-1, keepdims=True)
    moved = values - average
    variance = jnp.mean(moved * moved, axis=-1, keepdims=True)
    inverse_std = lax.rsqrt(variance + norm_eps)
    return moved * inverse_std, inverse_std


def pick(spot, pieces):
    out = pieces[0]
    for index in range(1, 4):
        out = jnp.where(spot == index, pieces[index], out)
    return out


def norm_kernel(spot_ref, packed_ref, mod_ref, core_ref, side_ref):
    width = mod_ref.shape[1] // 2
    quarter = width // 8
    centered, _ = stats(packed_ref[:, :width].astype(F32))
    normed = (centered * (1.0 + mod_ref[:, width:]) + mod_ref[:, :width]).astype(BF16)
    cot = packed_ref[:, width : width + 4 * quarter].astype(F32)
    pieces = [cot[:, i * quarter : (i + 1) * quarter] for i in range(4)]
    spot = spot_ref[0]
    own, side, core, both = (pick(spot, [pieces[i ^ flip] for i in range(4)]) for flip in range(4))
    side_ref[:, :width] = normed
    side_ref[:, width : width + 2 * quarter] = jnp.concatenate([side, both], axis=1).astype(BF16)
    core_ref[:, :width] = normed
    core_ref[:, width : width + 2 * quarter] = jnp.concatenate([core, own], axis=1).astype(BF16)


def norm_back_kernel(packed_ref, mod_ref, *refs):
    out_ref = refs[-1]
    width = mod_ref.shape[1] // 2
    centered, inverse_std = stats(packed_ref[:, :width].astype(F32))
    grads = refs[0][...].astype(F32)
    for ref in refs[1:-1]:
        grads = grads + ref[...].astype(F32)
    grads = grads.astype(BF16).astype(F32)
    upstream = grads * (1.0 + mod_ref[:, width:])
    first = jnp.mean(upstream, axis=-1, keepdims=True)
    second = jnp.mean(upstream * centered, axis=-1, keepdims=True)
    out_ref[...] = (inverse_std * (upstream - first - centered * second)).astype(BF16)


def dot(left, right, over):
    return lax.dot_general(left, right, ((over[0], over[1]), ((), ())), preferred_element_type=F32)


def attend_block(projected, out_grad, same, lane):
    factor = 1.0 / math.sqrt(HDIM)
    wide = 2 * HDIM
    query = projected[:, :wide]
    keys = projected[:, wide : 2 * wide]
    values = projected[:, 2 * wide :].astype(BF16)
    query_low, keys_low = query.astype(BF16), keys.astype(BF16)
    query_grad = key_grad = value_grad = None
    for head in range(2):
        mine = (lane >= head * HDIM) & (lane < (head + 1) * HDIM)
        own_query = jnp.where(mine, query, 0.0).astype(BF16)
        own_keys = jnp.where(mine, keys, 0.0).astype(BF16)
        own_out = jnp.where(mine, out_grad, 0.0).astype(BF16)
        scores = dot(own_query, keys_low, ((1,), (1,))) * factor
        scores = jnp.where(same, scores, -1e30)
        top = jnp.max(scores, axis=-1, keepdims=True)
        expo = jnp.exp(scores - top)
        attention = expo / jnp.sum(expo, axis=-1, keepdims=True)
        prob_grad = dot(own_out, values, ((1,), (1,)))
        row_dot = jnp.sum(attention * prob_grad, axis=-1, keepdims=True)
        score_grad = (attention * (prob_grad - row_dot)).astype(BF16)
        parts = (
            dot(score_grad, own_keys, ((1,), (0,))),
            dot(score_grad, own_query, ((0,), (0,))),
            dot(attention.astype(BF16), own_out, ((0,), (0,))),
        )
        if head == 0:
            query_grad, key_grad, value_grad = parts
        else:
            query_grad, key_grad, value_grad = (
                query_grad + parts[0],
                key_grad + parts[1],
                value_grad + parts[2],
            )
    return jnp.concatenate([query_grad * factor, key_grad * factor, value_grad], axis=1)


def tiles_of(block):
    rows = [block[8 * i : 8 * i + 8] for i in range(block.shape[0] // 8)]
    tiles = [row[:, 128 * k : 128 * k + 128] for row in rows for k in range(3)]
    rest = [row[:, 384:] for row in rows] + [jnp.zeros_like(rows[0][:, 384:])]
    pad = jnp.zeros((8, 128 - 2 * rest[0].shape[1]), block.dtype)
    tiles += [jnp.concatenate([rest[i], rest[i + 1], pad], axis=1) for i in range(0, len(rest), 2)]
    return tiles


def block_of(tiles, height):
    count = height // 8
    rows = []
    for i in range(count):
        last = tiles[3 * count + i // 2][:, 48 * (i % 2) : 48 * (i % 2) + 48]
        rows.append(jnp.concatenate(tiles[3 * i : 3 * i + 3] + [last], axis=1))
    return jnp.concatenate(rows, axis=0)


def main_kernel(
    spot_ref, near_hbm, up_hbm, low_hbm, high_hbm, down_hbm, own_hbm, core_hbm, side_hbm, both_hbm, packed_hbm, inner_hbm, outer_hbm,
    raw_ref, own_ref, core_ref, side_ref, both_ref, weight_ref, packed_ref, parts_ref, total_ref, in_sems, out_sems,
):
    tokens = own_ref.shape[0]
    model_width, cols = total_ref.shape
    quarter = cols // 3
    lows = [lax.rem(spot_ref[1] + ahead, 4) for ahead in range(4)]
    half = raw_ref.shape[1] // 2
    tokens_in = ((own_hbm, own_ref), (core_hbm, core_ref), (side_hbm, side_ref), (both_hbm, both_ref))
    pairs = (
        (near_hbm, raw_ref.at[lows[0]]),
        (up_hbm, raw_ref.at[lows[1]]),
        (low_hbm, raw_ref.at[lows[2], pl.ds(0, half)]),
        (high_hbm, raw_ref.at[lows[2], pl.ds(half, half)]),
        (down_hbm, raw_ref.at[lows[3]]),
    ) + tokens_in
    loads = [pltpu.make_async_copy(source, target, in_sems.at[i]) for i, (source, target) in enumerate(pairs)]
    for load in loads:
        load.start()
    row = lax.broadcasted_iota(jnp.int32, (tokens, tokens), 0)
    col = lax.broadcasted_iota(jnp.int32, (tokens, tokens), 1)
    same = lax.rem(row, 16) == lax.rem(col, 16)
    lane = lax.broadcasted_iota(jnp.int32, (tokens, quarter), 1)
    stores = []
    for load in loads[:5]:
        load.wait()
    blocks = [raw_ref[low, group].astype(F32) for group in range(4) for low in range(4)]
    weight_ref[...] = jnp.concatenate(blocks, axis=0).astype(BF16)
    places = ((inner_hbm, 0, 1), (outer_hbm, 0, 0), (inner_hbm, 1, 0), (outer_hbm, 1, 1))
    for index, (target, place, skip) in enumerate(places):
        ref = tokens_in[index][1]
        loads[index + 5].wait()
        projected = dot(ref[:, :model_width], weight_ref[...], ((1,), (0,)))
        projected = projected.astype(BF16).astype(F32)
        cot = ref[:, model_width:].astype(F32)
        out_grad = cot[:, skip * quarter : (skip + 1) * quarter]
        grads = attend_block(projected, out_grad, same, lane).astype(BF16)
        part = dot(ref[:, :model_width], grads, ((0,), (0,)))
        if index == 0:
            total_ref[...] = part
        else:
            total_ref[...] += part
        parts_ref[index] = dot(grads, weight_ref[...], ((1,), (1,))).astype(BF16)
        stores.append(
            pltpu.make_async_copy(
                parts_ref.at[index], target.at[pl.ds(place * tokens, tokens)], out_sems.at[index]
            )
        )
        stores[-1].start()
    height = model_width // 16
    for owner in range(16):
        tiles = tiles_of(total_ref[owner * height : (owner + 1) * height, :])
        packed_ref[owner] = jnp.concatenate(tiles, axis=0).astype(BF16)
        if owner % 4 == 3:
            part = pl.ds(owner - 3, 4)
            stores.append(pltpu.make_async_copy(packed_ref.at[part], packed_hbm.at[part], out_sems.at[4 + owner // 4]))
            stores[-1].start()
    for store in stores:
        store.wait()


def add_kernel(near_ref, got_ref, own_ref, side_ref):
    half = own_ref.shape[0]
    side_ref[...] = (near_ref[half:].astype(F32) + got_ref[half:].astype(F32)).astype(BF16)
    own_ref[...] = (near_ref[:half].astype(F32) + got_ref[:half].astype(F32)).astype(BF16)


def columns_kernel(spot_ref, master_ref, mine_ref, theirs_ref):
    quarter = master_ref.shape[1] // 12
    spot = spot_ref[0]
    for flip, ref in ((0, mine_ref), (2, theirs_ref)):
        parts = []
        for part in range(3):
            pieces = [master_ref[:, (4 * part + i) * quarter : (4 * part + i + 1) * quarter] for i in range(4)]
            parts.append(pick(spot, [pieces[i ^ flip] for i in range(4)]))
        ref[...] = jnp.concatenate(parts, axis=1).astype(BF16)


def pair_kernel(spot_ref, mine_ref, theirs_ref, out_ref):
    mine, theirs = mine_ref[...].astype(F32), theirs_ref[...].astype(F32)
    first = spot_ref[0] < 2
    upper, lower = jnp.where(first, mine, theirs), jnp.where(first, theirs, mine)
    out_ref[...] = jnp.concatenate([upper, lower], axis=0).astype(BF16)


def quad_kernel(spot_ref, own_ref, far_ref, across_ref, both_ref, out_ref):
    place = spot_ref[2]
    out_ref[place] = own_ref[...]
    out_ref[place + 1 - 2 * lax.rem(place, 2)] = far_ref[...]
    out_ref[lax.rem(place + 2, 4)] = across_ref[...]
    out_ref[3 - place] = both_ref[...]


def sum_kernel(parts_ref, out_ref):
    total = parts_ref[0].astype(F32)
    for index in range(1, parts_ref.shape[0]):
        total = total + parts_ref[index].astype(F32)
    out_ref[...] = total.astype(out_ref.dtype)


def join_kernel(left_ref, right_ref, out_ref):
    out_ref[...] = (left_ref[...].astype(F32) + right_ref[...].astype(F32)).astype(BF16)


def rows_kernel(spot_ref, left_ref, right_ref, own_ref, other_ref):
    total = left_ref[...].astype(F32) + right_ref[...].astype(F32)
    height = own_ref.shape[0]
    block = block_of([total[8 * i : 8 * i + 8] for i in range(total.shape[0] // 8)], 2 * height)
    first = spot_ref[0] < 2
    upper, lower = block[:height], block[height:]
    own_ref[...] = jnp.where(first, upper, lower)
    other_ref[...] = jnp.where(first, lower, upper)


def average_kernel(spot_ref, decay_ref, own_ref, side_ref, core_ref, both_ref, slow_ref, fast_ref, slow_out, fast_out):
    quarter = own_ref.shape[1] // 3
    spot = spot_ref[0]
    values = [ref[...] for ref in (own_ref, side_ref, core_ref, both_ref)]
    picked = [pick(spot, [values[i ^ place] for i in range(4)]) for place in range(4)]
    columns = [picked[place][:, part * quarter : (part + 1) * quarter] for part in range(3) for place in range(4)]
    grad = jnp.concatenate(columns, axis=1) / loss_scale
    slow_out[...] = decay_ref[0] * slow_ref[...] + (1.0 - decay_ref[0]) * grad
    fast_out[...] = decay_ref[1] * fast_ref[...] + (1.0 - decay_ref[1]) * grad


def call(kernel, outs, *args, flops=0, scratch=(), mib=16, smem=0, hbm_in=False, hbm_out=()):
    moved = sum(a.size * a.dtype.itemsize for a in args)
    moved += sum(math.prod(shape) * jnp.dtype(kind).itemsize for shape, kind in outs)
    shapes = [jax.ShapeDtypeStruct(shape, kind) for shape, kind in outs]
    body = pltpu.HBM if hbm_in else pltpu.VMEM
    specs = [pl.BlockSpec(memory_space=pltpu.SMEM if i < smem else body) for i in range(len(args))]
    got = pl.pallas_call(
        kernel,
        out_shape=shapes,
        in_specs=specs,
        out_specs=[pl.BlockSpec(memory_space=pltpu.HBM if i in hbm_out else pltpu.VMEM) for i in range(len(shapes))],
        scratch_shapes=list(scratch),
        compiler_params=params(mib),
        cost_estimate=cost(flops, moved),
    )(*args)
    return got[0] if len(got) == 1 else got


def lanes(count):
    return -(-count // 128) * 128


def on_device(hidden, timesteps, ada_weight, master, ema_slow, ema_fast, step_count, cotangent):
    patches, width = hidden.shape[2:]
    inner = cotangent.shape[3]
    own_rows, triple = master.shape
    n_seq = lax.axis_size("xl") * lax.axis_size("y")
    n_rows = lax.axis_size("xh") * lax.axis_size("z")
    quarter = inner // 4
    cols = 3 * quarter
    pair_rows = 2 * own_rows
    core, side = lax.axis_index("c"), lax.axis_index("xl")
    across, along = lax.axis_index("xh"), lax.axis_index("z")
    spots = jnp.stack([2 * core + side, lax.rem(along, 4), 2 * across + along // 4]).astype(jnp.int32)

    loose = lanes(inner)
    packed = call(
        pack_kernel,
        [((patches, width + loose), BF16)],
        hidden[0, 0], cotangent[0, 0].T,
        scratch=[
            pltpu.VMEM((patches, width), BF16),
            pltpu.VMEM((inner, patches), BF16),
            pltpu.VMEM((patches, loose), BF16),
            pltpu.SemaphoreType.DMA((4,)),
        ],
        mib=58,
        hbm_in=True,
        hbm_out=(0,),
    )
    tokens = lax.all_to_all(packed.reshape(n_seq, patches // n_seq, width + loose), SEQ, 0, 0, tiled=True)
    tokens = tokens.reshape(patches, width + loose)

    mine, theirs = call(columns_kernel, [((own_rows, cols), BF16)] * 2, spots, master, smem=1)
    pair = call(pair_kernel, [((pair_rows, cols), BF16)], spots, mine, swap(theirs, "c"), smem=1)
    quad = call(
        quad_kernel,
        [((4, pair_rows, cols), BF16)],
        spots, pair, half_turn(pair), swap(pair, "xh"), both_turn(pair),
        smem=1,
    )
    quad, tokens = lax.optimization_barrier((quad, tokens))

    modulation = modulate_table(timesteps, ada_weight)
    broad = lanes(width + 2 * quarter)
    to_core, to_side = call(norm_kernel, [((patches, broad), BF16)] * 2, spots, tokens, modulation, smem=1)
    from_side = swap(to_side, "xl")
    up, low, high, down = shift(quad, -1), shift(quad[:2], -2), shift(quad[2:], 2), shift(quad, 1)
    to_core, low = lax.optimization_barrier((to_core, low))
    from_core = swap(to_core, "c")
    from_side, up, low, high, down = lax.optimization_barrier((from_side, up, low, high, down))
    from_both = swap(from_side, "c")

    packed, near, far = call(
        main_kernel,
        [((n_rows, 256, 128), BF16), ((2 * patches, width), BF16), ((2 * patches, width), BF16)],
        spots, quad, up, low, high, down, to_core, from_core, from_side, from_both,
        flops=6 * 4 * patches * width * cols,
        scratch=[
            pltpu.VMEM((4, 4, pair_rows, cols), BF16),
            pltpu.VMEM((patches, broad), BF16),
            pltpu.VMEM((patches, broad), BF16),
            pltpu.VMEM((patches, broad), BF16),
            pltpu.VMEM((patches, broad), BF16),
            pltpu.VMEM((width, cols), BF16),
            pltpu.VMEM((n_rows, 256, 128), BF16),
            pltpu.VMEM((4, patches, width), BF16),
            pltpu.VMEM((width, cols), F32),
            pltpu.SemaphoreType.DMA((9,)),
            pltpu.SemaphoreType.DMA((8,)),
        ],
        mib=58,
        smem=1,
        hbm_in=True,
        hbm_out=(0, 1, 2),
    )

    part, give = call(add_kernel, [((patches, width), BF16)] * 2, near, swap(far, "c"))
    back = call(norm_back_kernel, [((patches, width), BF16)], tokens, modulation, part, swap(give, "xl"))

    back = lax.all_to_all(back.reshape(n_seq, patches // n_seq, width), SEQ, 0, 0, tiled=True)

    parts = lax.all_to_all(packed, ROWS, 0, 0, tiled=True)
    piece = ((256, 128), BF16)
    summed = call(sum_kernel, [piece], parts)
    for bit in (1, 2):
        summed = call(join_kernel, [piece], summed, flip(summed, bit))
    own_grad, other_grad = call(rows_kernel, [((own_rows, cols), F32)] * 2, spots, summed, flip(summed, 4), smem=1)
    base = 1.0 - 1.0 / step_count[0].astype(F32)
    decays = jnp.stack([jnp.power(base, gamma_slow + 1.0), jnp.power(base, gamma_fast + 1.0)])
    ema_slow_next, ema_fast_next = call(
        average_kernel,
        [((own_rows, triple), F32)] * 2,
        spots, decays, own_grad, swap(own_grad, "xl"), swap(other_grad, "c"), corner_swap(other_grad), ema_slow, ema_fast,
        smem=2,
    )
    return (back.reshape(hidden.shape), ema_slow_next, ema_fast_next)


def solution(mesh):
    fine = Mesh(mesh.devices.reshape(2, 8, 2, 2, 8), AXES)
    dp, seq = ROWS + ("c",), SEQ
    placed = (
        P(dp, seq, None, None),
        P(dp),
        P(),
        P(dp, None),
        P(dp, None),
        P(dp, None),
        P(),
        P(dp, seq, None, None),
    )
    return jax.shard_map(
        on_device,
        mesh=fine,
        in_specs=placed,
        out_specs=(P(dp, seq, None, None), P(dp, None), P(dp, None)),
        check_vma=False,
    )
```

```python
import math

import jax
import jax.numpy as jnp
from jax import lax
from jax.experimental import pallas as pl
from jax.experimental.pallas import tpu as pltpu
from jax.sharding import Mesh
from jax.sharding import PartitionSpec as P

HEADS = 8
HDIM = 72
norm_eps = 1e-06
loss_scale = 128.0
gamma_slow = 16.97
gamma_fast = 6.94
AXES = ("xh", "z", "c", "xl", "y")
SEQ = ("xl", "y")
ROWS = ("xh", "z")
F32 = jnp.float32
BF16 = jnp.bfloat16
MIB = 1024 * 1024


def params(mib=48):
    return pltpu.CompilerParams(vmem_limit_bytes=mib * MIB)


def cost(flops, moved):
    return pl.CostEstimate(flops=flops, bytes_accessed=moved, transcendentals=0)


def swap(value, axis):
    return lax.ppermute(value, axis, [(0, 1), (1, 0)])


def shift(value, away):
    count = lax.axis_size("z")
    return lax.ppermute(value, "z", [(i, (i + away) % count) for i in range(count)])


def half_turn(value):
    return shift(value, lax.axis_size("z") // 2)


def both_turn(value):
    count = lax.axis_size("z")
    pairs = [(i, (count - count * (i // count)) + (i % count + count // 2) % count) for i in range(2 * count)]
    return lax.ppermute(value, ("xh", "z"), pairs)


def modulate_table(timesteps, ada_weight):
    half_freq = ada_weight.shape[0] // 2
    frequency = jnp.exp(-math.log(10000.0) * jnp.arange(half_freq, dtype=F32) / half_freq)
    angles = timesteps.astype(F32)[:, None] * frequency[None, :]
    embedding = jnp.concatenate([jnp.cos(angles), jnp.sin(angles)], axis=1).astype(BF16)
    return jnp.dot(embedding, ada_weight, preferred_element_type=F32)


def pack_kernel(hidden_hbm, cot_hbm, out_hbm, hidden_ref, cot_ref, turned_ref, sems):
    width = hidden_hbm.shape[1]
    first = pltpu.make_async_copy(cot_hbm, cot_ref, sems.at[0])
    second = pltpu.make_async_copy(hidden_hbm, hidden_ref, sems.at[1])
    first.start()
    second.start()
    first.wait()
    inner = cot_ref.shape[0]
    turned_ref[:, :inner] = cot_ref[...].T
    right = pltpu.make_async_copy(turned_ref, out_hbm.at[:, pl.ds(width, turned_ref.shape[1])], sems.at[2])
    right.start()
    second.wait()
    left = pltpu.make_async_copy(hidden_ref, out_hbm.at[:, pl.ds(0, width)], sems.at[3])
    left.start()
    right.wait()
    left.wait()


def stats(values):
    average = jnp.mean(values, axis=-1, keepdims=True)
    moved = values - average
    variance = jnp.mean(moved * moved, axis=-1, keepdims=True)
    inverse_std = lax.rsqrt(variance + norm_eps)
    return moved * inverse_std, inverse_std


def pick(spot, pieces):
    out = pieces[0]
    for index in range(1, 4):
        out = jnp.where(spot == index, pieces[index], out)
    return out


def norm_kernel(spot_ref, packed_ref, mod_ref, core_ref, side_ref):
    width = mod_ref.shape[1] // 2
    quarter = width // 8
    centered, _ = stats(packed_ref[:, :width].astype(F32))
    normed = (centered * (1.0 + mod_ref[:, width:]) + mod_ref[:, :width]).astype(BF16)
    cot = packed_ref[:, width : width + 4 * quarter].astype(F32)
    pieces = [cot[:, i * quarter : (i + 1) * quarter] for i in range(4)]
    spot = spot_ref[0]
    own, side, core, both = (pick(spot, [pieces[i ^ flip] for i in range(4)]) for flip in range(4))
    side_ref[:, :width] = normed
    side_ref[:, width : width + 2 * quarter] = jnp.concatenate([side, both], axis=1).astype(BF16)
    core_ref[:, :width] = normed
    core_ref[:, width : width + 2 * quarter] = jnp.concatenate([core, own], axis=1).astype(BF16)


def norm_back_kernel(packed_ref, mod_ref, *refs):
    out_ref = refs[-1]
    width = mod_ref.shape[1] // 2
    centered, inverse_std = stats(packed_ref[:, :width].astype(F32))
    grads = refs[0][...].astype(F32)
    for ref in refs[1:-1]:
        grads = grads + ref[...].astype(F32)
    grads = grads.astype(BF16).astype(F32)
    upstream = grads * (1.0 + mod_ref[:, width:])
    first = jnp.mean(upstream, axis=-1, keepdims=True)
    second = jnp.mean(upstream * centered, axis=-1, keepdims=True)
    out_ref[...] = (inverse_std * (upstream - first - centered * second)).astype(BF16)


def dot(left, right, over):
    return lax.dot_general(left, right, ((over[0], over[1]), ((), ())), preferred_element_type=F32)


def attend_block(projected, out_grad, same, lane):
    factor = 1.0 / math.sqrt(HDIM)
    wide = 2 * HDIM
    query = projected[:, :wide]
    keys = projected[:, wide : 2 * wide]
    values = projected[:, 2 * wide :].astype(BF16)
    query_low, keys_low = query.astype(BF16), keys.astype(BF16)
    query_grad = key_grad = value_grad = None
    for head in range(2):
        mine = (lane >= head * HDIM) & (lane < (head + 1) * HDIM)
        own_query = jnp.where(mine, query, 0.0).astype(BF16)
        own_keys = jnp.where(mine, keys, 0.0).astype(BF16)
        own_out = jnp.where(mine, out_grad, 0.0).astype(BF16)
        scores = dot(own_query, keys_low, ((1,), (1,))) * factor
        scores = jnp.where(same, scores, -1e30)
        top = jnp.max(scores, axis=-1, keepdims=True)
        expo = jnp.exp(scores - top)
        attention = expo / jnp.sum(expo, axis=-1, keepdims=True)
        prob_grad = dot(own_out, values, ((1,), (1,)))
        row_dot = jnp.sum(attention * prob_grad, axis=-1, keepdims=True)
        score_grad = (attention * (prob_grad - row_dot)).astype(BF16)
        parts = (
            dot(score_grad, own_keys, ((1,), (0,))),
            dot(score_grad, own_query, ((0,), (0,))),
            dot(attention.astype(BF16), own_out, ((0,), (0,))),
        )
        if head == 0:
            query_grad, key_grad, value_grad = parts
        else:
            query_grad, key_grad, value_grad = (
                query_grad + parts[0],
                key_grad + parts[1],
                value_grad + parts[2],
            )
    return jnp.concatenate([query_grad * factor, key_grad * factor, value_grad], axis=1)


def tiles_of(block):
    rows = [block[8 * i : 8 * i + 8] for i in range(block.shape[0] // 8)]
    tiles = [row[:, 128 * k : 128 * k + 128] for row in rows for k in range(3)]
    rest = [row[:, 384:] for row in rows] + [jnp.zeros_like(rows[0][:, 384:])]
    pad = jnp.zeros((8, 128 - 2 * rest[0].shape[1]), block.dtype)
    tiles += [jnp.concatenate([rest[i], rest[i + 1], pad], axis=1) for i in range(0, len(rest), 2)]
    return tiles


def block_of(tiles, height):
    count = height // 8
    rows = []
    for i in range(count):
        last = tiles[3 * count + i // 2][:, 48 * (i % 2) : 48 * (i % 2) + 48]
        rows.append(jnp.concatenate(tiles[3 * i : 3 * i + 3] + [last], axis=1))
    return jnp.concatenate(rows, axis=0)


def main_kernel(
    spot_ref, near_hbm, up_hbm, low_hbm, high_hbm, down_hbm, own_hbm, core_hbm, side_hbm, both_hbm, packed_hbm, inner_hbm, outer_hbm,
    raw_ref, own_ref, core_ref, side_ref, both_ref, weight_ref, packed_ref, parts_ref, total_ref, in_sems, out_sems,
):
    tokens = own_ref.shape[0]
    model_width, cols = total_ref.shape
    quarter = cols // 3
    lows = [lax.rem(spot_ref[1] + ahead, 4) for ahead in range(4)]
    half = raw_ref.shape[1] // 2
    tokens_in = ((own_hbm, own_ref), (core_hbm, core_ref), (side_hbm, side_ref), (both_hbm, both_ref))
    pairs = (
        (near_hbm, raw_ref.at[lows[0]]),
        (up_hbm, raw_ref.at[lows[1]]),
        (low_hbm, raw_ref.at[lows[2], pl.ds(0, half)]),
        (high_hbm, raw_ref.at[lows[2], pl.ds(half, half)]),
        (down_hbm, raw_ref.at[lows[3]]),
    ) + tokens_in
    loads = [pltpu.make_async_copy(source, target, in_sems.at[i]) for i, (source, target) in enumerate(pairs)]
    for load in loads:
        load.start()
    row = lax.broadcasted_iota(jnp.int32, (tokens, tokens), 0)
    col = lax.broadcasted_iota(jnp.int32, (tokens, tokens), 1)
    same = lax.rem(row, 16) == lax.rem(col, 16)
    lane = lax.broadcasted_iota(jnp.int32, (tokens, quarter), 1)
    stores = []
    for load in loads[:5]:
        load.wait()
    blocks = [raw_ref[low, group].astype(F32) for group in range(4) for low in range(4)]
    weight_ref[...] = jnp.concatenate(blocks, axis=0).astype(BF16)
    places = ((inner_hbm, 0, 1), (outer_hbm, 0, 0), (inner_hbm, 1, 0), (outer_hbm, 1, 1))
    for index, (target, place, skip) in enumerate(places):
        ref = tokens_in[index][1]
        loads[index + 5].wait()
        projected = dot(ref[:, :model_width], weight_ref[...], ((1,), (0,)))
        projected = projected.astype(BF16).astype(F32)
        cot = ref[:, model_width:].astype(F32)
        out_grad = cot[:, skip * quarter : (skip + 1) * quarter]
        grads = attend_block(projected, out_grad, same, lane).astype(BF16)
        part = dot(ref[:, :model_width], grads, ((0,), (0,)))
        if index == 0:
            total_ref[...] = part
        else:
            total_ref[...] += part
        parts_ref[index] = dot(grads, weight_ref[...], ((1,), (1,))).astype(BF16)
        stores.append(
            pltpu.make_async_copy(
                parts_ref.at[index], target.at[pl.ds(place * tokens, tokens)], out_sems.at[index]
            )
        )
        stores[-1].start()
    height = model_width // 16
    pieces = packed_ref.shape[0] // 16
    for owner in range(16):
        tiles = tiles_of(total_ref[owner * height : (owner + 1) * height, :])
        each = len(tiles) // pieces
        for piece in range(pieces):
            packed_ref[owner * pieces + piece] = jnp.concatenate(tiles[each * piece : each * piece + each], axis=0).astype(BF16)
        if owner % 4 == 3:
            part = pl.ds((owner - 3) * pieces, 4 * pieces)
            stores.append(pltpu.make_async_copy(packed_ref.at[part], packed_hbm.at[part], out_sems.at[4 + owner // 4]))
            stores[-1].start()
    for store in stores:
        store.wait()


def add_kernel(near_ref, got_ref, own_ref, side_ref):
    half = own_ref.shape[0]
    side_ref[...] = (near_ref[half:].astype(F32) + got_ref[half:].astype(F32)).astype(BF16)
    own_ref[...] = (near_ref[:half].astype(F32) + got_ref[:half].astype(F32)).astype(BF16)


def columns_kernel(spot_ref, master_ref, mine_ref, theirs_ref):
    quarter = master_ref.shape[1] // 12
    spot = spot_ref[0]
    for flip, ref in ((0, mine_ref), (2, theirs_ref)):
        parts = []
        for part in range(3):
            pieces = [master_ref[:, (4 * part + i) * quarter : (4 * part + i + 1) * quarter] for i in range(4)]
            parts.append(pick(spot, [pieces[i ^ flip] for i in range(4)]))
        ref[...] = jnp.concatenate(parts, axis=1).astype(BF16)


def pair_kernel(spot_ref, mine_ref, theirs_ref, out_ref):
    mine, theirs = mine_ref[...].astype(F32), theirs_ref[...].astype(F32)
    first = spot_ref[0] < 2
    upper, lower = jnp.where(first, mine, theirs), jnp.where(first, theirs, mine)
    out_ref[...] = jnp.concatenate([upper, lower], axis=0).astype(BF16)


def quad_kernel(spot_ref, own_ref, far_ref, across_ref, both_ref, out_ref):
    place = spot_ref[2]
    out_ref[place] = own_ref[...]
    out_ref[place + 1 - 2 * lax.rem(place, 2)] = far_ref[...]
    out_ref[lax.rem(place + 2, 4)] = across_ref[...]
    out_ref[3 - place] = both_ref[...]


def payload_kernel(parts_ref, back_ref, out_ref):
    total = parts_ref[0].astype(F32)
    for index in range(1, parts_ref.shape[0]):
        total = total + parts_ref[index].astype(F32)
    half = total.shape[0] // 2
    piece = jnp.concatenate([total[:half], total[half:]], axis=1).astype(BF16)
    width = back_ref.shape[1]
    out_ref[:, :width] = back_ref[...]
    for index in range(out_ref.shape[0] // half):
        out_ref[index * half : (index + 1) * half, width:] = piece


def rows_kernel(spot_ref, pieces_ref, own_ref, other_ref):
    width = pieces_ref.shape[2] - 256
    count = pieces_ref.shape[0] // 2
    height = own_ref.shape[1]
    first = spot_ref[0] < 2
    for side in range(2):
        tiles = []
        for index in range(count):
            piece = pieces_ref[side * count + index][:, width:].astype(F32)
            tiles += [piece[:8, :128], piece[8:, :128], piece[:8, 128:], piece[8:, 128:]]
        total = block_of(tiles, 2 * height)
        upper, lower = total[:height], total[height:]
        own_ref[side] = jnp.where(first, upper, lower)
        other_ref[side] = jnp.where(first, lower, upper)


def average_kernel(spot_ref, decay_ref, own_ref, core_ref, slow_ref, fast_ref, slow_out, fast_out):
    quarter = own_ref.shape[2] // 3
    first = spot_ref[0] < 2
    own, other = [own_ref[0], own_ref[1]], [core_ref[0], core_ref[1]]
    places = [jnp.where(first, a, b) for a, b in zip(own + other, other + own)]
    columns = [place[:, part * quarter : (part + 1) * quarter] for part in range(3) for place in places]
    grad = jnp.concatenate(columns, axis=1) / loss_scale
    slow_out[...] = decay_ref[0] * slow_ref[...] + (1.0 - decay_ref[0]) * grad
    fast_out[...] = decay_ref[1] * fast_ref[...] + (1.0 - decay_ref[1]) * grad


def call(kernel, outs, *args, flops=0, scratch=(), mib=16, smem=0, hbm_in=False, hbm_out=()):
    moved = sum(a.size * a.dtype.itemsize for a in args)
    moved += sum(math.prod(shape) * jnp.dtype(kind).itemsize for shape, kind in outs)
    shapes = [jax.ShapeDtypeStruct(shape, kind) for shape, kind in outs]
    body = pltpu.HBM if hbm_in else pltpu.VMEM
    specs = [pl.BlockSpec(memory_space=pltpu.SMEM if i < smem else body) for i in range(len(args))]
    got = pl.pallas_call(
        kernel,
        out_shape=shapes,
        in_specs=specs,
        out_specs=[pl.BlockSpec(memory_space=pltpu.HBM if i in hbm_out else pltpu.VMEM) for i in range(len(shapes))],
        scratch_shapes=list(scratch),
        compiler_params=params(mib),
        cost_estimate=cost(flops, moved),
    )(*args)
    return got[0] if len(got) == 1 else got


def lanes(count):
    return -(-count // 128) * 128


def on_device(hidden, timesteps, ada_weight, master, ema_slow, ema_fast, step_count, cotangent):
    patches, width = hidden.shape[2:]
    inner = cotangent.shape[3]
    own_rows, triple = master.shape
    n_seq = lax.axis_size("xl") * lax.axis_size("y")
    n_rows = lax.axis_size("xh") * lax.axis_size("z")
    n_y = lax.axis_size("y")
    quarter = inner // 4
    cols = 3 * quarter
    pair_rows = 2 * own_rows
    core, side = lax.axis_index("c"), lax.axis_index("xl")
    across, along = lax.axis_index("xh"), lax.axis_index("z")
    spots = jnp.stack([2 * core + side, lax.rem(along, 4), 2 * across + along // 4]).astype(jnp.int32)

    loose = lanes(inner)
    packed = call(
        pack_kernel,
        [((patches, width + loose), BF16)],
        hidden[0, 0], cotangent[0, 0].T,
        scratch=[
            pltpu.VMEM((patches, width), BF16),
            pltpu.VMEM((inner, patches), BF16),
            pltpu.VMEM((patches, loose), BF16),
            pltpu.SemaphoreType.DMA((4,)),
        ],
        mib=58,
        hbm_in=True,
        hbm_out=(0,),
    )
    tokens = lax.all_to_all(packed.reshape(n_seq, patches // n_seq, width + loose), SEQ, 0, 0, tiled=True)
    tokens = tokens.reshape(patches, width + loose)

    mine, theirs = call(columns_kernel, [((own_rows, cols), BF16)] * 2, spots, master, smem=1)
    pair = call(pair_kernel, [((pair_rows, cols), BF16)], spots, mine, swap(theirs, "c"), smem=1)
    quad = call(
        quad_kernel,
        [((4, pair_rows, cols), BF16)],
        spots, pair, half_turn(pair), swap(pair, "xh"), both_turn(pair),
        smem=1,
    )
    quad, tokens = lax.optimization_barrier((quad, tokens))

    modulation = modulate_table(timesteps, ada_weight)
    broad = lanes(width + 2 * quarter)
    to_core, to_side = call(norm_kernel, [((patches, broad), BF16)] * 2, spots, tokens, modulation, smem=1)
    from_side = swap(to_side, "xl")
    up, low, high, down = shift(quad, -1), shift(quad[:2], -2), shift(quad[2:], 2), shift(quad, 1)
    to_core, low = lax.optimization_barrier((to_core, low))
    from_core = swap(to_core, "c")
    from_side, up, low, high, down = lax.optimization_barrier((from_side, up, low, high, down))
    from_both = swap(from_side, "c")

    pieces = n_rows * n_y
    packed, near, far = call(
        main_kernel,
        [((pieces, 32, 128), BF16), ((2 * patches, width), BF16), ((2 * patches, width), BF16)],
        spots, quad, up, low, high, down, to_core, from_core, from_side, from_both,
        flops=6 * 4 * patches * width * cols,
        scratch=[
            pltpu.VMEM((4, 4, pair_rows, cols), BF16),
            pltpu.VMEM((patches, broad), BF16),
            pltpu.VMEM((patches, broad), BF16),
            pltpu.VMEM((patches, broad), BF16),
            pltpu.VMEM((patches, broad), BF16),
            pltpu.VMEM((width, cols), BF16),
            pltpu.VMEM((pieces, 32, 128), BF16),
            pltpu.VMEM((4, patches, width), BF16),
            pltpu.VMEM((width, cols), F32),
            pltpu.SemaphoreType.DMA((9,)),
            pltpu.SemaphoreType.DMA((8,)),
        ],
        mib=58,
        smem=1,
        hbm_in=True,
        hbm_out=(0, 1, 2),
    )

    part, give = call(add_kernel, [((patches, width), BF16)] * 2, near, swap(far, "c"))
    back = call(norm_back_kernel, [((patches, width), BF16)], tokens, modulation, part, swap(give, "xl"))

    parts = lax.all_to_all(packed, ROWS + ("y",), 0, 0, tiled=True)
    joint = call(payload_kernel, [((patches, width + 256), BF16)], parts, back)
    joint = lax.all_to_all(joint.reshape(n_seq, patches // n_seq, width + 256), SEQ, 0, 0, tiled=True)
    own_grad, other_grad = call(rows_kernel, [((2, own_rows, cols), F32)] * 2, spots, joint, smem=1)
    base = 1.0 - 1.0 / step_count[0].astype(F32)
    decays = jnp.stack([jnp.power(base, gamma_slow + 1.0), jnp.power(base, gamma_fast + 1.0)])
    ema_slow_next, ema_fast_next = call(
        average_kernel,
        [((own_rows, triple), F32)] * 2,
        spots, decays, own_grad, swap(other_grad, "c"), ema_slow, ema_fast,
        smem=2,
    )
    return (joint[:, :, :width].reshape(hidden.shape), ema_slow_next, ema_fast_next)


def solution(mesh):
    fine = Mesh(mesh.devices.reshape(2, 8, 2, 2, 8), AXES)
    dp, seq = ROWS + ("c",), SEQ
    placed = (
        P(dp, seq, None, None),
        P(dp),
        P(),
        P(dp, None),
        P(dp, None),
        P(dp, None),
        P(),
        P(dp, seq, None, None),
    )
    return jax.shard_map(
        on_device,
        mesh=fine,
        in_specs=placed,
        out_specs=(P(dp, seq, None, None), P(dp, None), P(dp, None)),
        check_vma=False,
    )
```

```python
import math

import jax
import jax.numpy as jnp
from jax import lax
from jax.experimental import pallas as pl
from jax.experimental.pallas import tpu as pltpu
from jax.sharding import Mesh
from jax.sharding import PartitionSpec as P

HEADS = 8
HDIM = 72
norm_eps = 1e-06
loss_scale = 128.0
gamma_slow = 16.97
gamma_fast = 6.94
AXES = ("xh", "z", "c", "xl", "y")
SEQ = ("xl", "y")
ROWS = ("xh", "z")
F32 = jnp.float32
BF16 = jnp.bfloat16
MIB = 1024 * 1024


def params(mib=48):
    return pltpu.CompilerParams(vmem_limit_bytes=mib * MIB)


def cost(flops, moved):
    return pl.CostEstimate(flops=flops, bytes_accessed=moved, transcendentals=0)


def swap(value, axis):
    return lax.ppermute(value, axis, [(0, 1), (1, 0)])


def shift(value, away):
    count = lax.axis_size("z")
    return lax.ppermute(value, "z", [(i, (i + away) % count) for i in range(count)])


def half_turn(value):
    return shift(value, lax.axis_size("z") // 2)


def both_turn(value):
    count = lax.axis_size("z")
    pairs = [(i, (count - count * (i // count)) + (i % count + count // 2) % count) for i in range(2 * count)]
    return lax.ppermute(value, ("xh", "z"), pairs)


def modulate_table(timesteps, ada_weight):
    half_freq = ada_weight.shape[0] // 2
    frequency = jnp.exp(-math.log(10000.0) * jnp.arange(half_freq, dtype=F32) / half_freq)
    angles = timesteps.astype(F32)[:, None] * frequency[None, :]
    embedding = jnp.concatenate([jnp.cos(angles), jnp.sin(angles)], axis=1).astype(BF16)
    return jnp.dot(embedding, ada_weight, preferred_element_type=F32)


def pack_kernel(hidden_hbm, cot_hbm, out_hbm, hidden_ref, cot_ref, turned_ref, sems):
    width = hidden_hbm.shape[1]
    first = pltpu.make_async_copy(cot_hbm, cot_ref, sems.at[0])
    second = pltpu.make_async_copy(hidden_hbm, hidden_ref, sems.at[1])
    first.start()
    second.start()
    first.wait()
    inner = cot_ref.shape[0]
    turned_ref[:, :inner] = cot_ref[...].T
    right = pltpu.make_async_copy(turned_ref, out_hbm.at[:, pl.ds(width, turned_ref.shape[1])], sems.at[2])
    right.start()
    second.wait()
    left = pltpu.make_async_copy(hidden_ref, out_hbm.at[:, pl.ds(0, width)], sems.at[3])
    left.start()
    right.wait()
    left.wait()


def stats(values):
    average = jnp.mean(values, axis=-1, keepdims=True)
    moved = values - average
    variance = jnp.mean(moved * moved, axis=-1, keepdims=True)
    inverse_std = lax.rsqrt(variance + norm_eps)
    return moved * inverse_std, inverse_std


def pick(spot, pieces):
    out = pieces[0]
    for index in range(1, 4):
        out = jnp.where(spot == index, pieces[index], out)
    return out


def norm_kernel(spot_ref, packed_ref, mod_ref, core_ref, side_ref):
    width = mod_ref.shape[1] // 2
    quarter = width // 8
    centered, _ = stats(packed_ref[:, :width].astype(F32))
    normed = (centered * (1.0 + mod_ref[:, width:]) + mod_ref[:, :width]).astype(BF16)
    cot = packed_ref[:, width : width + 4 * quarter].astype(F32)
    pieces = [cot[:, i * quarter : (i + 1) * quarter] for i in range(4)]
    spot = spot_ref[0]
    own, side, core, both = (pick(spot, [pieces[i ^ flip] for i in range(4)]) for flip in range(4))
    side_ref[:, :width] = normed
    side_ref[:, width : width + 2 * quarter] = jnp.concatenate([side, both], axis=1).astype(BF16)
    core_ref[:, :width] = normed
    core_ref[:, width : width + 2 * quarter] = jnp.concatenate([core, own], axis=1).astype(BF16)


def norm_back_kernel(packed_ref, mod_ref, *refs):
    out_ref = refs[-1]
    width = mod_ref.shape[1] // 2
    centered, inverse_std = stats(packed_ref[:, :width].astype(F32))
    grads = refs[0][...].astype(F32)
    for ref in refs[1:-1]:
        grads = grads + ref[...].astype(F32)
    grads = grads.astype(BF16).astype(F32)
    upstream = grads * (1.0 + mod_ref[:, width:])
    first = jnp.mean(upstream, axis=-1, keepdims=True)
    second = jnp.mean(upstream * centered, axis=-1, keepdims=True)
    out_ref[...] = (inverse_std * (upstream - first - centered * second)).astype(BF16)


def dot(left, right, over):
    return lax.dot_general(left, right, ((over[0], over[1]), ((), ())), preferred_element_type=F32)


def attend_block(projected, out_grad, same, lane):
    factor = 1.0 / math.sqrt(HDIM)
    wide = 2 * HDIM
    query = projected[:, :wide]
    keys = projected[:, wide : 2 * wide]
    values = projected[:, 2 * wide :].astype(BF16)
    query_low, keys_low = query.astype(BF16), keys.astype(BF16)
    query_grad = key_grad = value_grad = None
    for head in range(2):
        mine = (lane >= head * HDIM) & (lane < (head + 1) * HDIM)
        own_query = jnp.where(mine, query, 0.0).astype(BF16)
        own_keys = jnp.where(mine, keys, 0.0).astype(BF16)
        own_out = jnp.where(mine, out_grad, 0.0).astype(BF16)
        scores = dot(own_query, keys_low, ((1,), (1,))) * factor
        scores = jnp.where(same, scores, -1e30)
        top = jnp.max(scores, axis=-1, keepdims=True)
        expo = jnp.exp(scores - top)
        attention = expo * (1.0 / jnp.sum(expo, axis=-1, keepdims=True))
        prob_grad = dot(own_out, values, ((1,), (1,)))
        row_dot = jnp.sum(attention * prob_grad, axis=-1, keepdims=True)
        score_grad = (attention * (prob_grad - row_dot)).astype(BF16)
        parts = (
            dot(score_grad, own_keys, ((1,), (0,))),
            dot(score_grad, own_query, ((0,), (0,))),
            dot(attention.astype(BF16), own_out, ((0,), (0,))),
        )
        if head == 0:
            query_grad, key_grad, value_grad = parts
        else:
            query_grad, key_grad, value_grad = (
                query_grad + parts[0],
                key_grad + parts[1],
                value_grad + parts[2],
            )
    return jnp.concatenate([query_grad * factor, key_grad * factor, value_grad], axis=1)


def tiles_of(block):
    rows = [block[8 * i : 8 * i + 8] for i in range(block.shape[0] // 8)]
    tiles = [row[:, 128 * k : 128 * k + 128] for row in rows for k in range(3)]
    rest = [row[:, 384:] for row in rows] + [jnp.zeros_like(rows[0][:, 384:])]
    pad = jnp.zeros((8, 128 - 2 * rest[0].shape[1]), block.dtype)
    tiles += [jnp.concatenate([rest[i], rest[i + 1], pad], axis=1) for i in range(0, len(rest), 2)]
    return tiles


def block_of(tiles, height):
    count = height // 8
    rows = []
    for i in range(count):
        last = tiles[3 * count + i // 2][:, 48 * (i % 2) : 48 * (i % 2) + 48]
        rows.append(jnp.concatenate(tiles[3 * i : 3 * i + 3] + [last], axis=1))
    return jnp.concatenate(rows, axis=0)


def main_kernel(
    spot_ref, near_hbm, up_hbm, low_hbm, high_hbm, down_hbm, own_hbm, core_hbm, side_hbm, both_hbm, packed_hbm, inner_hbm, outer_hbm,
    raw_ref, token_ref, weight_ref, packed_ref, parts_ref, total_ref, grads_ref, in_sems, out_sems,
):
    tokens = own_hbm.shape[0]
    model_width, cols = total_ref.shape
    quarter = cols // 3
    lows = [lax.rem(spot_ref[1] + ahead, 4) for ahead in range(4)]
    half = raw_ref.shape[1] // 2
    sources = (own_hbm, core_hbm, side_hbm, both_hbm)
    pairs = (
        (near_hbm, raw_ref.at[lows[0]]),
        (up_hbm, raw_ref.at[lows[1]]),
        (low_hbm, raw_ref.at[lows[2], pl.ds(0, half)]),
        (high_hbm, raw_ref.at[lows[2], pl.ds(half, half)]),
        (down_hbm, raw_ref.at[lows[3]]),
    ) + tuple((source, token_ref.at[pl.ds(i * tokens, tokens)]) for i, source in enumerate(sources))
    loads = [pltpu.make_async_copy(source, target, in_sems.at[i]) for i, (source, target) in enumerate(pairs)]
    for load in loads:
        load.start()
    row = lax.broadcasted_iota(jnp.int32, (tokens, tokens), 0)
    col = lax.broadcasted_iota(jnp.int32, (tokens, tokens), 1)
    same = lax.rem(row, 16) == lax.rem(col, 16)
    lane = lax.broadcasted_iota(jnp.int32, (tokens, quarter), 1)
    for load in loads[:5]:
        load.wait()
    blocks = [raw_ref[low, group].astype(F32) for group in range(4) for low in range(4)]
    weight_ref[...] = jnp.concatenate(blocks, axis=0).astype(BF16)
    for load in loads[5:]:
        load.wait()
    projected_all = dot(token_ref[:, :model_width], weight_ref[...], ((1,), (0,)))
    for index, skip in enumerate((1, 0, 0, 1)):
        here = slice(index * tokens, (index + 1) * tokens)
        projected = projected_all[here]
        projected = projected.astype(BF16).astype(F32)
        out_grad = token_ref[here, model_width + skip * quarter : model_width + (skip + 1) * quarter].astype(F32)
        grads_ref[here, :] = attend_block(projected, out_grad, same, lane).astype(BF16)
    total_ref[...] = dot(token_ref[:, :model_width], grads_ref[...], ((0,), (0,)))
    height = model_width // 16
    pieces = packed_ref.shape[0] // 16
    stores = []
    for owner in range(16):
        tiles = tiles_of(total_ref[owner * height : (owner + 1) * height, :])
        each = len(tiles) // pieces
        for piece in range(pieces):
            packed_ref[owner * pieces + piece] = jnp.concatenate(tiles[each * piece : each * piece + each], axis=0).astype(BF16)
        if owner % 4 == 3:
            part = pl.ds((owner - 3) * pieces, 4 * pieces)
            stores.append(pltpu.make_async_copy(packed_ref.at[part], packed_hbm.at[part], out_sems.at[4 + owner // 4]))
            stores[-1].start()
    for index, (target, place) in enumerate(((inner_hbm, 0), (outer_hbm, 0), (inner_hbm, 1), (outer_hbm, 1))):
        parts_ref[index] = dot(grads_ref[index * tokens : (index + 1) * tokens, :], weight_ref[...], ((1,), (1,))).astype(BF16)
        stores.append(
            pltpu.make_async_copy(parts_ref.at[index], target.at[pl.ds(place * tokens, tokens)], out_sems.at[index])
        )
        stores[-1].start()
    for store in stores:
        store.wait()


def add_kernel(near_ref, got_ref, own_ref, side_ref):
    half = own_ref.shape[0]
    side_ref[...] = (near_ref[half:].astype(F32) + got_ref[half:].astype(F32)).astype(BF16)
    own_ref[...] = (near_ref[:half].astype(F32) + got_ref[:half].astype(F32)).astype(BF16)


def columns_kernel(spot_ref, master_ref, mine_ref, theirs_ref):
    quarter = master_ref.shape[1] // 12
    spot = spot_ref[0]
    for flip, ref in ((0, mine_ref), (2, theirs_ref)):
        parts = []
        for part in range(3):
            pieces = [master_ref[:, (4 * part + i) * quarter : (4 * part + i + 1) * quarter] for i in range(4)]
            parts.append(pick(spot, [pieces[i ^ flip] for i in range(4)]))
        ref[...] = jnp.concatenate(parts, axis=1).astype(BF16)


def pair_kernel(spot_ref, mine_ref, theirs_ref, out_ref):
    mine, theirs = mine_ref[...].astype(F32), theirs_ref[...].astype(F32)
    first = spot_ref[0] < 2
    upper, lower = jnp.where(first, mine, theirs), jnp.where(first, theirs, mine)
    out_ref[...] = jnp.concatenate([upper, lower], axis=0).astype(BF16)


def quad_kernel(spot_ref, own_ref, far_ref, across_ref, both_ref, out_ref):
    place = spot_ref[2]
    out_ref[place] = own_ref[...]
    out_ref[place + 1 - 2 * lax.rem(place, 2)] = far_ref[...]
    out_ref[lax.rem(place + 2, 4)] = across_ref[...]
    out_ref[3 - place] = both_ref[...]


def payload_kernel(parts_ref, back_ref, out_ref):
    total = parts_ref[0].astype(F32)
    for index in range(1, parts_ref.shape[0]):
        total = total + parts_ref[index].astype(F32)
    half = total.shape[0] // 2
    piece = jnp.concatenate([total[:half], total[half:]], axis=1).astype(BF16)
    width = back_ref.shape[1]
    out_ref[:, :width] = back_ref[...]
    for index in range(out_ref.shape[0] // half):
        out_ref[index * half : (index + 1) * half, width:] = piece


def rows_kernel(spot_ref, pieces_ref, own_ref, other_ref):
    width = pieces_ref.shape[2] - 256
    count = pieces_ref.shape[0] // 2
    height = own_ref.shape[1]
    first = spot_ref[0] < 2
    for side in range(2):
        tiles = []
        for index in range(count):
            piece = pieces_ref[side * count + index][:, width:].astype(F32)
            tiles += [piece[:8, :128], piece[8:, :128], piece[:8, 128:], piece[8:, 128:]]
        total = block_of(tiles, 2 * height)
        upper, lower = total[:height], total[height:]
        own_ref[side] = jnp.where(first, upper, lower)
        other_ref[side] = jnp.where(first, lower, upper)


def average_kernel(spot_ref, decay_ref, own_ref, core_ref, slow_ref, fast_ref, slow_out, fast_out):
    quarter = own_ref.shape[2] // 3
    first = spot_ref[0] < 2
    own, other = [own_ref[0], own_ref[1]], [core_ref[0], core_ref[1]]
    places = [jnp.where(first, a, b) for a, b in zip(own + other, other + own)]
    columns = [place[:, part * quarter : (part + 1) * quarter] for part in range(3) for place in places]
    grad = jnp.concatenate(columns, axis=1) / loss_scale
    slow_out[...] = decay_ref[0] * slow_ref[...] + (1.0 - decay_ref[0]) * grad
    fast_out[...] = decay_ref[1] * fast_ref[...] + (1.0 - decay_ref[1]) * grad


def call(kernel, outs, *args, flops=0, scratch=(), mib=16, smem=0, hbm_in=False, hbm_out=()):
    moved = sum(a.size * a.dtype.itemsize for a in args)
    moved += sum(math.prod(shape) * jnp.dtype(kind).itemsize for shape, kind in outs)
    shapes = [jax.ShapeDtypeStruct(shape, kind) for shape, kind in outs]
    body = pltpu.HBM if hbm_in else pltpu.VMEM
    specs = [pl.BlockSpec(memory_space=pltpu.SMEM if i < smem else body) for i in range(len(args))]
    got = pl.pallas_call(
        kernel,
        out_shape=shapes,
        in_specs=specs,
        out_specs=[pl.BlockSpec(memory_space=pltpu.HBM if i in hbm_out else pltpu.VMEM) for i in range(len(shapes))],
        scratch_shapes=list(scratch),
        compiler_params=params(mib),
        cost_estimate=cost(flops, moved),
    )(*args)
    return got[0] if len(got) == 1 else got


def lanes(count):
    return -(-count // 128) * 128


def on_device(hidden, timesteps, ada_weight, master, ema_slow, ema_fast, step_count, cotangent):
    patches, width = hidden.shape[2:]
    inner = cotangent.shape[3]
    own_rows, triple = master.shape
    n_seq = lax.axis_size("xl") * lax.axis_size("y")
    n_rows = lax.axis_size("xh") * lax.axis_size("z")
    n_y = lax.axis_size("y")
    quarter = inner // 4
    cols = 3 * quarter
    pair_rows = 2 * own_rows
    core, side = lax.axis_index("c"), lax.axis_index("xl")
    across, along = lax.axis_index("xh"), lax.axis_index("z")
    spots = jnp.stack([2 * core + side, lax.rem(along, 4), 2 * across + along // 4]).astype(jnp.int32)

    loose = lanes(inner)
    packed = call(
        pack_kernel,
        [((patches, width + loose), BF16)],
        hidden[0, 0], cotangent[0, 0].T,
        scratch=[
            pltpu.VMEM((patches, width), BF16),
            pltpu.VMEM((inner, patches), BF16),
            pltpu.VMEM((patches, loose), BF16),
            pltpu.SemaphoreType.DMA((4,)),
        ],
        mib=58,
        hbm_in=True,
        hbm_out=(0,),
    )
    tokens = lax.all_to_all(packed.reshape(n_seq, patches // n_seq, width + loose), SEQ, 0, 0, tiled=True)
    tokens = tokens.reshape(patches, width + loose)

    mine, theirs = call(columns_kernel, [((own_rows, cols), BF16)] * 2, spots, master, smem=1)
    pair = call(pair_kernel, [((pair_rows, cols), BF16)], spots, mine, swap(theirs, "c"), smem=1)
    quad = call(
        quad_kernel,
        [((4, pair_rows, cols), BF16)],
        spots, pair, half_turn(pair), swap(pair, "xh"), both_turn(pair),
        smem=1,
    )
    quad, tokens = lax.optimization_barrier((quad, tokens))

    modulation = modulate_table(timesteps, ada_weight)
    broad = lanes(width + 2 * quarter)
    to_core, to_side = call(norm_kernel, [((patches, broad), BF16)] * 2, spots, tokens, modulation, smem=1)
    from_side = swap(to_side, "xl")
    up, low, high, down = shift(quad, -1), shift(quad[:2], -2), shift(quad[2:], 2), shift(quad, 1)
    to_core, low = lax.optimization_barrier((to_core, low))
    from_core = swap(to_core, "c")
    from_side, up, low, high, down = lax.optimization_barrier((from_side, up, low, high, down))
    from_both = swap(from_side, "c")

    pieces = n_rows * n_y
    packed, near, far = call(
        main_kernel,
        [((pieces, 32, 128), BF16), ((2 * patches, width), BF16), ((2 * patches, width), BF16)],
        spots, quad, up, low, high, down, to_core, from_core, from_side, from_both,
        flops=6 * 4 * patches * width * cols,
        scratch=[
            pltpu.VMEM((4, 4, pair_rows, cols), BF16),
            pltpu.VMEM((4 * patches, broad), BF16),
            pltpu.VMEM((width, cols), BF16),
            pltpu.VMEM((pieces, 32, 128), BF16),
            pltpu.VMEM((4, patches, width), BF16),
            pltpu.VMEM((width, cols), F32),
            pltpu.VMEM((4 * patches, cols), BF16),
            pltpu.SemaphoreType.DMA((9,)),
            pltpu.SemaphoreType.DMA((8,)),
        ],
        mib=58,
        smem=1,
        hbm_in=True,
        hbm_out=(0, 1, 2),
    )

    part, give = call(add_kernel, [((patches, width), BF16)] * 2, near, swap(far, "c"))
    back = call(norm_back_kernel, [((patches, width), BF16)], tokens, modulation, part, swap(give, "xl"))

    parts = lax.all_to_all(packed, ROWS + ("y",), 0, 0, tiled=True)
    joint = call(payload_kernel, [((patches, width + 256), BF16)], parts, back)
    joint = lax.all_to_all(joint.reshape(n_seq, patches // n_seq, width + 256), SEQ, 0, 0, tiled=True)
    own_grad, other_grad = call(rows_kernel, [((2, own_rows, cols), F32)] * 2, spots, joint, smem=1)
    base = 1.0 - 1.0 / step_count[0].astype(F32)
    decays = jnp.stack([jnp.power(base, gamma_slow + 1.0), jnp.power(base, gamma_fast + 1.0)])
    ema_slow_next, ema_fast_next = call(
        average_kernel,
        [((own_rows, triple), F32)] * 2,
        spots, decays, own_grad, swap(other_grad, "c"), ema_slow, ema_fast,
        smem=2,
    )
    return (joint[:, :, :width].reshape(hidden.shape), ema_slow_next, ema_fast_next)


def solution(mesh):
    fine = Mesh(mesh.devices.reshape(2, 8, 2, 2, 8), AXES)
    dp, seq = ROWS + ("c",), SEQ
    placed = (
        P(dp, seq, None, None),
        P(dp),
        P(),
        P(dp, None),
        P(dp, None),
        P(dp, None),
        P(),
        P(dp, seq, None, None),
    )
    return jax.shard_map(
        on_device,
        mesh=fine,
        in_specs=placed,
        out_specs=(P(dp, seq, None, None), P(dp, None), P(dp, None)),
        check_vma=False,
    )
```

```python
import math

import jax
import jax.numpy as jnp
from jax import lax
from jax.experimental import pallas as pl
from jax.experimental.pallas import tpu as pltpu
from jax.sharding import Mesh
from jax.sharding import PartitionSpec as P

HEADS = 8
HDIM = 72
norm_eps = 1e-06
loss_scale = 128.0
gamma_slow = 16.97
gamma_fast = 6.94
AXES = ("xh", "z", "c", "xl", "y")
SEQ = ("xl", "y")
ROWS = ("xh", "z")
F32 = jnp.float32
BF16 = jnp.bfloat16
MIB = 1024 * 1024


def params(mib=48):
    return pltpu.CompilerParams(vmem_limit_bytes=mib * MIB)


def cost(flops, moved):
    return pl.CostEstimate(flops=flops, bytes_accessed=moved, transcendentals=0)


def swap(value, axis):
    return lax.ppermute(value, axis, [(0, 1), (1, 0)])


def shift(value, away):
    count = lax.axis_size("z")
    return lax.ppermute(value, "z", [(i, (i + away) % count) for i in range(count)])


def half_turn(value):
    return shift(value, lax.axis_size("z") // 2)


def both_turn(value):
    count = lax.axis_size("z")
    pairs = [(i, (count - count * (i // count)) + (i % count + count // 2) % count) for i in range(2 * count)]
    return lax.ppermute(value, ("xh", "z"), pairs)


def modulate_table(timesteps, ada_weight):
    half_freq = ada_weight.shape[0] // 2
    frequency = jnp.exp(-math.log(10000.0) * jnp.arange(half_freq, dtype=F32) / half_freq)
    angles = timesteps.astype(F32)[:, None] * frequency[None, :]
    embedding = jnp.concatenate([jnp.cos(angles), jnp.sin(angles)], axis=1).astype(BF16)
    return jnp.dot(embedding, ada_weight, preferred_element_type=F32)


def pack_kernel(hidden_hbm, cot_hbm, out_hbm, hidden_ref, cot_ref, turned_ref, sems):
    width = hidden_hbm.shape[1]
    first = pltpu.make_async_copy(cot_hbm, cot_ref, sems.at[0])
    second = pltpu.make_async_copy(hidden_hbm, hidden_ref, sems.at[1])
    first.start()
    second.start()
    first.wait()
    inner = cot_ref.shape[0]
    turned_ref[:, :inner] = cot_ref[...].T
    right = pltpu.make_async_copy(turned_ref, out_hbm.at[:, pl.ds(width, turned_ref.shape[1])], sems.at[2])
    right.start()
    second.wait()
    left = pltpu.make_async_copy(hidden_ref, out_hbm.at[:, pl.ds(0, width)], sems.at[3])
    left.start()
    right.wait()
    left.wait()


def stats(values):
    average = jnp.mean(values, axis=-1, keepdims=True)
    moved = values - average
    variance = jnp.mean(moved * moved, axis=-1, keepdims=True)
    inverse_std = lax.rsqrt(variance + norm_eps)
    return moved * inverse_std, inverse_std


def pick(spot, pieces):
    out = pieces[0]
    for index in range(1, 4):
        out = jnp.where(spot == index, pieces[index], out)
    return out


def norm_kernel(spot_ref, packed_ref, mod_ref, core_ref, side_ref):
    width = mod_ref.shape[1] // 2
    quarter = width // 8
    centered, _ = stats(packed_ref[:, :width].astype(F32))
    normed = (centered * (1.0 + mod_ref[:, width:]) + mod_ref[:, :width]).astype(BF16)
    cot = packed_ref[:, width : width + 4 * quarter].astype(F32)
    pieces = [cot[:, i * quarter : (i + 1) * quarter] for i in range(4)]
    spot = spot_ref[0]
    own, side, core, both = (pick(spot, [pieces[i ^ flip] for i in range(4)]) for flip in range(4))
    side_ref[:, :width] = normed
    side_ref[:, width : width + 2 * quarter] = jnp.concatenate([side, both], axis=1).astype(BF16)
    core_ref[:, :width] = normed
    core_ref[:, width : width + 2 * quarter] = jnp.concatenate([core, own], axis=1).astype(BF16)


def norm_back_kernel(packed_ref, mod_ref, *refs):
    out_ref = refs[-1]
    width = mod_ref.shape[1] // 2
    centered, inverse_std = stats(packed_ref[:, :width].astype(F32))
    grads = refs[0][...].astype(F32)
    for ref in refs[1:-1]:
        grads = grads + ref[...].astype(F32)
    grads = grads.astype(BF16).astype(F32)
    upstream = grads * (1.0 + mod_ref[:, width:])
    first = jnp.mean(upstream, axis=-1, keepdims=True)
    second = jnp.mean(upstream * centered, axis=-1, keepdims=True)
    out_ref[...] = (inverse_std * (upstream - first - centered * second)).astype(BF16)


def dot(left, right, over):
    return lax.dot_general(left, right, ((over[0], over[1]), ((), ())), preferred_element_type=F32)


def attend_block(projected, out_grad, same, lane):
    factor = 1.0 / math.sqrt(HDIM)
    wide = 2 * HDIM
    query = projected[:, :wide]
    keys = projected[:, wide : 2 * wide]
    values = projected[:, 2 * wide :].astype(BF16)
    query_low, keys_low = query.astype(BF16), keys.astype(BF16)
    query_grad = key_grad = value_grad = None
    for head in range(2):
        mine = (lane >= head * HDIM) & (lane < (head + 1) * HDIM)
        own_query = jnp.where(mine, query, 0.0).astype(BF16)
        own_keys = jnp.where(mine, keys, 0.0).astype(BF16)
        own_out = jnp.where(mine, out_grad, 0.0).astype(BF16)
        scores = dot(own_query, keys_low, ((1,), (1,))) * factor
        scores = jnp.where(same, scores, -1e30)
        top = jnp.max(scores, axis=-1, keepdims=True)
        expo = jnp.exp(scores - top)
        attention = expo * (1.0 / jnp.sum(expo, axis=-1, keepdims=True))
        prob_grad = dot(own_out, values, ((1,), (1,)))
        row_dot = jnp.sum(attention * prob_grad, axis=-1, keepdims=True)
        score_grad = (attention * (prob_grad - row_dot)).astype(BF16)
        parts = (
            dot(score_grad, own_keys, ((1,), (0,))),
            dot(score_grad, own_query, ((0,), (0,))),
            dot(attention.astype(BF16), own_out, ((0,), (0,))),
        )
        if head == 0:
            query_grad, key_grad, value_grad = parts
        else:
            query_grad, key_grad, value_grad = (
                query_grad + parts[0],
                key_grad + parts[1],
                value_grad + parts[2],
            )
    return jnp.concatenate([query_grad * factor, key_grad * factor, value_grad], axis=1)


def tiles_of(block):
    rows = [block[8 * i : 8 * i + 8] for i in range(block.shape[0] // 8)]
    tiles = [row[:, 128 * k : 128 * k + 128] for row in rows for k in range(3)]
    rest = [row[:, 384:] for row in rows] + [jnp.zeros_like(rows[0][:, 384:])]
    pad = jnp.zeros((8, 128 - 2 * rest[0].shape[1]), block.dtype)
    tiles += [jnp.concatenate([rest[i], rest[i + 1], pad], axis=1) for i in range(0, len(rest), 2)]
    return tiles


def block_of(tiles, height):
    count = height // 8
    rows = []
    for i in range(count):
        last = tiles[3 * count + i // 2][:, 48 * (i % 2) : 48 * (i % 2) + 48]
        rows.append(jnp.concatenate(tiles[3 * i : 3 * i + 3] + [last], axis=1))
    return jnp.concatenate(rows, axis=0)


def main_kernel(
    spot_ref, near_hbm, up_hbm, low_hbm, high_hbm, down_hbm, own_hbm, core_hbm, side_hbm, both_hbm, packed_hbm, inner_hbm, outer_hbm,
    raw_ref, token_ref, weight_ref, packed_ref, parts_ref, total_ref, grads_ref, in_sems, out_sems,
):
    tokens = own_hbm.shape[0]
    model_width, cols = total_ref.shape
    quarter = cols // 3
    lows = [lax.rem(spot_ref[1] + ahead, 4) for ahead in range(4)]
    half = raw_ref.shape[1] // 2
    sources = (own_hbm, core_hbm, side_hbm, both_hbm)
    pairs = (
        (near_hbm, raw_ref.at[lows[0]]),
        (up_hbm, raw_ref.at[lows[1]]),
        (low_hbm, raw_ref.at[lows[2], pl.ds(0, half)]),
        (high_hbm, raw_ref.at[lows[2], pl.ds(half, half)]),
        (down_hbm, raw_ref.at[lows[3]]),
    ) + tuple((source, token_ref.at[pl.ds(i * tokens, tokens)]) for i, source in enumerate(sources))
    loads = [pltpu.make_async_copy(source, target, in_sems.at[i]) for i, (source, target) in enumerate(pairs)]
    for load in loads:
        load.start()
    row = lax.broadcasted_iota(jnp.int32, (tokens, tokens), 0)
    col = lax.broadcasted_iota(jnp.int32, (tokens, tokens), 1)
    same = lax.rem(row, 16) == lax.rem(col, 16)
    lane = lax.broadcasted_iota(jnp.int32, (tokens, quarter), 1)
    for load in loads[:5]:
        load.wait()
    blocks = [raw_ref[low, group].astype(F32) for group in range(4) for low in range(4)]
    weight_ref[...] = jnp.concatenate(blocks, axis=0).astype(BF16)
    halves = []
    for side in range(2):
        for load in loads[5 + 2 * side : 7 + 2 * side]:
            load.wait()
        rows = token_ref[2 * side * tokens : 2 * (side + 1) * tokens, :model_width]
        halves.append(dot(rows, weight_ref[...], ((1,), (0,))))
    projected_all = jnp.concatenate(halves, axis=0)
    for index, skip in enumerate((1, 0, 0, 1)):
        here = slice(index * tokens, (index + 1) * tokens)
        projected = projected_all[here]
        projected = projected.astype(BF16).astype(F32)
        out_grad = token_ref[here, model_width + skip * quarter : model_width + (skip + 1) * quarter].astype(F32)
        grads_ref[here, :] = attend_block(projected, out_grad, same, lane).astype(BF16)
    total_ref[...] = dot(token_ref[:, :model_width], grads_ref[...], ((0,), (0,)))
    height = model_width // 16
    pieces = packed_ref.shape[0] // 16
    stores = []
    for owner in range(16):
        tiles = tiles_of(total_ref[owner * height : (owner + 1) * height, :])
        each = len(tiles) // pieces
        for piece in range(pieces):
            packed_ref[owner * pieces + piece] = jnp.concatenate(tiles[each * piece : each * piece + each], axis=0).astype(BF16)
        if owner % 4 == 3:
            part = pl.ds((owner - 3) * pieces, 4 * pieces)
            stores.append(pltpu.make_async_copy(packed_ref.at[part], packed_hbm.at[part], out_sems.at[4 + owner // 4]))
            stores[-1].start()
    for index, (target, place) in enumerate(((inner_hbm, 0), (outer_hbm, 0), (inner_hbm, 1), (outer_hbm, 1))):
        parts_ref[index] = dot(grads_ref[index * tokens : (index + 1) * tokens, :], weight_ref[...], ((1,), (1,))).astype(BF16)
        stores.append(
            pltpu.make_async_copy(parts_ref.at[index], target.at[pl.ds(place * tokens, tokens)], out_sems.at[index])
        )
        stores[-1].start()
    for store in stores:
        store.wait()


def add_kernel(near_ref, got_ref, own_ref, side_ref):
    half = own_ref.shape[0]
    side_ref[...] = (near_ref[half:].astype(F32) + got_ref[half:].astype(F32)).astype(BF16)
    own_ref[...] = (near_ref[:half].astype(F32) + got_ref[:half].astype(F32)).astype(BF16)


def columns_kernel(spot_ref, master_ref, mine_ref, theirs_ref):
    quarter = master_ref.shape[1] // 12
    spot = spot_ref[0]
    for flip, ref in ((0, mine_ref), (2, theirs_ref)):
        parts = []
        for part in range(3):
            pieces = [master_ref[:, (4 * part + i) * quarter : (4 * part + i + 1) * quarter] for i in range(4)]
            parts.append(pick(spot, [pieces[i ^ flip] for i in range(4)]))
        ref[...] = jnp.concatenate(parts, axis=1).astype(BF16)


def pair_kernel(spot_ref, mine_ref, theirs_ref, out_ref):
    mine, theirs = mine_ref[...].astype(F32), theirs_ref[...].astype(F32)
    first = spot_ref[0] < 2
    upper, lower = jnp.where(first, mine, theirs), jnp.where(first, theirs, mine)
    out_ref[...] = jnp.concatenate([upper, lower], axis=0).astype(BF16)


def quad_kernel(spot_ref, own_ref, far_ref, across_ref, both_ref, out_ref, lower_ref, upper_ref):
    place = spot_ref[2]
    out_ref[place] = own_ref[...]
    out_ref[place + 1 - 2 * lax.rem(place, 2)] = far_ref[...]
    out_ref[lax.rem(place + 2, 4)] = across_ref[...]
    out_ref[3 - place] = both_ref[...]
    lower_ref[...] = out_ref[:2]
    upper_ref[...] = out_ref[2:]


def payload_kernel(parts_ref, back_ref, out_ref):
    total = parts_ref[0].astype(F32)
    for index in range(1, parts_ref.shape[0]):
        total = total + parts_ref[index].astype(F32)
    half = total.shape[0] // 2
    piece = jnp.concatenate([total[:half], total[half:]], axis=1).astype(BF16)
    width = back_ref.shape[1]
    out_ref[:, :width] = back_ref[...]
    for index in range(out_ref.shape[0] // half):
        out_ref[index * half : (index + 1) * half, width:] = piece


def rows_kernel(spot_ref, pieces_ref, own_ref, other_ref):
    width = pieces_ref.shape[2] - 256
    count = pieces_ref.shape[0] // 2
    height = own_ref.shape[1]
    first = spot_ref[0] < 2
    for side in range(2):
        tiles = []
        for index in range(count):
            piece = pieces_ref[side * count + index][:, width:].astype(F32)
            tiles += [piece[:8, :128], piece[8:, :128], piece[:8, 128:], piece[8:, 128:]]
        total = block_of(tiles, 2 * height)
        upper, lower = total[:height], total[height:]
        own_ref[side] = jnp.where(first, upper, lower)
        other_ref[side] = jnp.where(first, lower, upper)


def average_kernel(spot_ref, decay_ref, own_ref, core_ref, slow_ref, fast_ref, slow_out, fast_out):
    quarter = own_ref.shape[2] // 3
    first = spot_ref[0] < 2
    own, other = [own_ref[0], own_ref[1]], [core_ref[0], core_ref[1]]
    places = [jnp.where(first, a, b) for a, b in zip(own + other, other + own)]
    columns = [place[:, part * quarter : (part + 1) * quarter] for part in range(3) for place in places]
    grad = jnp.concatenate(columns, axis=1) / loss_scale
    slow_out[...] = decay_ref[0] * slow_ref[...] + (1.0 - decay_ref[0]) * grad
    fast_out[...] = decay_ref[1] * fast_ref[...] + (1.0 - decay_ref[1]) * grad


def call(kernel, outs, *args, flops=0, scratch=(), mib=16, smem=0, hbm_in=False, hbm_out=()):
    moved = sum(a.size * a.dtype.itemsize for a in args)
    moved += sum(math.prod(shape) * jnp.dtype(kind).itemsize for shape, kind in outs)
    shapes = [jax.ShapeDtypeStruct(shape, kind) for shape, kind in outs]
    body = pltpu.HBM if hbm_in else pltpu.VMEM
    specs = [pl.BlockSpec(memory_space=pltpu.SMEM if i < smem else body) for i in range(len(args))]
    got = pl.pallas_call(
        kernel,
        out_shape=shapes,
        in_specs=specs,
        out_specs=[pl.BlockSpec(memory_space=pltpu.HBM if i in hbm_out else pltpu.VMEM) for i in range(len(shapes))],
        scratch_shapes=list(scratch),
        compiler_params=params(mib),
        cost_estimate=cost(flops, moved),
    )(*args)
    return got[0] if len(got) == 1 else got


def lanes(count):
    return -(-count // 128) * 128


def on_device(hidden, timesteps, ada_weight, master, ema_slow, ema_fast, step_count, cotangent):
    patches, width = hidden.shape[2:]
    inner = cotangent.shape[3]
    own_rows, triple = master.shape
    n_seq = lax.axis_size("xl") * lax.axis_size("y")
    n_rows = lax.axis_size("xh") * lax.axis_size("z")
    n_y = lax.axis_size("y")
    quarter = inner // 4
    cols = 3 * quarter
    pair_rows = 2 * own_rows
    core, side = lax.axis_index("c"), lax.axis_index("xl")
    across, along = lax.axis_index("xh"), lax.axis_index("z")
    spots = jnp.stack([2 * core + side, lax.rem(along, 4), 2 * across + along // 4]).astype(jnp.int32)

    loose = lanes(inner)
    packed = call(
        pack_kernel,
        [((patches, width + loose), BF16)],
        hidden[0, 0], cotangent[0, 0].T,
        scratch=[
            pltpu.VMEM((patches, width), BF16),
            pltpu.VMEM((inner, patches), BF16),
            pltpu.VMEM((patches, loose), BF16),
            pltpu.SemaphoreType.DMA((4,)),
        ],
        mib=58,
        hbm_in=True,
        hbm_out=(0,),
    )
    tokens = lax.all_to_all(packed.reshape(n_seq, patches // n_seq, width + loose), SEQ, 0, 0, tiled=True)
    tokens = tokens.reshape(patches, width + loose)

    mine, theirs = call(columns_kernel, [((own_rows, cols), BF16)] * 2, spots, master, smem=1)
    pair = call(pair_kernel, [((pair_rows, cols), BF16)], spots, mine, swap(theirs, "c"), smem=1)
    turned, opposite, diagonal = half_turn(pair), swap(pair, "xh"), both_turn(pair)
    turned, opposite, diagonal, tokens = lax.optimization_barrier((turned, opposite, diagonal, tokens))

    modulation = modulate_table(timesteps, ada_weight)
    broad = lanes(width + 2 * quarter)
    to_core, to_side = call(norm_kernel, [((patches, broad), BF16)] * 2, spots, tokens, modulation, smem=1)
    from_side = swap(to_side, "xl")
    pair, turned, opposite, diagonal, to_core = lax.optimization_barrier((pair, turned, opposite, diagonal, to_core))
    quad, lower, upper = call(
        quad_kernel,
        [((4, pair_rows, cols), BF16), ((2, pair_rows, cols), BF16), ((2, pair_rows, cols), BF16)],
        spots, pair, turned, opposite, diagonal,
        smem=1,
    )
    up, low, high, down = shift(quad, -1), shift(lower, -2), shift(upper, 2), shift(quad, 1)
    to_core, low = lax.optimization_barrier((to_core, low))
    from_core = swap(to_core, "c")
    from_side, up, low, high, down = lax.optimization_barrier((from_side, up, low, high, down))
    from_both = swap(from_side, "c")

    pieces = n_rows * n_y
    packed, near, far = call(
        main_kernel,
        [((pieces, 32, 128), BF16), ((2 * patches, width), BF16), ((2 * patches, width), BF16)],
        spots, quad, up, low, high, down, to_core, from_core, from_side, from_both,
        flops=6 * 4 * patches * width * cols,
        scratch=[
            pltpu.VMEM((4, 4, pair_rows, cols), BF16),
            pltpu.VMEM((4 * patches, broad), BF16),
            pltpu.VMEM((width, cols), BF16),
            pltpu.VMEM((pieces, 32, 128), BF16),
            pltpu.VMEM((4, patches, width), BF16),
            pltpu.VMEM((width, cols), F32),
            pltpu.VMEM((4 * patches, cols), BF16),
            pltpu.SemaphoreType.DMA((9,)),
            pltpu.SemaphoreType.DMA((8,)),
        ],
        mib=58,
        smem=1,
        hbm_in=True,
        hbm_out=(0, 1, 2),
    )

    part, give = call(add_kernel, [((patches, width), BF16)] * 2, near, swap(far, "c"))
    back = call(norm_back_kernel, [((patches, width), BF16)], tokens, modulation, part, swap(give, "xl"))

    parts = lax.all_to_all(packed, ROWS + ("y",), 0, 0, tiled=True)
    joint = call(payload_kernel, [((patches, width + 256), BF16)], parts, back)
    joint = lax.all_to_all(joint.reshape(n_seq, patches // n_seq, width + 256), SEQ, 0, 0, tiled=True)
    own_grad, other_grad = call(rows_kernel, [((2, own_rows, cols), F32)] * 2, spots, joint, smem=1)
    base = 1.0 - 1.0 / step_count[0].astype(F32)
    decays = jnp.stack([jnp.power(base, gamma_slow + 1.0), jnp.power(base, gamma_fast + 1.0)])
    ema_slow_next, ema_fast_next = call(
        average_kernel,
        [((own_rows, triple), F32)] * 2,
        spots, decays, own_grad, swap(other_grad, "c"), ema_slow, ema_fast,
        smem=2,
    )
    return (joint[:, :, :width].reshape(hidden.shape), ema_slow_next, ema_fast_next)


def solution(mesh):
    fine = Mesh(mesh.devices.reshape(2, 8, 2, 2, 8), AXES)
    dp, seq = ROWS + ("c",), SEQ
    placed = (
        P(dp, seq, None, None),
        P(dp),
        P(),
        P(dp, None),
        P(dp, None),
        P(dp, None),
        P(),
        P(dp, seq, None, None),
    )
    return jax.shard_map(
        on_device,
        mesh=fine,
        in_specs=placed,
        out_specs=(P(dp, seq, None, None), P(dp, None), P(dp, None)),
        check_vma=False,
    )
```

```python
import math

import jax
import jax.numpy as jnp
from jax import lax
from jax.experimental import pallas as pl
from jax.experimental.pallas import tpu as pltpu
from jax.sharding import Mesh
from jax.sharding import PartitionSpec as P

HEADS = 8
HDIM = 72
norm_eps = 1e-06
loss_scale = 128.0
gamma_slow = 16.97
gamma_fast = 6.94
AXES = ("xh", "z", "c", "xl", "y")
SEQ = ("xl", "y")
ROWS = ("xh", "z")
F32 = jnp.float32
BF16 = jnp.bfloat16
MIB = 1024 * 1024


def params(mib=48):
    return pltpu.CompilerParams(vmem_limit_bytes=mib * MIB)


def cost(flops, moved):
    return pl.CostEstimate(flops=flops, bytes_accessed=moved, transcendentals=0)


def swap(value, axis):
    return lax.ppermute(value, axis, [(0, 1), (1, 0)])


def shift(value, away):
    count = lax.axis_size("z")
    return lax.ppermute(value, "z", [(i, (i + away) % count) for i in range(count)])


def half_turn(value):
    return shift(value, lax.axis_size("z") // 2)


def both_turn(value):
    count = lax.axis_size("z")
    pairs = [(i, (count - count * (i // count)) + (i % count + count // 2) % count) for i in range(2 * count)]
    return lax.ppermute(value, ("xh", "z"), pairs)


def modulate_table(timesteps, ada_weight):
    half_freq = ada_weight.shape[0] // 2
    frequency = jnp.exp(-math.log(10000.0) * jnp.arange(half_freq, dtype=F32) / half_freq)
    angles = timesteps.astype(F32)[:, None] * frequency[None, :]
    embedding = jnp.concatenate([jnp.cos(angles), jnp.sin(angles)], axis=1).astype(BF16)
    return jnp.dot(embedding, ada_weight, preferred_element_type=F32)


def pack_kernel(hidden_hbm, cot_hbm, out_hbm, hidden_ref, cot_ref, turned_ref, sems):
    width = hidden_hbm.shape[1]
    first = pltpu.make_async_copy(cot_hbm, cot_ref, sems.at[0])
    second = pltpu.make_async_copy(hidden_hbm, hidden_ref, sems.at[1])
    first.start()
    second.start()
    first.wait()
    inner = cot_ref.shape[0]
    turned_ref[:, :inner] = cot_ref[...].T
    right = pltpu.make_async_copy(turned_ref, out_hbm.at[:, pl.ds(width, turned_ref.shape[1])], sems.at[2])
    right.start()
    second.wait()
    left = pltpu.make_async_copy(hidden_ref, out_hbm.at[:, pl.ds(0, width)], sems.at[3])
    left.start()
    right.wait()
    left.wait()


def stats(values):
    average = jnp.mean(values, axis=-1, keepdims=True)
    moved = values - average
    variance = jnp.mean(moved * moved, axis=-1, keepdims=True)
    inverse_std = lax.rsqrt(variance + norm_eps)
    return moved * inverse_std, inverse_std


def pick(spot, pieces):
    out = pieces[0]
    for index in range(1, 4):
        out = jnp.where(spot == index, pieces[index], out)
    return out


def norm_kernel(spot_ref, packed_ref, mod_ref, core_ref, side_ref):
    width = mod_ref.shape[1] // 2
    quarter = width // 8
    centered, _ = stats(packed_ref[:, :width].astype(F32))
    normed = (centered * (1.0 + mod_ref[:, width:]) + mod_ref[:, :width]).astype(BF16)
    cot = packed_ref[:, width : width + 4 * quarter].astype(F32)
    pieces = [cot[:, i * quarter : (i + 1) * quarter] for i in range(4)]
    spot = spot_ref[0]
    own, side, core, both = (pick(spot, [pieces[i ^ flip] for i in range(4)]) for flip in range(4))
    side_ref[:, :width] = normed
    side_ref[:, width : width + 2 * quarter] = jnp.concatenate([side, both], axis=1).astype(BF16)
    core_ref[:, :width] = normed
    core_ref[:, width : width + 2 * quarter] = jnp.concatenate([core, own], axis=1).astype(BF16)


def norm_back_kernel(packed_ref, mod_ref, *refs):
    out_ref = refs[-1]
    width = mod_ref.shape[1] // 2
    centered, inverse_std = stats(packed_ref[:, :width].astype(F32))
    grads = refs[0][...].astype(F32)
    for ref in refs[1:-1]:
        grads = grads + ref[...].astype(F32)
    grads = grads.astype(BF16).astype(F32)
    upstream = grads * (1.0 + mod_ref[:, width:])
    first = jnp.mean(upstream, axis=-1, keepdims=True)
    second = jnp.mean(upstream * centered, axis=-1, keepdims=True)
    out_ref[...] = (inverse_std * (upstream - first - centered * second)).astype(BF16)


def dot(left, right, over):
    return lax.dot_general(left, right, ((over[0], over[1]), ((), ())), preferred_element_type=F32)


def attend_block(projected, out_grad, same, lane):
    factor = 1.0 / math.sqrt(HDIM)
    wide = 2 * HDIM
    query = projected[:, :wide]
    keys = projected[:, wide : 2 * wide]
    values = projected[:, 2 * wide :].astype(BF16)
    query_low, keys_low = query.astype(BF16), keys.astype(BF16)
    query_grad = key_grad = value_grad = None
    for head in range(2):
        mine = (lane >= head * HDIM) & (lane < (head + 1) * HDIM)
        own_query = jnp.where(mine, query, 0.0).astype(BF16)
        own_keys = jnp.where(mine, keys, 0.0).astype(BF16)
        own_out = jnp.where(mine, out_grad, 0.0).astype(BF16)
        scores = dot(own_query, keys_low, ((1,), (1,))) * factor
        scores = jnp.where(same, scores, -1e30)
        top = jnp.max(scores, axis=-1, keepdims=True)
        expo = jnp.exp(scores - top)
        attention = expo * (1.0 / jnp.sum(expo, axis=-1, keepdims=True))
        prob_grad = dot(own_out, values, ((1,), (1,)))
        row_dot = jnp.sum(attention * prob_grad, axis=-1, keepdims=True)
        score_grad = (attention * (prob_grad - row_dot)).astype(BF16)
        parts = (
            dot(score_grad, own_keys, ((1,), (0,))),
            dot(score_grad, own_query, ((0,), (0,))),
            dot(attention.astype(BF16), own_out, ((0,), (0,))),
        )
        if head == 0:
            query_grad, key_grad, value_grad = parts
        else:
            query_grad, key_grad, value_grad = (
                query_grad + parts[0],
                key_grad + parts[1],
                value_grad + parts[2],
            )
    return jnp.concatenate([query_grad * factor, key_grad * factor, value_grad], axis=1)


def tiles_of(block):
    rows = [block[8 * i : 8 * i + 8] for i in range(block.shape[0] // 8)]
    tiles = [row[:, 128 * k : 128 * k + 128] for row in rows for k in range(3)]
    rest = [row[:, 384:] for row in rows] + [jnp.zeros_like(rows[0][:, 384:])]
    pad = jnp.zeros((8, 128 - 2 * rest[0].shape[1]), block.dtype)
    tiles += [jnp.concatenate([rest[i], rest[i + 1], pad], axis=1) for i in range(0, len(rest), 2)]
    return tiles


def block_of(tiles, height):
    count = height // 8
    rows = []
    for i in range(count):
        last = tiles[3 * count + i // 2][:, 48 * (i % 2) : 48 * (i % 2) + 48]
        rows.append(jnp.concatenate(tiles[3 * i : 3 * i + 3] + [last], axis=1))
    return jnp.concatenate(rows, axis=0)


def main_kernel(
    spot_ref, near_hbm, up_hbm, low_hbm, high_hbm, down_hbm, own_hbm, core_hbm, side_hbm, both_hbm, packed_hbm, inner_hbm, outer_hbm,
    raw_ref, token_ref, weight_ref, packed_ref, parts_ref, total_ref, grads_ref, in_sems, out_sems,
):
    tokens = own_hbm.shape[0]
    model_width, cols = total_ref.shape
    quarter = cols // 3
    lows = [lax.rem(spot_ref[1] + ahead, 4) for ahead in range(4)]
    half = raw_ref.shape[1] // 2
    sources = (own_hbm, core_hbm, side_hbm, both_hbm)
    pairs = (
        (near_hbm, raw_ref.at[lows[0]]),
        (up_hbm, raw_ref.at[lows[1]]),
        (low_hbm, raw_ref.at[lows[2], pl.ds(0, half)]),
        (high_hbm, raw_ref.at[lows[2], pl.ds(half, half)]),
        (down_hbm, raw_ref.at[lows[3]]),
    ) + tuple((source, token_ref.at[pl.ds(i * tokens, tokens)]) for i, source in enumerate(sources))
    loads = [pltpu.make_async_copy(source, target, in_sems.at[i]) for i, (source, target) in enumerate(pairs)]
    for load in loads:
        load.start()
    row = lax.broadcasted_iota(jnp.int32, (tokens, tokens), 0)
    col = lax.broadcasted_iota(jnp.int32, (tokens, tokens), 1)
    same = lax.rem(row, 16) == lax.rem(col, 16)
    lane = lax.broadcasted_iota(jnp.int32, (tokens, quarter), 1)
    for load in loads[:5]:
        load.wait()
    blocks = [raw_ref[low, group].astype(F32) for group in range(4) for low in range(4)]
    weight_ref[...] = jnp.concatenate(blocks, axis=0).astype(BF16)
    halves = []
    for side in range(2):
        for load in loads[5 + 2 * side : 7 + 2 * side]:
            load.wait()
        rows = token_ref[2 * side * tokens : 2 * (side + 1) * tokens, :model_width]
        halves.append(dot(rows, weight_ref[...], ((1,), (0,))))
    projected_all = jnp.concatenate(halves, axis=0)
    for index, skip in enumerate((1, 0, 0, 1)):
        here = slice(index * tokens, (index + 1) * tokens)
        projected = projected_all[here]
        projected = projected.astype(BF16).astype(F32)
        out_grad = token_ref[here, model_width + skip * quarter : model_width + (skip + 1) * quarter].astype(F32)
        grads_ref[here, :] = attend_block(projected, out_grad, same, lane).astype(BF16)
    total_ref[...] = dot(token_ref[:, :model_width], grads_ref[...], ((0,), (0,)))
    height = model_width // 16
    pieces = packed_ref.shape[0] // 16
    stores = []
    for owner in range(16):
        tiles = tiles_of(total_ref[owner * height : (owner + 1) * height, :])
        each = len(tiles) // pieces
        for piece in range(pieces):
            packed_ref[piece * 16 + owner] = jnp.concatenate(tiles[each * piece : each * piece + each], axis=0).astype(BF16)
    for group in range(4):
        part = pl.ds(group * 4 * pieces, 4 * pieces)
        stores.append(pltpu.make_async_copy(packed_ref.at[part], packed_hbm.at[part], out_sems.at[4 + group]))
        stores[-1].start()
    for index, (target, place) in enumerate(((inner_hbm, 0), (outer_hbm, 0), (inner_hbm, 1), (outer_hbm, 1))):
        parts_ref[index] = dot(grads_ref[index * tokens : (index + 1) * tokens, :], weight_ref[...], ((1,), (1,))).astype(BF16)
        stores.append(
            pltpu.make_async_copy(parts_ref.at[index], target.at[pl.ds(place * tokens, tokens)], out_sems.at[index])
        )
        stores[-1].start()
    for store in stores:
        store.wait()


def add_kernel(near_ref, got_ref, own_ref, side_ref):
    half = own_ref.shape[0]
    side_ref[...] = (near_ref[half:].astype(F32) + got_ref[half:].astype(F32)).astype(BF16)
    own_ref[...] = (near_ref[:half].astype(F32) + got_ref[:half].astype(F32)).astype(BF16)


def columns_kernel(spot_ref, master_ref, mine_ref, theirs_ref):
    quarter = master_ref.shape[1] // 12
    spot = spot_ref[0]
    for flip, ref in ((0, mine_ref), (2, theirs_ref)):
        parts = []
        for part in range(3):
            pieces = [master_ref[:, (4 * part + i) * quarter : (4 * part + i + 1) * quarter] for i in range(4)]
            parts.append(pick(spot, [pieces[i ^ flip] for i in range(4)]))
        ref[...] = jnp.concatenate(parts, axis=1).astype(BF16)


def pair_kernel(spot_ref, mine_ref, theirs_ref, out_ref):
    mine, theirs = mine_ref[...].astype(F32), theirs_ref[...].astype(F32)
    first = spot_ref[0] < 2
    upper, lower = jnp.where(first, mine, theirs), jnp.where(first, theirs, mine)
    out_ref[...] = jnp.concatenate([upper, lower], axis=0).astype(BF16)


def quad_kernel(spot_ref, own_ref, far_ref, across_ref, both_ref, out_ref, lower_ref, upper_ref):
    place = spot_ref[2]
    out_ref[place] = own_ref[...]
    out_ref[place + 1 - 2 * lax.rem(place, 2)] = far_ref[...]
    out_ref[lax.rem(place + 2, 4)] = across_ref[...]
    out_ref[3 - place] = both_ref[...]
    lower_ref[...] = out_ref[:2]
    upper_ref[...] = out_ref[2:]


def payload_kernel(parts_ref, back_ref, out_ref):
    total = parts_ref[0].astype(F32)
    for index in range(1, parts_ref.shape[0]):
        total = total + parts_ref[index].astype(F32)
    half = total.shape[0] // 2
    piece = jnp.concatenate([total[:half], total[half:]], axis=1).astype(BF16)
    width = back_ref.shape[1]
    out_ref[:, :width] = back_ref[...]
    for index in range(out_ref.shape[0] // half):
        out_ref[index * half : (index + 1) * half, width:] = piece


def rows_kernel(spot_ref, pieces_ref, own_ref, other_ref):
    width = pieces_ref.shape[2] - 256
    count = pieces_ref.shape[0] // 2
    height = own_ref.shape[1]
    first = spot_ref[0] < 2
    for side in range(2):
        tiles = []
        for index in range(count):
            piece = pieces_ref[side * count + index][:, width:].astype(F32)
            tiles += [piece[:8, :128], piece[8:, :128], piece[:8, 128:], piece[8:, 128:]]
        total = block_of(tiles, 2 * height)
        upper, lower = total[:height], total[height:]
        own_ref[side] = jnp.where(first, upper, lower)
        other_ref[side] = jnp.where(first, lower, upper)


def average_kernel(spot_ref, decay_ref, own_ref, core_ref, slow_ref, fast_ref, slow_out, fast_out):
    quarter = own_ref.shape[2] // 3
    first = spot_ref[0] < 2
    own, other = [own_ref[0], own_ref[1]], [core_ref[0], core_ref[1]]
    places = [jnp.where(first, a, b) for a, b in zip(own + other, other + own)]
    columns = [place[:, part * quarter : (part + 1) * quarter] for part in range(3) for place in places]
    grad = jnp.concatenate(columns, axis=1) / loss_scale
    slow_out[...] = decay_ref[0] * slow_ref[...] + (1.0 - decay_ref[0]) * grad
    fast_out[...] = decay_ref[1] * fast_ref[...] + (1.0 - decay_ref[1]) * grad


def call(kernel, outs, *args, flops=0, scratch=(), mib=16, smem=0, hbm_in=False, hbm_out=()):
    moved = sum(a.size * a.dtype.itemsize for a in args)
    moved += sum(math.prod(shape) * jnp.dtype(kind).itemsize for shape, kind in outs)
    shapes = [jax.ShapeDtypeStruct(shape, kind) for shape, kind in outs]
    body = pltpu.HBM if hbm_in else pltpu.VMEM
    specs = [pl.BlockSpec(memory_space=pltpu.SMEM if i < smem else body) for i in range(len(args))]
    got = pl.pallas_call(
        kernel,
        out_shape=shapes,
        in_specs=specs,
        out_specs=[pl.BlockSpec(memory_space=pltpu.HBM if i in hbm_out else pltpu.VMEM) for i in range(len(shapes))],
        scratch_shapes=list(scratch),
        compiler_params=params(mib),
        cost_estimate=cost(flops, moved),
    )(*args)
    return got[0] if len(got) == 1 else got


def lanes(count):
    return -(-count // 128) * 128


def on_device(hidden, timesteps, ada_weight, master, ema_slow, ema_fast, step_count, cotangent):
    patches, width = hidden.shape[2:]
    inner = cotangent.shape[3]
    own_rows, triple = master.shape
    n_seq = lax.axis_size("xl") * lax.axis_size("y")
    n_rows = lax.axis_size("xh") * lax.axis_size("z")
    n_y = lax.axis_size("y")
    quarter = inner // 4
    cols = 3 * quarter
    pair_rows = 2 * own_rows
    core, side = lax.axis_index("c"), lax.axis_index("xl")
    across, along = lax.axis_index("xh"), lax.axis_index("z")
    spots = jnp.stack([2 * core + side, lax.rem(along, 4), 2 * across + along // 4]).astype(jnp.int32)

    loose = lanes(inner)
    packed = call(
        pack_kernel,
        [((patches, width + loose), BF16)],
        hidden[0, 0], cotangent[0, 0].T,
        scratch=[
            pltpu.VMEM((patches, width), BF16),
            pltpu.VMEM((inner, patches), BF16),
            pltpu.VMEM((patches, loose), BF16),
            pltpu.SemaphoreType.DMA((4,)),
        ],
        mib=58,
        hbm_in=True,
        hbm_out=(0,),
    )
    tokens = lax.all_to_all(packed.reshape(n_seq, patches // n_seq, width + loose), SEQ, 0, 0, tiled=True)
    tokens = tokens.reshape(patches, width + loose)

    mine, theirs = call(columns_kernel, [((own_rows, cols), BF16)] * 2, spots, master, smem=1)
    pair = call(pair_kernel, [((pair_rows, cols), BF16)], spots, mine, swap(theirs, "c"), smem=1)
    turned, opposite, diagonal = half_turn(pair), swap(pair, "xh"), both_turn(pair)
    turned, opposite, diagonal, tokens = lax.optimization_barrier((turned, opposite, diagonal, tokens))

    modulation = modulate_table(timesteps, ada_weight)
    broad = lanes(width + 2 * quarter)
    to_core, to_side = call(norm_kernel, [((patches, broad), BF16)] * 2, spots, tokens, modulation, smem=1)
    from_side = swap(to_side, "xl")
    pair, turned, opposite, diagonal, to_core = lax.optimization_barrier((pair, turned, opposite, diagonal, to_core))
    quad, lower, upper = call(
        quad_kernel,
        [((4, pair_rows, cols), BF16), ((2, pair_rows, cols), BF16), ((2, pair_rows, cols), BF16)],
        spots, pair, turned, opposite, diagonal,
        smem=1,
    )
    up, low, high, down = shift(quad, -1), shift(lower, -2), shift(upper, 2), shift(quad, 1)
    to_core, low = lax.optimization_barrier((to_core, low))
    from_core = swap(to_core, "c")
    from_side, up, low, high, down = lax.optimization_barrier((from_side, up, low, high, down))
    from_both = swap(from_side, "c")

    pieces = n_rows * n_y
    packed, near, far = call(
        main_kernel,
        [((pieces, 32, 128), BF16), ((2 * patches, width), BF16), ((2 * patches, width), BF16)],
        spots, quad, up, low, high, down, to_core, from_core, from_side, from_both,
        flops=6 * 4 * patches * width * cols,
        scratch=[
            pltpu.VMEM((4, 4, pair_rows, cols), BF16),
            pltpu.VMEM((4 * patches, broad), BF16),
            pltpu.VMEM((width, cols), BF16),
            pltpu.VMEM((pieces, 32, 128), BF16),
            pltpu.VMEM((4, patches, width), BF16),
            pltpu.VMEM((width, cols), F32),
            pltpu.VMEM((4 * patches, cols), BF16),
            pltpu.SemaphoreType.DMA((9,)),
            pltpu.SemaphoreType.DMA((8,)),
        ],
        mib=58,
        smem=1,
        hbm_in=True,
        hbm_out=(0, 1, 2),
    )

    part, give = call(add_kernel, [((patches, width), BF16)] * 2, near, swap(far, "c"))
    back = call(norm_back_kernel, [((patches, width), BF16)], tokens, modulation, part, swap(give, "xl"))

    parts = lax.all_to_all(packed, ("y",) + ROWS, 0, 0, tiled=True)
    joint = call(payload_kernel, [((patches, width + 256), BF16)], parts, back)
    joint = lax.all_to_all(joint.reshape(n_seq, patches // n_seq, width + 256), SEQ, 0, 0, tiled=True)
    own_grad, other_grad = call(rows_kernel, [((2, own_rows, cols), F32)] * 2, spots, joint, smem=1)
    base = 1.0 - 1.0 / step_count[0].astype(F32)
    decays = jnp.stack([jnp.power(base, gamma_slow + 1.0), jnp.power(base, gamma_fast + 1.0)])
    ema_slow_next, ema_fast_next = call(
        average_kernel,
        [((own_rows, triple), F32)] * 2,
        spots, decays, own_grad, swap(other_grad, "c"), ema_slow, ema_fast,
        smem=2,
    )
    return (joint[:, :, :width].reshape(hidden.shape), ema_slow_next, ema_fast_next)


def solution(mesh):
    fine = Mesh(mesh.devices.reshape(2, 8, 2, 2, 8), AXES)
    dp, seq = ROWS + ("c",), SEQ
    placed = (
        P(dp, seq, None, None),
        P(dp),
        P(),
        P(dp, None),
        P(dp, None),
        P(dp, None),
        P(),
        P(dp, seq, None, None),
    )
    return jax.shard_map(
        on_device,
        mesh=fine,
        in_specs=placed,
        out_specs=(P(dp, seq, None, None), P(dp, None), P(dp, None)),
        check_vma=False,
    )
```

```python
import math

import jax
import jax.numpy as jnp
from jax import lax
from jax.experimental import pallas as pl
from jax.experimental.pallas import tpu as pltpu
from jax.sharding import Mesh
from jax.sharding import PartitionSpec as P

HEADS = 8
HDIM = 72
norm_eps = 1e-06
loss_scale = 128.0
gamma_slow = 16.97
gamma_fast = 6.94
AXES = ("xh", "z", "c", "xl", "y")
SEQ = ("xl", "y")
ROWS = ("xh", "z")
F32 = jnp.float32
BF16 = jnp.bfloat16
MIB = 1024 * 1024


def params(mib=48):
    return pltpu.CompilerParams(vmem_limit_bytes=mib * MIB)


def cost(flops, moved):
    return pl.CostEstimate(flops=flops, bytes_accessed=moved, transcendentals=0)


def swap(value, axis):
    return lax.ppermute(value, axis, [(0, 1), (1, 0)])


def shift(value, away):
    count = lax.axis_size("z")
    return lax.ppermute(value, "z", [(i, (i + away) % count) for i in range(count)])


def half_turn(value):
    return shift(value, lax.axis_size("z") // 2)


def both_turn(value):
    count = lax.axis_size("z")
    pairs = [(i, (count - count * (i // count)) + (i % count + count // 2) % count) for i in range(2 * count)]
    return lax.ppermute(value, ("xh", "z"), pairs)


def modulate_table(timesteps, ada_weight):
    half_freq = ada_weight.shape[0] // 2
    frequency = jnp.exp(-math.log(10000.0) * jnp.arange(half_freq, dtype=F32) / half_freq)
    angles = timesteps.astype(F32)[:, None] * frequency[None, :]
    embedding = jnp.concatenate([jnp.cos(angles), jnp.sin(angles)], axis=1).astype(BF16)
    return jnp.dot(embedding, ada_weight, preferred_element_type=F32)


def pack_kernel(hidden_hbm, cot_hbm, out_hbm, hidden_ref, cot_ref, turned_ref, sems):
    width = hidden_hbm.shape[1]
    first = pltpu.make_async_copy(cot_hbm, cot_ref, sems.at[0])
    second = pltpu.make_async_copy(hidden_hbm, hidden_ref, sems.at[1])
    first.start()
    second.start()
    first.wait()
    inner = cot_ref.shape[0]
    turned_ref[:, :inner] = cot_ref[...].T
    right = pltpu.make_async_copy(turned_ref, out_hbm.at[:, pl.ds(width, turned_ref.shape[1])], sems.at[2])
    right.start()
    second.wait()
    left = pltpu.make_async_copy(hidden_ref, out_hbm.at[:, pl.ds(0, width)], sems.at[3])
    left.start()
    right.wait()
    left.wait()


def stats(values):
    average = jnp.mean(values, axis=-1, keepdims=True)
    moved = values - average
    variance = jnp.mean(moved * moved, axis=-1, keepdims=True)
    inverse_std = lax.rsqrt(variance + norm_eps)
    return moved * inverse_std, inverse_std


def pick(spot, pieces):
    out = pieces[0]
    for index in range(1, 4):
        out = jnp.where(spot == index, pieces[index], out)
    return out


def norm_kernel(spot_ref, packed_ref, mod_ref, core_ref, side_ref):
    width = mod_ref.shape[1] // 2
    quarter = width // 8
    centered, _ = stats(packed_ref[:, :width].astype(F32))
    normed = (centered * (1.0 + mod_ref[:, width:]) + mod_ref[:, :width]).astype(BF16)
    cot = packed_ref[:, width : width + 4 * quarter].astype(F32)
    pieces = [cot[:, i * quarter : (i + 1) * quarter] for i in range(4)]
    spot = spot_ref[0]
    own, side, core, both = (pick(spot, [pieces[i ^ flip] for i in range(4)]) for flip in range(4))
    side_ref[:, :width] = normed
    side_ref[:, width : width + 2 * quarter] = jnp.concatenate([side, both], axis=1).astype(BF16)
    core_ref[:, :width] = normed
    core_ref[:, width : width + 2 * quarter] = jnp.concatenate([core, own], axis=1).astype(BF16)


def norm_back_kernel(packed_ref, mod_ref, *refs):
    out_ref = refs[-1]
    width = mod_ref.shape[1] // 2
    centered, inverse_std = stats(packed_ref[:, :width].astype(F32))
    grads = refs[0][...].astype(F32)
    for ref in refs[1:-1]:
        grads = grads + ref[...].astype(F32)
    grads = grads.astype(BF16).astype(F32)
    upstream = grads * (1.0 + mod_ref[:, width:])
    first = jnp.mean(upstream, axis=-1, keepdims=True)
    second = jnp.mean(upstream * centered, axis=-1, keepdims=True)
    out_ref[...] = (inverse_std * (upstream - first - centered * second)).astype(BF16)


def dot(left, right, over):
    return lax.dot_general(left, right, ((over[0], over[1]), ((), ())), preferred_element_type=F32)


def attend_block(projected, out_grad, same, lane):
    factor = 1.0 / math.sqrt(HDIM)
    wide = 2 * HDIM
    query = projected[:, :wide]
    keys = projected[:, wide : 2 * wide]
    values = projected[:, 2 * wide :].astype(BF16)
    query_low, keys_low = query.astype(BF16), keys.astype(BF16)
    query_grad = key_grad = value_grad = None
    for head in range(2):
        mine = (lane >= head * HDIM) & (lane < (head + 1) * HDIM)
        own_query = jnp.where(mine, query, 0.0).astype(BF16)
        own_keys = jnp.where(mine, keys, 0.0).astype(BF16)
        own_out = jnp.where(mine, out_grad, 0.0).astype(BF16)
        scores = dot(own_query, keys_low, ((1,), (1,))) * factor
        scores = jnp.where(same, scores, -1e30)
        top = jnp.max(scores, axis=-1, keepdims=True)
        expo = jnp.exp(scores - top)
        attention = expo * (1.0 / jnp.sum(expo, axis=-1, keepdims=True))
        prob_grad = dot(own_out, values, ((1,), (1,)))
        row_dot = jnp.sum(attention * prob_grad, axis=-1, keepdims=True)
        score_grad = (attention * (prob_grad - row_dot)).astype(BF16)
        parts = (
            dot(score_grad, own_keys, ((1,), (0,))),
            dot(score_grad, own_query, ((0,), (0,))),
            dot(attention.astype(BF16), own_out, ((0,), (0,))),
        )
        if head == 0:
            query_grad, key_grad, value_grad = parts
        else:
            query_grad, key_grad, value_grad = (
                query_grad + parts[0],
                key_grad + parts[1],
                value_grad + parts[2],
            )
    return jnp.concatenate([query_grad * factor, key_grad * factor, value_grad], axis=1)


def tiles_of(block):
    rows = [block[8 * i : 8 * i + 8] for i in range(block.shape[0] // 8)]
    tiles = [row[:, 128 * k : 128 * k + 128] for row in rows for k in range(3)]
    rest = [row[:, 384:] for row in rows] + [jnp.zeros_like(rows[0][:, 384:])]
    pad = jnp.zeros((8, 128 - 2 * rest[0].shape[1]), block.dtype)
    tiles += [jnp.concatenate([rest[i], rest[i + 1], pad], axis=1) for i in range(0, len(rest), 2)]
    return tiles


def block_of(tiles, height):
    count = height // 8
    rows = []
    for i in range(count):
        last = tiles[3 * count + i // 2][:, 48 * (i % 2) : 48 * (i % 2) + 48]
        rows.append(jnp.concatenate(tiles[3 * i : 3 * i + 3] + [last], axis=1))
    return jnp.concatenate(rows, axis=0)


def main_kernel(
    spot_ref, near_hbm, up_hbm, low_hbm, high_hbm, down_hbm, own_hbm, core_hbm, side_hbm, both_hbm, packed_hbm, inner_hbm, outer_hbm,
    raw_ref, token_ref, weight_ref, packed_ref, parts_ref, total_ref, grads_ref, in_sems, out_sems,
):
    tokens = own_hbm.shape[0]
    model_width, cols = total_ref.shape
    quarter = cols // 3
    lows = [lax.rem(spot_ref[1] + ahead, 4) for ahead in range(4)]
    half = raw_ref.shape[1] // 2
    sources = (own_hbm, core_hbm, side_hbm, both_hbm)
    pairs = (
        (near_hbm, raw_ref.at[lows[0]]),
        (up_hbm, raw_ref.at[lows[1]]),
        (low_hbm, raw_ref.at[lows[2], pl.ds(0, half)]),
        (high_hbm, raw_ref.at[lows[2], pl.ds(half, half)]),
        (down_hbm, raw_ref.at[lows[3]]),
    ) + tuple((source, token_ref.at[pl.ds(i * tokens, tokens)]) for i, source in enumerate(sources))
    loads = [pltpu.make_async_copy(source, target, in_sems.at[i]) for i, (source, target) in enumerate(pairs)]
    for load in loads:
        load.start()
    row = lax.broadcasted_iota(jnp.int32, (tokens, tokens), 0)
    col = lax.broadcasted_iota(jnp.int32, (tokens, tokens), 1)
    same = lax.rem(row, 16) == lax.rem(col, 16)
    lane = lax.broadcasted_iota(jnp.int32, (tokens, quarter), 1)
    for load in loads[:5]:
        load.wait()
    blocks = [raw_ref[low, group].astype(F32) for group in range(4) for low in range(4)]
    weight_ref[...] = jnp.concatenate(blocks, axis=0).astype(BF16)
    halves = []
    for side in range(2):
        for load in loads[5 + 2 * side : 7 + 2 * side]:
            load.wait()
        rows = token_ref[2 * side * tokens : 2 * (side + 1) * tokens, :model_width]
        halves.append(dot(rows, weight_ref[...], ((1,), (0,))))
    projected_all = jnp.concatenate(halves, axis=0)
    for index, skip in enumerate((1, 0, 0, 1)):
        here = slice(index * tokens, (index + 1) * tokens)
        projected = projected_all[here]
        projected = projected.astype(BF16).astype(F32)
        out_grad = token_ref[here, model_width + skip * quarter : model_width + (skip + 1) * quarter].astype(F32)
        grads_ref[here, :] = attend_block(projected, out_grad, same, lane).astype(BF16)
    total_ref[...] = dot(token_ref[:, :model_width], grads_ref[...], ((0,), (0,)))
    height = model_width // 16
    pieces = packed_ref.shape[0] // 16
    stores = []
    for owner in range(16):
        tiles = tiles_of(total_ref[owner * height : (owner + 1) * height, :])
        each = len(tiles) // pieces
        for piece in range(pieces):
            packed_ref[owner * pieces + piece] = jnp.concatenate(tiles[each * piece : each * piece + each], axis=0).astype(BF16)
        if owner % 4 == 3:
            part = pl.ds((owner - 3) * pieces, 4 * pieces)
            stores.append(pltpu.make_async_copy(packed_ref.at[part], packed_hbm.at[part], out_sems.at[4 + owner // 4]))
            stores[-1].start()
    for index, (target, place) in enumerate(((inner_hbm, 0), (outer_hbm, 0), (inner_hbm, 1), (outer_hbm, 1))):
        parts_ref[index] = dot(grads_ref[index * tokens : (index + 1) * tokens, :], weight_ref[...], ((1,), (1,))).astype(BF16)
        stores.append(
            pltpu.make_async_copy(parts_ref.at[index], target.at[pl.ds(place * tokens, tokens)], out_sems.at[index])
        )
        stores[-1].start()
    for store in stores:
        store.wait()


def add_kernel(near_hbm, got_hbm, own_ref, side_ref, near_ref, got_ref, sems):
    half = own_ref.shape[0]
    pairs = [(side_ref, pl.ds(half, half)), (own_ref, pl.ds(0, half))]
    loads = []
    for index, (_, rows) in enumerate(pairs):
        loads.append(pltpu.make_async_copy(near_hbm.at[rows], near_ref.at[rows], sems.at[2 * index]))
        loads.append(pltpu.make_async_copy(got_hbm.at[rows], got_ref.at[rows], sems.at[2 * index + 1]))
    for load in loads:
        load.start()
    for index, (target, rows) in enumerate(pairs):
        loads[2 * index].wait()
        loads[2 * index + 1].wait()
        target[...] = (near_ref[rows, :].astype(F32) + got_ref[rows, :].astype(F32)).astype(BF16)


def columns_kernel(spot_ref, master_ref, mine_ref, theirs_ref):
    quarter = master_ref.shape[1] // 12
    spot = spot_ref[0]
    for flip, ref in ((0, mine_ref), (2, theirs_ref)):
        parts = []
        for part in range(3):
            pieces = [master_ref[:, (4 * part + i) * quarter : (4 * part + i + 1) * quarter] for i in range(4)]
            parts.append(pick(spot, [pieces[i ^ flip] for i in range(4)]))
        ref[...] = jnp.concatenate(parts, axis=1).astype(BF16)


def pair_kernel(spot_ref, mine_ref, theirs_ref, out_ref):
    mine, theirs = mine_ref[...].astype(F32), theirs_ref[...].astype(F32)
    first = spot_ref[0] < 2
    upper, lower = jnp.where(first, mine, theirs), jnp.where(first, theirs, mine)
    out_ref[...] = jnp.concatenate([upper, lower], axis=0).astype(BF16)


def quad_kernel(spot_ref, own_ref, far_ref, across_ref, both_ref, out_ref, lower_ref, upper_ref):
    place = spot_ref[2]
    out_ref[place] = own_ref[...]
    out_ref[place + 1 - 2 * lax.rem(place, 2)] = far_ref[...]
    out_ref[lax.rem(place + 2, 4)] = across_ref[...]
    out_ref[3 - place] = both_ref[...]
    lower_ref[...] = out_ref[:2]
    upper_ref[...] = out_ref[2:]


def payload_kernel(parts_ref, back_ref, out_ref):
    total = parts_ref[0].astype(F32)
    for index in range(1, parts_ref.shape[0]):
        total = total + parts_ref[index].astype(F32)
    half = total.shape[0] // 2
    piece = jnp.concatenate([total[:half], total[half:]], axis=1).astype(BF16)
    width = back_ref.shape[1]
    out_ref[:, :width] = back_ref[...]
    for index in range(out_ref.shape[0] // half):
        out_ref[index * half : (index + 1) * half, width:] = piece


def rows_kernel(spot_ref, pieces_ref, own_ref, other_ref):
    width = pieces_ref.shape[2] - 256
    count = pieces_ref.shape[0] // 2
    height = own_ref.shape[1]
    first = spot_ref[0] < 2
    for side in range(2):
        tiles = []
        for index in range(count):
            piece = pieces_ref[side * count + index][:, width:].astype(F32)
            tiles += [piece[:8, :128], piece[8:, :128], piece[:8, 128:], piece[8:, 128:]]
        total = block_of(tiles, 2 * height)
        upper, lower = total[:height], total[height:]
        own_ref[side] = jnp.where(first, upper, lower)
        other_ref[side] = jnp.where(first, lower, upper)


def average_kernel(spot_ref, decay_ref, own_ref, core_ref, slow_ref, fast_ref, slow_out, fast_out):
    quarter = own_ref.shape[2] // 3
    first = spot_ref[0] < 2
    own, other = [own_ref[0], own_ref[1]], [core_ref[0], core_ref[1]]
    places = [jnp.where(first, a, b) for a, b in zip(own + other, other + own)]
    columns = [place[:, part * quarter : (part + 1) * quarter] for part in range(3) for place in places]
    grad = jnp.concatenate(columns, axis=1) / loss_scale
    slow_out[...] = decay_ref[0] * slow_ref[...] + (1.0 - decay_ref[0]) * grad
    fast_out[...] = decay_ref[1] * fast_ref[...] + (1.0 - decay_ref[1]) * grad


def call(kernel, outs, *args, flops=0, scratch=(), mib=16, smem=0, hbm_in=False, hbm_out=()):
    moved = sum(a.size * a.dtype.itemsize for a in args)
    moved += sum(math.prod(shape) * jnp.dtype(kind).itemsize for shape, kind in outs)
    shapes = [jax.ShapeDtypeStruct(shape, kind) for shape, kind in outs]
    body = pltpu.HBM if hbm_in else pltpu.VMEM
    specs = [pl.BlockSpec(memory_space=pltpu.SMEM if i < smem else body) for i in range(len(args))]
    got = pl.pallas_call(
        kernel,
        out_shape=shapes,
        in_specs=specs,
        out_specs=[pl.BlockSpec(memory_space=pltpu.HBM if i in hbm_out else pltpu.VMEM) for i in range(len(shapes))],
        scratch_shapes=list(scratch),
        compiler_params=params(mib),
        cost_estimate=cost(flops, moved),
    )(*args)
    return got[0] if len(got) == 1 else got


def lanes(count):
    return -(-count // 128) * 128


def on_device(hidden, timesteps, ada_weight, master, ema_slow, ema_fast, step_count, cotangent):
    patches, width = hidden.shape[2:]
    inner = cotangent.shape[3]
    own_rows, triple = master.shape
    n_seq = lax.axis_size("xl") * lax.axis_size("y")
    n_rows = lax.axis_size("xh") * lax.axis_size("z")
    n_y = lax.axis_size("y")
    quarter = inner // 4
    cols = 3 * quarter
    pair_rows = 2 * own_rows
    core, side = lax.axis_index("c"), lax.axis_index("xl")
    across, along = lax.axis_index("xh"), lax.axis_index("z")
    spots = jnp.stack([2 * core + side, lax.rem(along, 4), 2 * across + along // 4]).astype(jnp.int32)

    loose = lanes(inner)
    packed = call(
        pack_kernel,
        [((patches, width + loose), BF16)],
        hidden[0, 0], cotangent[0, 0].T,
        scratch=[
            pltpu.VMEM((patches, width), BF16),
            pltpu.VMEM((inner, patches), BF16),
            pltpu.VMEM((patches, loose), BF16),
            pltpu.SemaphoreType.DMA((4,)),
        ],
        mib=58,
        hbm_in=True,
        hbm_out=(0,),
    )
    tokens = lax.all_to_all(packed.reshape(n_seq, patches // n_seq, width + loose), SEQ, 0, 0, tiled=True)
    tokens = tokens.reshape(patches, width + loose)

    mine, theirs = call(columns_kernel, [((own_rows, cols), BF16)] * 2, spots, master, smem=1)
    pair = call(pair_kernel, [((pair_rows, cols), BF16)], spots, mine, swap(theirs, "c"), smem=1)
    turned, opposite, diagonal = half_turn(pair), swap(pair, "xh"), both_turn(pair)
    turned, opposite, diagonal, tokens = lax.optimization_barrier((turned, opposite, diagonal, tokens))

    modulation = modulate_table(timesteps, ada_weight)
    broad = lanes(width + 2 * quarter)
    to_core, to_side = call(norm_kernel, [((patches, broad), BF16)] * 2, spots, tokens, modulation, smem=1)
    from_side = swap(to_side, "xl")
    pair, turned, opposite, diagonal, to_core = lax.optimization_barrier((pair, turned, opposite, diagonal, to_core))
    quad, lower, upper = call(
        quad_kernel,
        [((4, pair_rows, cols), BF16), ((2, pair_rows, cols), BF16), ((2, pair_rows, cols), BF16)],
        spots, pair, turned, opposite, diagonal,
        smem=1,
    )
    up, low, high, down = shift(quad, -1), shift(lower, -2), shift(upper, 2), shift(quad, 1)
    to_core, low = lax.optimization_barrier((to_core, low))
    from_core = swap(to_core, "c")
    from_side, up, low, high, down = lax.optimization_barrier((from_side, up, low, high, down))
    from_both = swap(from_side, "c")

    pieces = n_rows * n_y
    packed, near, far = call(
        main_kernel,
        [((pieces, 32, 128), BF16), ((2 * patches, width), BF16), ((2 * patches, width), BF16)],
        spots, quad, up, low, high, down, to_core, from_core, from_side, from_both,
        flops=6 * 4 * patches * width * cols,
        scratch=[
            pltpu.VMEM((4, 4, pair_rows, cols), BF16),
            pltpu.VMEM((4 * patches, broad), BF16),
            pltpu.VMEM((width, cols), BF16),
            pltpu.VMEM((pieces, 32, 128), BF16),
            pltpu.VMEM((4, patches, width), BF16),
            pltpu.VMEM((width, cols), F32),
            pltpu.VMEM((4 * patches, cols), BF16),
            pltpu.SemaphoreType.DMA((9,)),
            pltpu.SemaphoreType.DMA((8,)),
        ],
        mib=58,
        smem=1,
        hbm_in=True,
        hbm_out=(0, 1, 2),
    )

    part, give = call(
        add_kernel,
        [((patches, width), BF16)] * 2,
        near, swap(far, "c"),
        scratch=[pltpu.VMEM((2 * patches, width), BF16)] * 2 + [pltpu.SemaphoreType.DMA((4,))],
        mib=56,
        hbm_in=True,
    )
    back = call(norm_back_kernel, [((patches, width), BF16)], tokens, modulation, part, swap(give, "xl"))

    parts = lax.all_to_all(packed, ROWS + ("y",), 0, 0, tiled=True)
    joint = call(payload_kernel, [((patches, width + 256), BF16)], parts, back)
    joint = lax.all_to_all(joint.reshape(n_seq, patches // n_seq, width + 256), SEQ, 0, 0, tiled=True)
    own_grad, other_grad = call(rows_kernel, [((2, own_rows, cols), F32)] * 2, spots, joint, smem=1)
    base = 1.0 - 1.0 / step_count[0].astype(F32)
    decays = jnp.stack([jnp.power(base, gamma_slow + 1.0), jnp.power(base, gamma_fast + 1.0)])
    ema_slow_next, ema_fast_next = call(
        average_kernel,
        [((own_rows, triple), F32)] * 2,
        spots, decays, own_grad, swap(other_grad, "c"), ema_slow, ema_fast,
        smem=2,
    )
    return (joint[:, :, :width].reshape(hidden.shape), ema_slow_next, ema_fast_next)


def solution(mesh):
    fine = Mesh(mesh.devices.reshape(2, 8, 2, 2, 8), AXES)
    dp, seq = ROWS + ("c",), SEQ
    placed = (
        P(dp, seq, None, None),
        P(dp),
        P(),
        P(dp, None),
        P(dp, None),
        P(dp, None),
        P(),
        P(dp, seq, None, None),
    )
    return jax.shard_map(
        on_device,
        mesh=fine,
        in_specs=placed,
        out_specs=(P(dp, seq, None, None), P(dp, None), P(dp, None)),
        check_vma=False,
    )
```
